32 devices in a mesh: fsdp: 2 (over x), ctx: 8 (over z, core), tp: 2 (over y).
Axes of the slice: x: 2, y: 2, z: 4, core: 2. Of those that a mesh axis runs over, the one named last changes fastest.
Arguments:
- tokens: bfloat16 [2, 1024, 2048], P('fsdp', 'ctx'), may hold values from -6 to 6
- w_query: bfloat16 [2048, 8, 256], P(('fsdp', 'ctx'), 'tp'), may hold values from -0.125 to 0.125
- w_key: bfloat16 [2048, 8, 256], P(('fsdp', 'ctx'), 'tp'), may hold values from -0.125 to 0.125
- w_value: bfloat16 [2048, 8, 512], P(('fsdp', 'ctx'), 'tp'), may hold values from -0.125 to 0.125
- w_swish: bfloat16 [2048, 8, 512], P(('fsdp', 'ctx'), 'tp'), may hold values from -0.125 to 0.125
- w_output: bfloat16 [2048, 8, 512], P(('fsdp', 'ctx'), 'tp'), may hold values from -0.1875 to 0.1875
- w_gelu: bfloat16 [2048, 4096], P(('fsdp', 'ctx'), 'tp'), may hold values from -0.125 to 0.125
- w_up: bfloat16 [2048, 4096], P(('fsdp', 'ctx'), 'tp'), may hold values from -0.125 to 0.125
- w_down: bfloat16 [2048, 4096], P(('fsdp', 'ctx'), 'tp'), may hold values from -0.125 to 0.125
- gain_first: bfloat16 [2048], P(('fsdp', 'ctx')), may hold values from 0.25 to 1.75
- gain_second: bfloat16 [2048], P(('fsdp', 'ctx')), may hold values from 0.25 to 1.75
- gain_group: bfloat16 [8, 512], P('tp', ('fsdp', 'ctx')), may hold values from 0.25 to 1.75
- decay_rate: float32 [8], P('tp'), may hold values from 0.9 to 1, as said below
- cotangent: bfloat16 [2, 1024, 2048], P('fsdp', 'ctx'), may hold values from -6 to 6
Outputs:
- result: float32 [2, 1024, 2048], P('fsdp', 'ctx')
- grad_tokens: float32 [2, 1024, 2048], P('fsdp', 'ctx')
- grad_query: float32 [2048, 8, 256], P(('fsdp', 'ctx'), 'tp')
- grad_key: float32 [2048, 8, 256], P(('fsdp', 'ctx'), 'tp')
- grad_value: float32 [2048, 8, 512], P(('fsdp', 'ctx'), 'tp')
- grad_swish: float32 [2048, 8, 512], P(('fsdp', 'ctx'), 'tp')
- grad_output: float32 [2048, 8, 512], P(('fsdp', 'ctx'), 'tp')
- grad_gelu: float32 [2048, 4096], P(('fsdp', 'ctx'), 'tp')
- grad_up: float32 [2048, 4096], P(('fsdp', 'ctx'), 'tp')
- grad_down: float32 [2048, 4096], P(('fsdp', 'ctx'), 'tp')
- grad_first: float32 [2048], P(('fsdp', 'ctx'))
- grad_second: float32 [2048], P(('fsdp', 'ctx'))
- grad_group: float32 [8, 512], P('tp', ('fsdp', 'ctx'))
The draws below stay inside these ranges and needn't reach their ends.
Inputs may be any that keep to these rules, and one draw needn't show every extreme that they name: `decay_rate`: each head's decay factor lies strictly between 0 and 1.
All inputs are finite; a program needn't handle non-finite values.
Results may differ from the reference program's by a relative error of at most 0.014.
Values may be sent and summed in bfloat16 or wider, within the bound.
A program may use at most 184 MiB of HBM per device.

```python
import math
import jax
import jax.numpy as jnp
from jax import lax

D = 2048
HEADS = 8
KH = 256
VH = 512
FF = 4096
PIECE = 128
SEQS = 2
LENGTH = 1024


def draw_decay_rate(key, part):
    key = jax.random.fold_in(key, 11)
    pick_key, fast_key, slow_key = jax.random.split(key, 3)
    share = 0.5
    fast = jax.random.uniform(pick_key, (HEADS,)) < share
    fast_rate = jnp.exp(jax.random.uniform(fast_key, (HEADS,), minval=math.log(1.0 / 50.0), maxval=math.log(1.0 / 30.0)))
    slow_rate = jnp.exp(jax.random.uniform(slow_key, (HEADS,), minval=math.log(0.3 / LENGTH), maxval=math.log(2.0 / LENGTH)))
    return jnp.exp(-jnp.where(fast, fast_rate, slow_rate)).astype(jnp.float32)


def block_levels(stream_key, shape, cuts, smallest, largest):
    def one(dim, shards_of):
        steps = jax.random.uniform(jax.random.fold_in(jax.random.fold_in(stream_key, 6), dim), (shards_of,), jnp.float32, smallest / len(cuts), largest / len(cuts))
        return jnp.repeat(jnp.exp(steps), shape[dim] // shards_of).reshape((-1,) + (1,) * (len(shape) - dim - 1))

    loudness = one(*cuts[0])
    for cut in cuts[1:]:
        loudness = loudness * one(*cut)
    return loudness


def noise(own_key, dims, scale, reach, cuts=(), kind=jnp.bfloat16):
    array = scale * jax.random.normal(own_key, dims, jnp.float32)
    if cuts:
        array = array * block_levels(own_key, dims, cuts, -0.22, 0.18)
    return jnp.clip(array, -reach, reach).astype(kind)


def setup_inputs(seed: int = 0) -> dict:
    key_list = jax.random.split(jax.random.key(seed), 15)
    tokens = noise(key_list[0], (SEQS, LENGTH, D), 1.0, 6.0, ((0, 2), (1, 8)))
    w_query = noise(key_list[1], (D, HEADS, KH), D ** -0.5, 0.125, ((0, 16), (1, 2)))
    w_key = noise(key_list[2], (D, HEADS, KH), D ** -0.5, 0.125, ((0, 16), (1, 2)))
    w_value = noise(key_list[3], (D, HEADS, VH), D ** -0.5, 0.125, ((0, 16), (1, 2)))
    w_swish = noise(key_list[4], (D, HEADS, VH), D ** -0.5, 0.125, ((0, 16), (1, 2)))
    w_output = noise(key_list[5], (D, HEADS, VH), (HEADS * VH // 4) ** -0.5, 0.1875, ((0, 16), (1, 2)))
    w_gelu = noise(key_list[6], (D, FF), D ** -0.5, 0.125, ((0, 16), (1, 2)))
    w_up = noise(key_list[7], (D, FF), D ** -0.5, 0.125, ((0, 16), (1, 2)))
    w_down = noise(key_list[8], (D, FF), (FF // 2) ** -0.5, 0.125, ((0, 16), (1, 2)))
    gain_first = jnp.clip(1.0 + 0.15 * jax.random.normal(key_list[9], (D,), jnp.float32), 0.25, 1.75).astype(jnp.bfloat16)
    gain_second = jnp.clip(1.0 + 0.15 * jax.random.normal(key_list[10], (D,), jnp.float32), 0.25, 1.75).astype(jnp.bfloat16)
    gain_group = jnp.clip(1.0 + 0.15 * jax.random.normal(key_list[11], (HEADS, VH), jnp.float32), 0.25, 1.75).astype(jnp.bfloat16)
    decay_rate = draw_decay_rate(jax.random.fold_in(key_list[14], 71), 0)
    cotangent = noise(key_list[13], (SEQS, LENGTH, D), 1.0, 6.0, ((0, 2), (1, 8)))
    return {"tokens": tokens, "w_query": w_query, "w_key": w_key, "w_value": w_value, "w_swish": w_swish, "w_output": w_output, "w_gelu": w_gelu, "w_up": w_up, "w_down": w_down, "gain_first": gain_first, "gain_second": gain_second, "gain_group": gain_group, "decay_rate": decay_rate, "cotangent": cotangent}


@jax.custom_vjp
def low(v):
    return lax.optimization_barrier(v.astype(jnp.bfloat16)).astype(jnp.float32)

@jax.custom_vjp
def low_back(v):
    return v

def low_keep(v):
    return (low(v), None)

def low_pass(kept, grad):
    return (grad,)

def back_keep(v):
    return (v, None)

def back_low(kept, grad):
    return (low(grad),)
low.defvjp(low_keep, low_pass)
low_back.defvjp(back_keep, back_low)
highest_precision = lax.Precision.HIGHEST

def norm_rows(values, gain):
    center = values - lax.optimization_barrier(jnp.mean(values, axis=-1, keepdims=True))
    spread = lax.optimization_barrier(jnp.mean(center * center, axis=-1, keepdims=True))
    return center * lax.rsqrt(spread + 1e-05) * gain

def retain_block(query_block, key_block_rows, value_block_rows, retention_state, log_rate):
    length = query_block.shape[0]
    position = jnp.arange(length).astype(jnp.float32)
    distance = position[:, None] - position[None, :]
    causal = distance >= 0.0
    decay_table = jnp.where(causal[None], jnp.exp(jnp.where(causal, distance, 0.0)[None] * log_rate[:, None, None]), 0.0)
    scores = jnp.einsum('thk,shk->hts', query_block, key_block_rows, precision=highest_precision) * decay_table
    within = jnp.einsum('hts,shv->thv', scores, value_block_rows, precision=highest_precision)
    decay_on_entry = jnp.exp((position[:, None] + 1.0) * log_rate[None, :])
    carried_state = jnp.einsum('pdo,dou->pdu', query_block * decay_on_entry[:, :, None], retention_state, precision=highest_precision)
    decay_on_exit = jnp.exp((length - 1.0 - position)[:, None] * log_rate[None, :])
    local_state = jnp.einsum('rdw,rdb->dwb', key_block_rows * decay_on_exit[:, :, None], value_block_rows, precision=highest_precision)
    return (within + carried_state, local_state)

def layer(inputs, w_query, w_key, w_value, w_swish, w_output, w_gelu, w_up, w_down, gain_first, gain_second, gain_group, log_rate):
    first = low(norm_rows(inputs, gain_first))
    query_block = low_back(low(jnp.einsum('td,dhk->thk', first, w_query, precision=highest_precision)))
    key_block_rows = low_back(low(jnp.einsum('td,dhk->thk', first, w_key, precision=highest_precision) * KH ** (-0.5)))
    value_block_rows = low_back(low(jnp.einsum('td,dhv->thv', first, w_value, precision=highest_precision)))
    swish_in = low_back(jnp.einsum('td,dhv->thv', first, w_swish, precision=highest_precision))
    blocks = LENGTH // PIECE
    factor = jnp.exp(PIECE * log_rate)

    def advance(retention_state, block):
        retained_block, local_state = retain_block(block[0], block[1], block[2], retention_state, log_rate)
        return (factor[:, None, None] * retention_state + local_state, retained_block)
    start = jnp.zeros((HEADS, KH, VH), jnp.float32)
    stacked = (query_block.reshape(blocks, PIECE, HEADS, KH), key_block_rows.reshape(blocks, PIECE, HEADS, KH), value_block_rows.reshape(blocks, PIECE, HEADS, VH))
    _, retained = lax.scan(jax.checkpoint(advance), start, stacked)
    retained = retained.reshape(LENGTH, HEADS, VH)
    gated = low(norm_rows(retained, gain_group) * jax.nn.silu(swish_in))
    attended = low_back(jnp.einsum('thv,dhv->td', gated, w_output, precision=highest_precision))
    hidden = inputs + attended
    second = low(norm_rows(hidden, gain_second))
    act_gelu = low_back(jnp.dot(second, w_gelu, precision=highest_precision))
    act_up = low_back(jnp.dot(second, w_up, precision=highest_precision))
    mixed = low(jax.nn.gelu(act_gelu) * act_up)
    return hidden + low_back(jnp.einsum('tf,df->td', mixed, w_down, precision=highest_precision))

def reference(tokens, w_query, w_key, w_value, w_swish, w_output, w_gelu, w_up, w_down, gain_first, gain_second, gain_group, decay_rate, cotangent):
    weights = tuple((w.astype(jnp.float32) for w in (w_query, w_key, w_value, w_swish, w_output, w_gelu, w_up, w_down, gain_first, gain_second, gain_group)))
    log_rate = jnp.log(decay_rate.astype(jnp.float32))

    def per_sequence(totals, pair):
        sequence, grad_out = pair
        result, pullback = jax.vjp(lambda rows, *params: layer(rows, *params, log_rate), sequence.astype(jnp.float32), *weights)
        grads = pullback(grad_out.astype(jnp.float32))
        totals = tuple((total + grad for total, grad in zip(totals, grads[1:])))
        return (totals, (result, grads[0]))
    zeros = tuple((jnp.zeros(w.shape, jnp.float32) for w in weights))
    totals, (result, grad_tokens) = lax.scan(per_sequence, zeros, (tokens, cotangent))
    return (result, grad_tokens, totals[0], totals[1], totals[2], totals[3], totals[4], totals[5], totals[6], totals[7], totals[8], totals[9], totals[10])
```

```python
import types

import jax
import jax.numpy as jnp
from jax import lax
from jax.experimental import pallas as pl
from jax.experimental.pallas import tpu as pltpu
from jax.sharding import PartitionSpec as P

MESH = pl.DeviceIdType.MESH
BF = jnp.bfloat16
F32 = jnp.float32

ZN = 4
BLK = 128
HALF = 64
TOK = ZN * BLK
D = 2048
CH = 512
NCH = 7
NC = 4
AC = 4
AR = HALF // AC
SETS = 4
VLIM = 62 * 2**20


def nt(a, b):
    return lax.dot_general(a, b, (((1,), (1,)), ((), ())), preferred_element_type=F32)


def nn(a, b):
    return lax.dot_general(a, b, (((1,), (0,)), ((), ())), preferred_element_type=F32)


def normed(v):
    center = v - jnp.mean(v, axis=-1, keepdims=True)
    rstd = lax.rsqrt(jnp.mean(center * center, axis=-1, keepdims=True) + 1e-05)
    return center * rstd, rstd


def norm_back(n, rstd, g):
    return rstd * (
        g - jnp.mean(g, axis=-1, keepdims=True) - n * jnp.mean(g * n, axis=-1, keepdims=True)
    )


def remote(src, dst, ss, rs, dev):
    return pltpu.make_async_remote_copy(src, dst, ss, rs, device_id=dev, device_id_type=MESH)


SCRATCH = dict(
    gall=((16, 8, 128), F32),
    W=((NCH, 16, BLK, CH), BF),
    first=((ZN, BLK, D), BF),
    cot=((ZN, BLK, D), BF),
    second=((ZN, BLK, D), BF),
    hlow=((ZN, BLK, D), BF),
    XT=((16, BLK, TOK), BF),
    qkv=((2, TOK, 1024), BF),
    swish=((TOK, CH), F32),
    ret=((TOK, CH), F32),
    gg=((TOK, CH), F32),
    dr=((TOK, CH), BF),
    YB=((NCH, TOK, CH), BF),
    dkv_s=((TOK, 768), BF),
    dkv_r=((TOK, 768), BF),
    tmp=((3, TOK, 256), F32),
    ysend=((2, NC, ZN, HALF, CH), BF),
    yrecv=((2, NC, ZN, HALF, CH), BF),
    zsend=((2, NC, ZN, HALF, CH), BF),
    zrecv=((2, NC, ZN, HALF, CH), BF),
    hidden=((HALF, D), F32),
    ghid=((HALF, D), F32),
    rsum=((HALF, D), F32),
    ostage=((2, HALF, D), BF),
    gcs=((2, ZN, BLK, CH), BF),
    gcr=((SETS, 2, ZN, BLK, CH), BF),
    gxs=((SETS, ZN, BLK, CH), BF),
    gxr=((SETS, ZN, BLK, CH), BF),
    gzs=((SETS, ZN, BLK, CH), BF),
    vec=((8, D), F32),
    vrc=((8, D), F32),
    vrx=((8, D), F32),
    vry=((8, D), F32),
    vz=((ZN, 8, D), F32),
)
SEMS = dict(
    g_s=(3, 8), g_r=(3, 8),
    wz_s=(NCH, 3), wz_r=(NCH, 3), wx_s=(NCH, 4), wx_r=(NCH, 4), wc_s=(NCH, 8), wc_r=(NCH, 8), wl=(NCH,),
    az_s=(4, AC, 3), az_r=(4, AC, 3), ay_s=(4, AC, 4), ay_r=(4, AC, 4),
    ry_s=(4, NC), ry_r=(4, NC), rz_s=(4, NC, 3), rz_r=(4, NC, 3),
    kv_s=(2,), kv_r=(2,),
    gc_s=(NCH, 2), gc_r=(NCH, 2), gx_s=(NCH,), gx_r=(NCH,), gz_s=(NCH, 3), gz_r=(NCH, 3), gl=(NCH,),
    v_s=(6,), v_r=(6,), o_s=(2,), o_r=(2,), ol=(4,),
    credit=None,
)
NAMES = list(SCRATCH) + list(SEMS)


def kernel(tok, gp, lr, cot_in, pk, wg, wu, wd, res_o, gtok_o, gwa_o, gwf_o, vec_o, *scratch):
    s = types.SimpleNamespace(**dict(zip(NAMES, scratch)))
    W, YB, XT = s.W, s.YB, s.XT
    x, k, y = lax.axis_index("fsdp"), lax.axis_index("ctx"), lax.axis_index("tp")
    z, c = k // 2, k % 2
    zup = [lax.rem(z + i, ZN) for i in range(ZN)]
    zdn = [lax.rem(z + ZN - i, ZN) for i in range(ZN)]
    zdev = [(x, zup[i] * 2 + c, y) for i in range(ZN)]
    xdev, ydev, cdev = (1 - x, k, y), (x, k, 1 - y), (x, z * 2 + 1 - c, y)
    peers = range(1, ZN)

    def place(xx, zz, cc):
        return xx * 8 + zz * 2 + cc

    me = place(x, z, c)
    log_rate = lr[z]

    def loop(n, f):
        def step(i, carry):
            f(i)
            return carry

        lax.fori_loop(0, n, step, 0)

    barrier = pltpu.get_barrier_semaphore()
    for dev in zdev[1:] + [xdev, ydev, cdev]:
        pl.semaphore_signal(barrier, inc=1, device_id=dev, device_id_type=MESH)
    pl.semaphore_wait(barrier, 6)

    def w_src(n, zz):
        if n < 4:
            return pk.at[zz, :, pl.ds(n * CH, CH)]
        return (wg, wu, wd)[n - 4].at[:, pl.ds(pl.multiple_of(zz * CH, CH), CH)]

    def w_local(n, zz):
        return pltpu.make_async_copy(w_src(n, zz), W.at[n, me], s.wl.at[n])

    def w_send(n):
        for i in peers:
            remote(w_src(n, zup[i]), W.at[n, me], s.wz_s.at[n, i - 1], s.wz_r.at[n, i - 1], zdev[i]).start()
        w_local(n, z).start()

    def w_z(n, i):
        blk = W.at[n, place(x, zdn[i], c)]
        return remote(blk, blk, s.wz_s.at[n, i - 1], s.wz_r.at[n, i - 1], zdev[i])

    def w_x(n, j, xx):
        blk = W.at[n, place(xx, zdn[j], c)]
        return remote(blk, blk, s.wx_s.at[n, j], s.wx_r.at[n, j], xdev)

    def w_c(n, j, cc):
        xx = x if j < 4 else 1 - x
        blk = W.at[n, place(xx, zdn[j % 4], cc)]
        return remote(blk, blk, s.wc_s.at[n, j], s.wc_r.at[n, j], cdev)

    def pump_z(n):
        for i in range(ZN):
            if i == 0:
                pltpu.make_async_copy(W.at[n, me], W.at[n, me], s.wl.at[n]).wait()
            else:
                w_z(n, i).wait_recv()
            w_x(n, i, x).start()
            w_c(n, i, c).start()

    def pump_x(n):
        for j in range(ZN):
            w_x(n, j, 1 - x).wait_recv()
            w_c(n, ZN + j, c).start()

    def w_fin(n):
        for j in range(8):
            w_c(n, j, 1 - c).wait_recv()

    def w_done(n):
        for i in peers:
            w_z(n, i).wait_send()
        for j in range(ZN):
            w_x(n, j, x).wait_send()
        for j in range(8):
            w_c(n, j, c).wait_send()

    def a_rows(yy, ch):
        return pl.ds(pl.multiple_of(yy * HALF + ch * AR, AR), AR)

    def a_z(buf, ia, ch, i, zz):
        blk = buf.at[zz, a_rows(y, ch)]
        return remote(blk, blk, s.az_s.at[ia, ch, i - 1], s.az_r.at[ia, ch, i - 1], zdev[i])

    def a_y(buf, ia, ch, i, yy):
        blk = buf.at[zdn[i], a_rows(yy, ch)]
        return remote(blk, blk, s.ay_s.at[ia, ch, i], s.ay_r.at[ia, ch, i], ydev)

    def ag_send(buf, ia, own):
        def f(ch):
            for i in peers:
                a_z(buf, ia, ch, i, z).start()
            if own:
                a_y(buf, ia, ch, 0, y).start()

        loop(AC, f)

    def ag_forward(buf, ia):
        def f(ch):
            for i in peers:
                a_z(buf, ia, ch, i, zdn[i]).wait_recv()
                a_y(buf, ia, ch, i, y).start()

        loop(AC, f)

    def ag_wait(buf, ia, own):
        def f(ch):
            for i in range(0 if own else 1, ZN):
                a_y(buf, ia, ch, i, 1 - y).wait_recv()

        loop(AC, f)

    def ag_done(buf, ia, own):
        def f(ch):
            for i in peers:
                a_z(buf, ia, ch, i, z).wait_send()
            for i in range(0 if own else 1, ZN):
                a_y(buf, ia, ch, i, y).wait_send()

        loop(AC, f)

    def product(chunks, j, yy):
        total = None
        for n in chunks:
            rows = [YB[n, pl.ds(pl.multiple_of(zz * BLK + yy * HALF, HALF), HALF), :] for zz in range(ZN)]
            lhs = jnp.concatenate(rows, axis=0)
            rhs = W[n, pl.ds(j * 4, 4)].reshape(CH, CH)
            part = nt(lhs, rhs)
            total = part if total is None else total + part
        return total.reshape(ZN, HALF, CH)

    def r_y(ir, b, j):
        return remote(s.ysend.at[b, j], s.yrecv.at[b, j], s.ry_s.at[ir, j], s.ry_r.at[ir, j], ydev)

    def r_z(ir, b, j, i):
        return remote(
            s.zsend.at[b, j, zup[i]], s.zrecv.at[b, j, i], s.rz_s.at[ir, j, i - 1], s.rz_r.at[ir, j, i - 1], zdev[i]
        )

    def rs_a(ir, b, chunks):
        def f(j):
            s.ysend[b, j] = product(chunks, j, 1 - y).astype(BF)
            r_y(ir, b, j).start()

        loop(NC, f)

    def rs_b(ir, b, chunks):
        def f(j):
            own = product(chunks, j, y)
            r_y(ir, b, j).wait_recv()
            s.zsend[b, j] = (own + s.yrecv[b, j].astype(F32)).astype(BF)
            for i in peers:
                r_z(ir, b, j, i).start()

        loop(NC, f)

    def rs_c(ir, b):
        def f(j):
            for i in peers:
                r_z(ir, b, j, i).wait_recv()
            total = s.zsend[b, j, z].astype(F32)
            for i in peers:
                total = total + s.zrecv[b, j, i].astype(F32)
            s.rsum[:, pl.ds(pl.multiple_of(j * CH, CH), CH)] = total

        loop(NC, f)

    def rs_done(ir, b):
        def f(j):
            r_y(ir, b, j).wait_send()
            for i in peers:
                r_z(ir, b, j, i).wait_send()

        loop(NC, f)

    def transpose(buf):
        def f(q):
            cols = pl.ds(pl.multiple_of(q * BLK, BLK), BLK)
            XT[q] = buf[:, :, cols].reshape(TOK, BLK).T

        loop(16, f)

    def grad_rows(n, xx, cc):
        lhs = jnp.concatenate([XT[place(xx, zz, cc)] for zz in range(ZN)], axis=0)
        return nn(lhs, YB[n]).reshape(ZN, BLK, CH)

    def g_c(n, xx):
        return remote(s.gcs.at[xx], s.gcr.at[n % SETS, xx], s.gc_s.at[n, xx], s.gc_r.at[n, xx], cdev)

    def g_x(n):
        return remote(s.gxs.at[n % SETS], s.gxr.at[n % SETS], s.gx_s.at[n], s.gx_r.at[n], xdev)

    def g_dst(n):
        if n < 4:
            return gwa_o.at[n, z]
        return gwf_o.at[n - 4, :, pl.ds(pl.multiple_of(z * CH, CH), CH)]

    def g_z(n, i):
        return remote(s.gzs.at[n % SETS, zup[i]], g_dst(n), s.gz_s.at[n, i - 1], s.gz_r.at[n, i - 1], zdev[i])

    def g_local(n):
        return pltpu.make_async_copy(s.gzs.at[n % SETS, z], g_dst(n), s.gl.at[n])

    def grad_a(n, first_use):
        b = n % SETS

        def f(t):
            xx = (1 - x) * (1 - t) + x * t
            s.gcs[xx] = grad_rows(n, xx, 1 - c).astype(BF)
            g_c(n, xx).start()

        loop(2, f)
        own = grad_rows(n, 1 - x, c)
        g_c(n, 1 - x).wait_recv()
        if not first_use:
            pl.semaphore_wait(s.credit, 1)
        s.gxs[b] = (own + s.gcr[b, 1 - x].astype(F32)).astype(BF)
        g_x(n).start()
        own = grad_rows(n, x, c)
        g_c(n, x).wait_recv()
        s.gzs[b] = (own + s.gcr[b, x].astype(F32)).astype(BF)
        for xx in range(2):
            g_c(n, xx).wait_send()

    def grad_b(n, more):
        b = n % SETS
        g_x(n).wait_recv()
        s.gzs[b] = (s.gzs[b].astype(F32) + s.gxr[b].astype(F32)).astype(BF)
        for i in peers:
            g_z(n, i).start()
        g_local(n).start()
        g_x(n).wait_send()
        if more:
            pl.semaphore_signal(s.credit, inc=1, device_id=xdev, device_id_type=MESH)

    def grad_sent(n):
        for i in peers:
            g_z(n, i).wait_send()
        g_local(n).wait()

    def grad_done(n):
        for i in peers:
            g_z(n, i).wait_recv()

    def gain_row(r):
        return jnp.concatenate([s.gall[q, r : r + 1, :] for q in range(16)], axis=1)

    def group_gain():
        pick = lax.broadcasted_iota(jnp.int32, (8, 128), 0) == 2 + z
        parts = []
        for r in range(4):
            total = s.gall[4 * r]
            for q in range(4 * r + 1, 4 * r + 4):
                total = total + s.gall[q]
            parts.append(jnp.sum(jnp.where(pick, total, 0.0), axis=0, keepdims=True))
        return jnp.concatenate(parts, axis=1)

    def position(shape, dim, both, start):
        r = lax.broadcasted_iota(jnp.int32, shape, dim) + start
        if both:
            core, r = r // TOK, lax.rem(r, TOK)
        else:
            core = c
        return r + (r // BLK) * BLK + core * BLK

    def decay(later, earlier):
        gap = later - earlier
        keep = gap >= 0
        return jnp.where(keep, jnp.exp(jnp.where(keep, gap, 0).astype(F32) * log_rate), 0.0)

    own_rows = pl.ds(pl.multiple_of(y * HALF, HALF), HALF)

    for n in range(3):
        w_send(n)
    cot_local = pltpu.make_async_copy(cot_in, s.cot.at[z], s.ol.at[0])
    cot_local.start()

    gall = s.gall
    gall[me] = gp[...]

    def g_gain(j, i, dev, q):
        return remote(gall.at[q], gall.at[q], s.g_s.at[j, i], s.g_r.at[j, i], dev)

    for i in peers:
        g_gain(0, i, zdev[i], me).start()
    for i in peers:
        g_gain(0, i, zdev[i], place(x, zdn[i], c)).wait_recv()
    for i in range(ZN):
        g_gain(1, i, xdev, place(x, zdn[i], c)).start()
    for i in range(ZN):
        g_gain(2, i, cdev, place(x, zdn[i], c)).start()
    for i in range(ZN):
        g_gain(1, i, xdev, place(1 - x, zdn[i], c)).wait_recv()
        g_gain(2, ZN + i, cdev, place(1 - x, zdn[i], c)).start()
    for i in range(8):
        xx = x if i < ZN else 1 - x
        g_gain(2, i, cdev, place(xx, zdn[i % ZN], 1 - c)).wait_recv()
    for i in peers:
        g_gain(0, i, zdev[i], me).wait_send()
    for i in range(ZN):
        g_gain(1, i, xdev, place(x, zdn[i], c)).wait_send()
    for i in range(8):
        xx = x if i < ZN else 1 - x
        g_gain(2, i, cdev, place(xx, zdn[i % ZN], c)).wait_send()

    tokens = tok[...].astype(F32)
    n_first, _ = normed(tokens)
    s.first[z] = (n_first * gain_row(0)).astype(BF)
    ag_send(s.first, 0, False)
    loop(2, pump_z)
    ag_forward(s.first, 0)
    pump_z(2)
    for n in range(3, NCH):
        w_send(n)
    cot_local.wait()
    ag_send(s.cot, 1, False)
    loop(3, pump_x)
    ag_wait(s.first, 0, False)

    qkv, swish = s.qkv, s.swish

    def columns(n, t):
        return W[n, :, :, pl.ds(pl.multiple_of(t * 256, 256), 256)].reshape(D, 256)

    w_fin(0)

    def project_qk(t):
        scale = jnp.where(t == 1, 0.0625, 1.0)
        out = nn(s.first[...].reshape(TOK, D), columns(0, t)) * scale
        qkv[c, :, pl.ds(pl.multiple_of(t * 256, 256), 256)] = out.astype(BF)

    loop(2, project_qk)
    w_fin(1)

    def project_v(t):
        out = nn(s.first[...].reshape(TOK, D), columns(1, t))
        qkv[c, :, pl.ds(pl.multiple_of(512 + t * 256, 256), 256)] = out.astype(BF)

    loop(2, project_v)

    def kv_copy(cc):
        blk = qkv.at[cc, :, pl.ds(256, 768)]
        return remote(blk, blk, s.kv_s.at[0], s.kv_r.at[0], cdev)

    kv_copy(c).start()
    w_fin(2)

    def project_s(t):
        out = nn(s.first[...].reshape(TOK, D), columns(2, t))
        swish[:, pl.ds(pl.multiple_of(t * 256, 256), 256)] = out

    loop(2, project_s)
    pump_z(3)
    kv_copy(1 - c).wait_recv()

    def all_keys():
        return qkv[:, :, 256:512].reshape(2 * TOK, 256)

    def all_values():
        return qkv[:, :, 512:1024].reshape(2 * TOK, CH)

    def retain(h):
        rows = pl.ds(pl.multiple_of(h * 256, 256), 256)
        later = position((256, 2 * TOK), 0, False, h * 256)
        earlier = position((256, 2 * TOK), 1, True, 0)
        scores = nt(qkv[c, rows, 0:256], all_keys()) * decay(later, earlier)
        s.ret[rows, :] = nn(scores.astype(BF), all_values())

    loop(2, retain)
    gain_g = group_gain()

    def gate(h):
        rows = pl.ds(pl.multiple_of(h * BLK, BLK), BLK)
        n, _ = normed(s.ret[rows, :])
        w = swish[rows, :]
        YB[3, rows, :] = (n * gain_g * (w / (1.0 + jnp.exp(-w)))).astype(BF)

    loop(ZN, gate)
    pump_x(3)
    w_fin(3)

    rs_a(0, 0, (3,))
    rs_b(0, 0, (3,))
    loop(2, lambda n: pump_z(n + 4))
    rs_c(0, 0)
    hidden = tok[own_rows, :].astype(F32) + s.rsum[...]
    s.hidden[...] = hidden
    n_second, _ = normed(hidden)
    s.second[z, own_rows, :] = (n_second * gain_row(1)).astype(BF)
    ag_send(s.second, 2, True)
    loop(2, lambda n: pump_x(n + 4))
    pump_z(6)
    pump_x(6)
    ag_forward(s.cot, 1)
    ag_forward(s.second, 2)
    for n in range(4, NCH):
        w_fin(n)
    ag_wait(s.cot, 1, False)
    ag_wait(s.second, 2, True)

    tmp = s.tmp

    def feed(t):
        cols = pl.ds(pl.multiple_of(t * 256, 256), 256)
        sec = s.second[...].reshape(TOK, D)
        tmp[0] = nn(sec, columns(4, t))
        tmp[1] = nn(sec, columns(5, t))
        tmp[2] = nn(s.cot[...].reshape(TOK, D), columns(6, t))

        def act(h):
            rows = pl.ds(pl.multiple_of(h * HALF, HALF), HALF)
            a, u, gm = tmp[0, rows, :], tmp[1, rows, :], tmp[2, rows, :]
            root = 0.7978845608028654
            th = jnp.tanh(root * (a + 0.044715 * (a * a * a)))
            half = 0.5 * (1.0 + th)
            gelu = a * half
            slope = half + 0.5 * a * (1.0 - th * th) * (root * (1.0 + 0.134145 * (a * a)))
            YB[6, rows, cols] = (gelu * u).astype(BF)
            YB[4, rows, cols] = (gm * u * slope).astype(BF)
            YB[5, rows, cols] = (gm * gelu).astype(BF)

        loop(TOK // HALF, act)

    loop(2, feed)
    rs_done(0, 0)
    rs_a(1, 0, (4, 5))
    rs_a(2, 1, (6,))
    rs_b(1, 0, (4, 5))
    transpose(s.second)
    grad_a(4, True)
    grad_a(5, True)
    rs_c(1, 0)
    n_second, rstd = normed(s.hidden[...])
    g_in = s.rsum[...]
    s.vec[1:2, :] = jnp.sum(g_in * n_second, axis=0, keepdims=True)
    ghid = s.cot[z, own_rows, :].astype(F32) + norm_back(n_second, rstd, g_in * gain_row(1))
    s.ghid[...] = ghid
    s.hlow[z, own_rows, :] = ghid.astype(BF)
    ag_send(s.hlow, 3, True)
    rs_b(2, 1, (6,))
    transpose(s.cot)
    grad_a(6, True)
    grad_b(4, True)
    grad_b(5, True)
    grad_b(6, True)
    ag_forward(s.hlow, 3)
    ag_wait(s.hlow, 3, True)

    def back_gated(t):
        out = nn(s.hlow[...].reshape(TOK, D), columns(3, t))
        s.gg[:, pl.ds(pl.multiple_of(t * 256, 256), 256)] = out

    loop(2, back_gated)

    def back_gate(h, total):
        rows = pl.ds(pl.multiple_of(h * BLK, BLK), BLK)
        n, rstd = normed(s.ret[rows, :])
        w, g = swish[rows, :], s.gg[rows, :]
        sig = 1.0 / (1.0 + jnp.exp(-w))
        silu = w * sig
        YB[2, rows, :] = (g * (n * gain_g) * (sig * (1.0 + w * (1.0 - sig)))).astype(BF)
        gs = g * silu
        s.dr[rows, :] = norm_back(n, rstd, gs * gain_g).astype(BF)
        return total + jnp.sum(gs * n, axis=0, keepdims=True)

    group = lax.fori_loop(0, ZN, back_gate, jnp.zeros((1, CH), F32))
    s.vec[2:3, 0:CH] = group

    def back_keys(core, h):
        rows = pl.ds(pl.multiple_of(h * 256, 256), 256)
        keys, values = qkv[core, rows, 256:512], qkv[core, rows, 512:1024]
        query = qkv[c, :, 0:256]
        r = lax.broadcasted_iota(jnp.int32, (256, TOK), 0) + h * 256
        earlier = r + (r // BLK) * BLK + core * BLK
        table = decay(position((256, TOK), 1, False, 0), earlier)
        weights = (nt(keys, query) * table).astype(BF)
        slopes = (nt(values, s.dr[...]) * table).astype(BF)
        return rows, nn(slopes, query), nn(weights, s.dr[...])

    def back_other(h):
        rows, dk, dv = back_keys(1 - c, h)
        s.dkv_s[rows, 0:256] = dk.astype(BF)
        s.dkv_s[rows, 256:768] = dv.astype(BF)

    def back_own(h):
        rows, dk, dv = back_keys(c, h)
        tmp[0, rows, :] = dk
        tmp[1, rows, :] = dv[:, 0:256]
        tmp[2, rows, :] = dv[:, 256:512]

    loop(2, back_other)
    dkv_copy = remote(s.dkv_s, s.dkv_r, s.kv_s.at[1], s.kv_r.at[1], cdev)
    dkv_copy.start()
    loop(2, back_own)

    def back_query(h):
        rows = pl.ds(pl.multiple_of(h * 256, 256), 256)
        later = position((256, 2 * TOK), 0, False, h * 256)
        earlier = position((256, 2 * TOK), 1, True, 0)
        slopes = nt(s.dr[rows, :], all_values()) * decay(later, earlier)
        YB[0, rows, 0:256] = nn(slopes.astype(BF), all_keys()).astype(BF)

    loop(2, back_query)
    dkv_copy.wait_recv()

    def back_sum(h):
        rows = pl.ds(pl.multiple_of(h * BLK, BLK), BLK)
        other = s.dkv_r[rows, :].astype(F32)
        YB[0, rows, 256:512] = ((tmp[0, rows, :] + other[:, 0:256]) * 0.0625).astype(BF)
        YB[1, rows, 0:256] = (tmp[1, rows, :] + other[:, 256:512]).astype(BF)
        YB[1, rows, 256:512] = (tmp[2, rows, :] + other[:, 512:768]).astype(BF)

    loop(ZN, back_sum)

    rs_done(1, 0)
    rs_a(3, 0, (0, 1, 2))
    rs_b(3, 0, (0, 1, 2))
    transpose(s.first)
    grad_sent(4)
    grad_a(0, False)
    grad_sent(5)
    grad_a(1, False)
    rs_c(3, 0)
    n_first, rstd = normed(tok[own_rows, :].astype(F32))
    g_in = s.rsum[...]
    s.vec[0:1, :] = jnp.sum(g_in * n_first, axis=0, keepdims=True)
    g_tok = s.ghid[...] + norm_back(n_first, rstd, g_in * gain_row(0))
    s.ostage[0] = g_tok.astype(BF)

    def out_copies(j, dst):
        there = dst.at[own_rows]
        return (
            remote(s.ostage.at[j], there, s.o_s.at[j], s.o_r.at[j], ydev),
            pltpu.make_async_copy(s.ostage.at[j], there, s.ol.at[1 + j]),
        )

    for copy in out_copies(0, gtok_o):
        copy.start()
    grad_b(0, False)
    grad_b(1, False)
    grad_sent(6)
    grad_a(2, False)
    transpose(s.hlow)
    grad_a(3, True)
    grad_b(2, False)
    grad_b(3, False)
    rs_c(2, 1)
    s.ostage[1] = (s.hidden[...] + s.rsum[...]).astype(BF)
    for copy in out_copies(1, res_o):
        copy.start()

    vec = s.vec

    def v_copy(j, dst, dev):
        return remote(vec, dst, s.v_s.at[j], s.v_r.at[j], dev)

    vec[3:8, :] = jnp.zeros((5, D), F32)
    vec[2:3, CH:D] = jnp.zeros((1, D - CH), F32)
    for j, (dst, dev) in enumerate(((s.vrc, cdev), (s.vrx, xdev), (s.vry, ydev))):
        copy = v_copy(j, dst, dev)
        copy.start()
        copy.wait()
        if j < 2:
            vec[...] = vec[...] + dst[...]
        else:
            vec[0:2, :] = vec[0:2, :] + dst[0:2, :]
    s.vz[z] = vec[...]
    for i in peers:
        remote(vec, s.vz.at[z], s.v_s.at[2 + i], s.v_r.at[2 + i], zdev[i]).start()
    for i in peers:
        there = s.vz.at[zdn[i]]
        copy = remote(there, there, s.v_s.at[2 + i], s.v_r.at[2 + i], zdev[i])
        copy.wait_recv()
    for i in peers:
        remote(vec, s.vz.at[z], s.v_s.at[2 + i], s.v_r.at[2 + i], zdev[i]).wait_send()
    vz = s.vz
    vec_o[0:2, :] = ((vz[0, 0:2, :] + vz[1, 0:2, :]) + vz[2, 0:2, :]) + vz[3, 0:2, :]
    vec_o[2:4, :] = jnp.zeros((2, D), F32)
    for zz in range(ZN):
        vec_o[4 + zz : 5 + zz, :] = vz[zz, 2:3, :]

    for j, dst in enumerate((gtok_o, res_o)):
        there = dst.at[pl.ds(pl.multiple_of((1 - y) * HALF, HALF), HALF)]
        a, b = out_copies(j, dst)
        a.wait_send()
        b.wait()
        remote(s.ostage.at[j], there, s.o_s.at[j], s.o_r.at[j], ydev).wait_recv()
    for n in range(4):
        grad_sent(n)
    for n in range(NCH):
        grad_done(n)
    loop(NCH, w_done)
    kv_copy(c).wait_send()
    dkv_copy.wait_send()
    for ia, (buf, own) in enumerate(((s.first, False), (s.cot, False), (s.second, True), (s.hlow, True))):
        ag_done(buf, ia, own)
    rs_done(2, 1)
    rs_done(3, 0)


def pieces(tokens, w_query, w_key, w_value, w_swish, w_output, w_gelu, w_up, w_down, gain_first, gain_second, gain_group, decay_rate, cotangent):
    me = lax.axis_index("fsdp") * 8 + lax.axis_index("ctx")
    pk = jnp.concatenate([w_query, w_key, w_value, w_swish, w_output], axis=2).transpose(1, 0, 2)
    lane = lax.broadcasted_iota(jnp.int32, (ZN, BLK), 1) // 32
    spread = jnp.where(lane == lax.rem(me, 4), jnp.tile(gain_group.astype(F32), (1, 4)), 0.0)
    gp = jnp.concatenate(
        [gain_first.astype(F32)[None], gain_second.astype(F32)[None], spread, jnp.zeros((2, BLK), F32)], axis=0
    )
    return (tokens[0], gp, jnp.log(decay_rate), cotangent[0], pk, w_gelu, w_up, w_down)


def fused(*args):
    shapes = [
        jax.ShapeDtypeStruct((BLK, D), BF),
        jax.ShapeDtypeStruct((BLK, D), BF),
        jax.ShapeDtypeStruct((4, ZN, BLK, CH), BF),
        jax.ShapeDtypeStruct((3, BLK, D), BF),
        jax.ShapeDtypeStruct((8, D), F32),
    ]
    hbm = pl.BlockSpec(memory_space=pl.ANY)
    vmem = pl.BlockSpec(memory_space=pltpu.VMEM)
    smem = pl.BlockSpec(memory_space=pltpu.SMEM)
    scratch = [pltpu.VMEM(*v) for v in SCRATCH.values()]
    for name, shape in SEMS.items():
        scratch.append(pltpu.SemaphoreType.REGULAR if shape is None else pltpu.SemaphoreType.DMA(shape))
    result, g_tok, gwa, gwf, vec = pl.pallas_call(
        kernel,
        out_shape=shapes,
        in_specs=[vmem, vmem, smem, hbm, hbm, hbm, hbm, hbm],
        out_specs=[hbm, hbm, hbm, hbm, vmem],
        scratch_shapes=scratch,
        compiler_params=pltpu.CompilerParams(collective_id=0, has_side_effects=True, vmem_limit_bytes=VLIM),
    )(*pieces(*args))
    me = lax.axis_index("fsdp") * 8 + lax.axis_index("ctx")
    swap = gwa.transpose(0, 2, 1, 3).astype(F32)
    gwf = gwf.astype(F32)
    g_first = lax.dynamic_slice(vec[0], (me * BLK,), (BLK,))
    g_second = lax.dynamic_slice(vec[1], (me * BLK,), (BLK,))
    g_group = lax.dynamic_slice(vec, (4, me * 32), (4, 32))
    return (
        result[None].astype(F32),
        g_tok[None].astype(F32),
        swap[0, :, :, 0:256],
        swap[0, :, :, 256:512],
        swap[1],
        swap[2],
        swap[3],
        gwf[0],
        gwf[1],
        gwf[2],
        g_first,
        g_second,
        g_group,
    )


highest_precision = lax.Precision.HIGHEST


def prefix(part, axis, combine, identity):
    place = lax.axis_index(axis)
    gathered = jax.tree.map(lambda a: lax.all_gather(a, axis), part)
    state = jax.tree.map(lambda a, e: jnp.zeros_like(a) + jnp.asarray(e, a.dtype), part, identity)

    def one(turn, state):
        return combine(
            state, jax.tree.map(lambda a: lax.dynamic_index_in_dim(a, turn, 0, False), gathered)
        )

    return lax.fori_loop(0, place, one, state)


def entering_2(value, axis, combine, identity):
    devices, mine = (lax.axis_size(axis), lax.axis_index(axis))
    everything = jax.tree.map(
        lambda part, kind: lax.all_gather(part.astype(kind), axis),
        value,
        jax.tree.map(lambda a: jnp.bfloat16 if a.dtype == jnp.float32 else a.dtype, value),
    )
    start = jax.tree.map(
        lambda part, zero: jnp.broadcast_to(jnp.asarray(zero, part.dtype), part.shape),
        value,
        identity,
    )

    def turn(k, before):
        at = devices - 1 - k
        reached = at > mine
        new = combine(
            before, jax.tree.map(lambda part, own: part[at].astype(own.dtype), everything, value)
        )
        return jax.tree.map(lambda a, b: jnp.where(reached, a, b), new, before)

    return lax.fori_loop(0, devices, turn, start)


def norm_rows(values, gain):
    center = values - jnp.mean(values, axis=-1, keepdims=True)
    spread = jnp.mean(center * center, axis=-1, keepdims=True)
    return center * lax.rsqrt(spread + 1e-05) * gain


def entry_weights(length, log_rate):
    position = jnp.arange(length).astype(jnp.float32)
    return jnp.exp((position[:, None] + 1.0) * log_rate[None, :])


def exit_weights(length, log_rate):
    position = jnp.arange(length).astype(jnp.float32)
    return jnp.exp((length - 1.0 - position)[:, None] * log_rate[None, :])


def decay_matrix(length, log_rate):
    position = jnp.arange(length).astype(jnp.float32)
    distance = position[:, None] - position[None, :]
    causal = distance >= 0.0
    return jnp.where(
        causal[None], jnp.exp(jnp.where(causal, distance, 0.0)[None] * log_rate[:, None, None]), 0.0
    )


def retain_out(query_block, key_block_rows, value_block_rows, retention_state, log_rate):
    length = query_block.shape[1]
    scores = (
        jnp.einsum("sthk,sqhk->shtq", query_block, key_block_rows, precision=highest_precision)
        * decay_matrix(length, log_rate)[None]
    )
    within = jnp.einsum("shtq,sqhv->sthv", scores, value_block_rows, precision=highest_precision)
    carried_state = jnp.einsum(
        "sthk,shkv->sthv",
        query_block * entry_weights(length, log_rate)[None, :, :, None],
        retention_state,
        precision=highest_precision,
    )
    return within + carried_state


def retain_low(query_low, key_low, query_wide, value_wide, retention_state, log_rate):
    length = query_low.shape[1]
    raw_scores = jnp.einsum(
        "sthk,sqhk->shtq", query_low, key_low, preferred_element_type=jnp.float32
    )
    scores = raw_scores * decay_matrix(length, log_rate)[None]
    within = jnp.einsum("shtq,sqhv->sthv", scores, value_wide, precision=highest_precision)
    carried_state = jnp.einsum(
        "sthk,shkv->sthv",
        query_wide * entry_weights(length, log_rate)[None, :, :, None],
        retention_state,
        precision=highest_precision,
    )
    return within + carried_state


def own_states(key_block_rows, value_block_rows, log_rate):
    length = key_block_rows.shape[1]
    return jnp.einsum(
        "sthk,sthv->shkv",
        key_block_rows * exit_weights(length, log_rate)[None, :, :, None],
        value_block_rows,
        precision=highest_precision,
    )


def combine_states(earlier, later):
    return (earlier[0] * later[0], later[0][None, :, None, None] * earlier[1] + later[1])


def gate_section(retained, swish_in, gain):
    return norm_rows(retained, gain) * jax.nn.silu(swish_in)


def mlp_section(act_gelu, act_up):
    return jax.nn.gelu(act_gelu) * act_up


def general(
    tokens,
    w_query,
    w_key,
    w_value,
    w_swish,
    w_output,
    w_gelu,
    w_up,
    w_down,
    gain_first,
    gain_second,
    gain_group,
    decay_rate,
    cotangent,
):
    f32 = jnp.float32
    bf16 = jnp.bfloat16
    gathered = (
        lax.all_gather(w_query, ("fsdp", "ctx"), axis=0, tiled=True),
        lax.all_gather(w_key, ("fsdp", "ctx"), axis=0, tiled=True),
        lax.all_gather(w_value, ("fsdp", "ctx"), axis=0, tiled=True),
        lax.all_gather(w_swish, ("fsdp", "ctx"), axis=0, tiled=True),
        lax.all_gather(w_output, ("fsdp", "ctx"), axis=0, tiled=True),
        lax.all_gather(w_gelu, ("fsdp", "ctx"), axis=0, tiled=True),
        lax.all_gather(w_up, ("fsdp", "ctx"), axis=0, tiled=True),
        lax.all_gather(w_down, ("fsdp", "ctx"), axis=0, tiled=True),
        lax.all_gather(gain_first, ("fsdp", "ctx"), axis=0, tiled=True),
        lax.all_gather(gain_second, ("fsdp", "ctx"), axis=0, tiled=True),
        lax.all_gather(gain_group, ("fsdp", "ctx"), axis=1, tiled=True),
    )
    (
        full_query,
        full_key,
        full_value,
        full_swish,
        full_output,
        full_gelu,
        full_up,
        full_down,
        full_first,
        full_second,
        full_group,
    ) = gathered
    log_rate = jnp.log(decay_rate)
    piece = tokens.shape[1]
    key_scale = full_query.shape[2] ** (-0.5)
    factor = jnp.exp(piece * log_rate)
    inputs = tokens.astype(f32)
    first_gain = full_first.astype(f32)
    second_gain = full_second.astype(f32)
    group_gain = full_group.astype(f32)
    first_low = norm_rows(inputs, first_gain).astype(bf16)
    query_block = jnp.einsum(
        "spd,dhk->sphk", first_low, full_query, preferred_element_type=f32
    ).astype(bf16)
    key_block_rows = (
        jnp.einsum("spd,dhk->sphk", first_low, full_key, preferred_element_type=f32) * key_scale
    ).astype(bf16)
    value_block_rows = jnp.einsum(
        "spd,dhv->sphv", first_low, full_value, preferred_element_type=f32
    ).astype(bf16)
    swish_in = jnp.einsum("spd,dhv->sphv", first_low, full_swish, preferred_element_type=f32)
    query_wide = query_block.astype(f32)
    key_wide = key_block_rows.astype(f32)
    value_wide = value_block_rows.astype(f32)
    local_state = own_states(key_wide, value_wide, log_rate)
    identity = (jnp.ones_like(factor), jnp.zeros_like(local_state))
    _, entering = prefix((factor, local_state), "ctx", combine_states, identity)
    retained = retain_low(query_block, key_block_rows, query_wide, value_wide, entering, log_rate)
    gated = gate_section(retained, swish_in, group_gain).astype(bf16)
    attn_terms = jnp.einsum("sphv,dhv->spd", gated, full_output, preferred_element_type=f32)
    hidden = inputs + lax.psum(attn_terms, "tp")
    second_low = norm_rows(hidden, second_gain).astype(bf16)
    act_gelu = jnp.einsum("spd,df->spf", second_low, full_gelu, preferred_element_type=f32)
    act_up = jnp.einsum("spd,df->spf", second_low, full_up, preferred_element_type=f32)
    mixed = mlp_section(act_gelu, act_up).astype(bf16)
    mlp_terms = jnp.einsum("spf,df->spd", mixed, full_down, preferred_element_type=f32)
    result = hidden + lax.psum(mlp_terms.astype(jnp.bfloat16), "tp").astype(jnp.float32)
    back_query, back_key, back_value, back_swish, back_output, back_gelu, back_up, back_down = gathered[:8]
    grad_mixed = jnp.einsum("spd,df->spf", cotangent, back_down, preferred_element_type=f32)
    grad_down = jnp.einsum("spd,spf->df", cotangent, mixed, preferred_element_type=f32).astype(bf16)
    _, pull_mlp = jax.vjp(mlp_section, act_gelu, act_up)
    grad_act_gelu, grad_act_up = pull_mlp(grad_mixed)
    gelu_low = grad_act_gelu.astype(bf16)
    up_low = grad_act_up.astype(bf16)
    grad_gelu = jnp.einsum("spd,spf->df", second_low, gelu_low, preferred_element_type=f32).astype(bf16)
    grad_up = jnp.einsum("spd,spf->df", second_low, up_low, preferred_element_type=f32).astype(bf16)
    second_terms = jnp.einsum(
        "spf,df->spd", gelu_low, back_gelu, preferred_element_type=f32
    ) + jnp.einsum("spf,df->spd", up_low, back_up, preferred_element_type=f32)
    grad_second_in = lax.psum(second_terms, "tp")
    _, pull_second = jax.vjp(norm_rows, hidden, second_gain)
    hidden_from_norm, grad_second = pull_second(grad_second_in)
    grad_hidden = cotangent.astype(f32) + hidden_from_norm
    hidden_low = grad_hidden.astype(bf16)
    grad_gated = jnp.einsum("spd,dhv->sphv", hidden_low, back_output, preferred_element_type=f32)
    grad_output = jnp.einsum("spd,sphv->dhv", hidden_low, gated, preferred_element_type=f32).astype(bf16)
    _, pull_gate = jax.vjp(gate_section, retained, swish_in, group_gain)
    grad_retained, grad_swish_in, grad_group = pull_gate(grad_gated)
    swish_low = grad_swish_in.astype(bf16)
    entry_grad = jnp.einsum(
        "sthk,sthv->shkv",
        query_wide * entry_weights(piece, log_rate)[None, :, :, None],
        grad_retained,
        precision=highest_precision,
    )
    _, later_grad = entering_2((factor, entry_grad), "ctx", combine_states, identity)
    _, pull_retain = jax.vjp(
        lambda rows_q, rows_k, rows_v: (
            retain_out(rows_q, rows_k, rows_v, entering, log_rate),
            own_states(rows_k, rows_v, log_rate),
        ),
        query_wide,
        key_wide,
        value_wide,
    )
    grad_query_act, grad_key_act, grad_value_act = pull_retain((grad_retained, later_grad))
    query_low = grad_query_act.astype(bf16)
    key_low = (grad_key_act.astype(bf16).astype(f32) * key_scale).astype(bf16)
    value_low = grad_value_act.astype(bf16)
    grad_query = jnp.einsum("spd,sphk->dhk", first_low, query_low, preferred_element_type=f32).astype(bf16)
    grad_key = jnp.einsum("spd,sphk->dhk", first_low, key_low, preferred_element_type=f32).astype(bf16)
    grad_value = jnp.einsum("spd,sphv->dhv", first_low, value_low, preferred_element_type=f32).astype(bf16)
    grad_swish = jnp.einsum("spd,sphv->dhv", first_low, swish_low, preferred_element_type=f32).astype(bf16)
    first_terms = jnp.einsum("sphk,dhk->spd", query_low, back_query, preferred_element_type=f32)
    first_terms = first_terms + jnp.einsum(
        "sphk,dhk->spd", key_low, back_key, preferred_element_type=f32
    )
    first_terms = first_terms + jnp.einsum(
        "sphv,dhv->spd", value_low, back_value, preferred_element_type=f32
    )
    first_terms = first_terms + jnp.einsum(
        "sphv,dhv->spd", swish_low, back_swish, preferred_element_type=f32
    )
    grad_first_in = lax.psum(first_terms.astype(jnp.bfloat16), "tp").astype(jnp.float32)
    _, pull_first = jax.vjp(norm_rows, inputs, first_gain)
    tokens_from_norm, grad_first = pull_first(grad_first_in)
    grad_tokens = grad_hidden + tokens_from_norm
    owned = tuple(
        lax.psum_scatter(g, ("fsdp", "ctx"), scatter_dimension=0, tiled=True).astype(f32)
        for g in (grad_query, grad_key, grad_value, grad_swish, grad_output, grad_gelu, grad_up, grad_down, grad_first, grad_second)
    ) + (lax.psum_scatter(grad_group, ("fsdp", "ctx"), scatter_dimension=1, tiled=True),)
    return (
        result,
        grad_tokens,
        owned[0],
        owned[1],
        owned[2],
        owned[3],
        owned[4],
        owned[5],
        owned[6],
        owned[7],
        owned[8],
        owned[9],
        owned[10],
    )


def solution(mesh):
    wide, flat = P(("fsdp", "ctx"), "tp", None), P(("fsdp", "ctx"), "tp")
    tok, row, group = P("fsdp", "ctx", None), P(("fsdp", "ctx")), P("tp", ("fsdp", "ctx"))
    in_specs = (tok,) + (wide,) * 5 + (flat,) * 3 + (row, row, group, P("tp"), tok)
    out_specs = (tok, tok) + (wide,) * 5 + (flat,) * 3 + (row, row, group)
    sizes = (mesh.shape["fsdp"], mesh.shape["ctx"], mesh.shape["tp"])
    local = fused if sizes == (2, 2 * ZN, 2) else general
    return jax.shard_map(local, mesh=mesh, in_specs=in_specs, out_specs=out_specs, check_vma=False)
```

```python
import types

import jax
import jax.numpy as jnp
from jax import lax
from jax.experimental import pallas as pl
from jax.experimental.pallas import tpu as pltpu
from jax.sharding import PartitionSpec as P

MESH = pl.DeviceIdType.MESH
BF = jnp.bfloat16
F32 = jnp.float32

ZN = 4
BLK = 128
HALF = 64
TOK = ZN * BLK
D = 2048
CH = 512
NCH = 7
NC = 4
AC = 4
AR = HALF // AC
SETS = 4
VLIM = 62 * 2**20


def nt(a, b):
    return lax.dot_general(a, b, (((1,), (1,)), ((), ())), preferred_element_type=F32)


def nn(a, b):
    return lax.dot_general(a, b, (((1,), (0,)), ((), ())), preferred_element_type=F32)


def normed(v):
    center = v - jnp.mean(v, axis=-1, keepdims=True)
    rstd = lax.rsqrt(jnp.mean(center * center, axis=-1, keepdims=True) + 1e-05)
    return center * rstd, rstd


def norm_back(n, rstd, g):
    return rstd * (
        g - jnp.mean(g, axis=-1, keepdims=True) - n * jnp.mean(g * n, axis=-1, keepdims=True)
    )


def remote(src, dst, ss, rs, dev):
    return pltpu.make_async_remote_copy(src, dst, ss, rs, device_id=dev, device_id_type=MESH)


SCRATCH = dict(
    gall=((16, 8, 128), F32),
    W=((NCH, 16, BLK, CH), BF),
    first=((ZN, BLK, D), BF),
    cot=((ZN, BLK, D), BF),
    second=((ZN, BLK, D), BF),
    hlow=((ZN, BLK, D), BF),
    XT=((16, BLK, TOK), BF),
    qkv=((2, TOK, 1024), BF),
    swish=((TOK, CH), F32),
    ret=((TOK, CH), F32),
    dr=((TOK, CH), BF),
    YB=((NCH, TOK, CH), BF),
    dkv_s=((TOK, 768), BF),
    dkv_r=((TOK, 768), BF),
    tmp=((3, TOK, 256), F32),
    ysend=((2, NC, ZN, HALF, CH), BF),
    yrecv=((2, NC, ZN, HALF, CH), BF),
    zsend=((2, NC, ZN, HALF, CH), BF),
    zrecv=((2, NC, ZN + 1, HALF, CH), BF),
    hidden=((HALF, D), F32),
    ghid=((HALF, D), F32),
    rsum=((HALF, D), F32),
    ostage=((2, HALF, D), BF),
    gcs=((2, ZN, BLK, CH), BF),
    gcr=((SETS, 2, ZN, BLK, CH), BF),
    gxs=((SETS, ZN, BLK, CH), BF),
    gxr=((SETS, ZN, BLK, CH), BF),
    gzs=((SETS, ZN, BLK, CH), BF),
    vec=((8, D), F32),
    vrc=((8, D), F32),
    vrx=((8, D), F32),
    vry=((8, D), F32),
    vz=((ZN, 8, D), F32),
)
SEMS = dict(
    g_s=(3, 8), g_r=(3, 8),
    wz_s=(NCH, 3), wz_r=(NCH, 3), wx_s=(NCH, 4), wx_r=(NCH, 4), wc_s=(NCH, 8), wc_r=(NCH, 8), wl=(NCH,),
    az_s=(4, AC, 2, ZN), az_r=(4, AC, ZN), ay_s=(4, AC, ZN), ay_r=(4, AC, ZN),
    ry_s=(4, NC), ry_r=(4, NC), rz_s=(4, NC, ZN), rz_r=(4, NC, ZN + 1),
    kv_s=(2,), kv_r=(2,),
    gc_s=(NCH, 2), gc_r=(NCH, 2), gx_s=(NCH,), gx_r=(NCH,), gz_s=(NCH, 3), gz_r=(NCH, 3), gl=(NCH,),
    v_s=(6,), v_r=(6,), o_s=(2,), o_r=(2,), ol=(4,),
    credit=None,
)
NAMES = list(SCRATCH) + list(SEMS)


def kernel(tok, gp, lr, cot_in, pk, wg, wu, wd, res_o, gtok_o, gwa_o, gwf_o, vec_o, *scratch):
    s = types.SimpleNamespace(**dict(zip(NAMES, scratch)))
    W, YB, XT = s.W, s.YB, s.XT
    x, k, y = lax.axis_index("fsdp"), lax.axis_index("ctx"), lax.axis_index("tp")
    z, c = k // 2, k % 2
    zup = [lax.rem(z + i, ZN) for i in range(ZN)]
    zdn = [lax.rem(z + ZN - i, ZN) for i in range(ZN)]
    zdev = [(x, zup[i] * 2 + c, y) for i in range(ZN)]
    updev, dndev = zdev[1], zdev[ZN - 1]
    xdev, ydev, cdev = (1 - x, k, y), (x, k, 1 - y), (x, z * 2 + 1 - c, y)
    peers = range(1, ZN)

    def place(xx, zz, cc):
        return xx * 8 + zz * 2 + cc

    me = place(x, z, c)
    log_rate = lr[z]

    def loop(n, f):
        def step(i, carry):
            f(i)
            return carry

        lax.fori_loop(0, n, step, 0)

    barrier = pltpu.get_barrier_semaphore()
    for dev in zdev[1:] + [xdev, ydev, cdev]:
        pl.semaphore_signal(barrier, inc=1, device_id=dev, device_id_type=MESH)
    pl.semaphore_wait(barrier, 6)

    def w_src(n, zz):
        if n < 4:
            return pk.at[zz, :, pl.ds(n * CH, CH)]
        return (wg, wu, wd)[n - 4].at[:, pl.ds(pl.multiple_of(zz * CH, CH), CH)]

    def w_local(n, zz):
        return pltpu.make_async_copy(w_src(n, zz), W.at[n, me], s.wl.at[n])

    def w_piece(n, i):
        remote(w_src(n, zup[i]), W.at[n, me], s.wz_s.at[n, i - 1], s.wz_r.at[n, i - 1], zdev[i]).start()

    def w_send(n):
        for i in peers:
            w_piece(n, i)

    def w_z(n, i):
        blk = W.at[n, place(x, zdn[i], c)]
        return remote(blk, blk, s.wz_s.at[n, i - 1], s.wz_r.at[n, i - 1], zdev[i])

    def w_x(n, j, xx):
        blk = W.at[n, place(xx, zdn[j], c)]
        return remote(blk, blk, s.wx_s.at[n, j], s.wx_r.at[n, j], xdev)

    def w_c(n, j, cc):
        xx = x if j < 4 else 1 - x
        blk = W.at[n, place(xx, zdn[j % 4], cc)]
        return remote(blk, blk, s.wc_s.at[n, j], s.wc_r.at[n, j], cdev)

    def w_own(n):
        pltpu.make_async_copy(W.at[n, me], W.at[n, me], s.wl.at[n]).wait()
        w_x(n, 0, x).start()
        w_c(n, 0, c).start()

    def pump_z(n):
        for i in peers:
            w_z(n, i).wait_recv()
            w_x(n, i, x).start()
            w_c(n, i, c).start()

    def pump_x(n):
        for j in range(ZN):
            w_x(n, j, 1 - x).wait_recv()
            w_c(n, ZN + j, c).start()

    def w_fin(n):
        for j in range(8):
            w_c(n, j, 1 - c).wait_recv()

    def w_done(n):
        for i in peers:
            w_z(n, i).wait_send()
        for j in range(ZN):
            w_x(n, j, x).wait_send()
        for j in range(8):
            w_c(n, j, c).wait_send()

    def a_rows(yy, ch):
        return pl.ds(pl.multiple_of(yy * HALF + ch * AR, AR), AR)

    def a_z(buf, ia, ch, zz, way):
        blk = buf.at[zz, a_rows(y, ch)]
        return remote(blk, blk, s.az_s.at[ia, ch, way, zz], s.az_r.at[ia, ch, zz], (updev, dndev)[way])

    def a_y(buf, ia, ch, zz, yy):
        blk = buf.at[zz, a_rows(yy, ch)]
        return remote(blk, blk, s.ay_s.at[ia, ch, zz], s.ay_r.at[ia, ch, zz], ydev)

    def ag_sends(buf, ia, ch, zz, do):
        pl.when((zz <= z) & (z < ZN - 1))(lambda: do(a_z(buf, ia, ch, zz, 0)))
        pl.when((zz >= z) & (z > 0))(lambda: do(a_z(buf, ia, ch, zz, 1)))

    def ag_send(buf, ia, own):
        def f(ch):
            ag_sends(buf, ia, ch, z, lambda copy: copy.start())
            if own:
                a_y(buf, ia, ch, z, y).start()

        loop(AC, f)

    def ag_forward(buf, ia, d):
        def f(ch):
            def pass_on(zz):
                a_z(buf, ia, ch, zz, 0).wait_recv()
                ag_sends(buf, ia, ch, zz, lambda copy: copy.start())
                a_y(buf, ia, ch, zz, y).start()

            pl.when(z >= d)(lambda: pass_on(z - d))
            pl.when(z + d < ZN)(lambda: pass_on(z + d))

        loop(AC, f)

    def ag_wait(buf, ia, own):
        def f(ch):
            for i in range(0 if own else 1, ZN):
                a_y(buf, ia, ch, zdn[i], 1 - y).wait_recv()

        loop(AC, f)

    def ag_done(buf, ia, own):
        def f(ch):
            for i in range(ZN):
                ag_sends(buf, ia, ch, zdn[i], lambda copy: copy.wait_send())
                if own or i > 0:
                    a_y(buf, ia, ch, zdn[i], y).wait_send()

        loop(AC, f)

    def product(chunks, j, yy):
        total = None
        for n in chunks:
            rows = [YB[n, pl.ds(pl.multiple_of(zz * BLK + yy * HALF, HALF), HALF), :] for zz in range(ZN)]
            lhs = jnp.concatenate(rows, axis=0)
            rhs = W[n, pl.ds(j * 4, 4)].reshape(CH, CH)
            part = nt(lhs, rhs)
            total = part if total is None else total + part
        return total.reshape(ZN, HALF, CH)

    def r_y(ir, b, j):
        return remote(s.ysend.at[b, j], s.yrecv.at[b, j], s.ry_s.at[ir, j], s.ry_r.at[ir, j], ydev)

    def r_z(ir, b, j, d, way):
        slot = d if way == 0 else jnp.where(d == z - 1, ZN, d)
        return remote(
            s.zsend.at[b, j, d], s.zrecv.at[b, j, slot], s.rz_s.at[ir, j, d], s.rz_r.at[ir, j, slot], (updev, dndev)[way]
        )

    def r_arrived(ir, b, j, slot):
        there = s.zrecv.at[b, j, slot]
        remote(there, there, s.rz_s.at[ir, j, 0], s.rz_r.at[ir, j, slot], updev).wait_recv()

    def rs_a(ir, b, chunks):
        def f(j):
            s.ysend[b, j] = product(chunks, j, 1 - y).astype(BF)
            r_y(ir, b, j).start()

        loop(NC, f)

    def r_pass(ir, b, j, level):
        def go(dests, way):
            for d in dests:
                if level > 0:
                    r_arrived(ir, b, j, d)
                    s.zsend[b, j, d] = (s.zsend[b, j, d].astype(F32) + s.zrecv[b, j, d].astype(F32)).astype(BF)
                r_z(ir, b, j, d, way).start()

        pl.when(z == level)(lambda: go(range(ZN - 1, level, -1), 0))
        pl.when(z == ZN - 1 - level)(lambda: go(range(ZN - 1 - level), 1))

    def rs_b(ir, b, chunks, between):
        for j in range(NC + 2):
            if j < NC:
                own = product(chunks, j, y)
                r_y(ir, b, j).wait_recv()
                s.zsend[b, j] = (own + s.yrecv[b, j].astype(F32)).astype(BF)
                r_pass(ir, b, j, 0)
            if 1 <= j <= NC:
                r_pass(ir, b, j - 1, 1)
            if j >= 2:
                r_pass(ir, b, j - 2, 2)
            for job in between.get(j, ()):
                job()

    def rs_c(ir, b):
        def f(j):
            cols = pl.ds(pl.multiple_of(j * CH, CH), CH)
            s.rsum[:, cols] = s.zsend[b, j, z].astype(F32)

            def add(slot):
                r_arrived(ir, b, j, slot)
                s.rsum[:, cols] = s.rsum[:, cols] + s.zrecv[b, j, slot].astype(F32)

            pl.when(z > 0)(lambda: add(z))
            pl.when(z < ZN - 1)(lambda: add(ZN))

        loop(NC, f)

    def rs_done(ir, b):
        def f(j):
            r_y(ir, b, j).wait_send()
            for i in peers:
                r_z(ir, b, j, zdn[i], 0).wait_send()

        loop(NC, f)

    def transpose(buf):
        def f(q):
            cols = pl.ds(pl.multiple_of(q * BLK, BLK), BLK)
            XT[q] = buf[:, :, cols].reshape(TOK, BLK).T

        loop(16, f)

    def grad_rows(n, xx, cc):
        lhs = jnp.concatenate([XT[place(xx, zz, cc)] for zz in range(ZN)], axis=0)
        return nn(lhs, YB[n]).reshape(ZN, BLK, CH)

    def g_c(n, xx):
        return remote(s.gcs.at[xx], s.gcr.at[n % SETS, xx], s.gc_s.at[n, xx], s.gc_r.at[n, xx], cdev)

    def g_x(n):
        return remote(s.gxs.at[n % SETS], s.gxr.at[n % SETS], s.gx_s.at[n], s.gx_r.at[n], xdev)

    def g_dst(n):
        if n < 4:
            return gwa_o.at[n, z]
        return gwf_o.at[n - 4, :, pl.ds(pl.multiple_of(z * CH, CH), CH)]

    def g_z(n, i):
        return remote(s.gzs.at[n % SETS, zup[i]], g_dst(n), s.gz_s.at[n, i - 1], s.gz_r.at[n, i - 1], zdev[i])

    def g_local(n):
        return pltpu.make_async_copy(s.gzs.at[n % SETS, z], g_dst(n), s.gl.at[n])

    def grad_a(n, first_use):
        b = n % SETS

        def f(t):
            xx = (1 - x) * (1 - t) + x * t
            s.gcs[xx] = grad_rows(n, xx, 1 - c).astype(BF)
            g_c(n, xx).start()

        loop(2, f)
        own = grad_rows(n, 1 - x, c)
        g_c(n, 1 - x).wait_recv()
        if not first_use:
            pl.semaphore_wait(s.credit, 1)
        s.gxs[b] = (own + s.gcr[b, 1 - x].astype(F32)).astype(BF)
        g_x(n).start()
        own = grad_rows(n, x, c)
        g_c(n, x).wait_recv()
        s.gzs[b] = (own + s.gcr[b, x].astype(F32)).astype(BF)
        for xx in range(2):
            g_c(n, xx).wait_send()

    def grad_b(n, more):
        b = n % SETS
        g_x(n).wait_recv()
        s.gzs[b] = (s.gzs[b].astype(F32) + s.gxr[b].astype(F32)).astype(BF)
        for i in peers:
            g_z(n, i).start()
        g_local(n).start()
        g_x(n).wait_send()
        if more:
            pl.semaphore_signal(s.credit, inc=1, device_id=xdev, device_id_type=MESH)

    def grad_sent(n):
        for i in peers:
            g_z(n, i).wait_send()
        g_local(n).wait()

    def grad_done(n):
        for i in peers:
            g_z(n, i).wait_recv()

    def gain_row(r):
        return jnp.concatenate([s.gall[q, r : r + 1, :] for q in range(16)], axis=1)

    def group_gain():
        pick = lax.broadcasted_iota(jnp.int32, (8, 128), 0) == 2 + z
        parts = []
        for r in range(4):
            total = s.gall[4 * r]
            for q in range(4 * r + 1, 4 * r + 4):
                total = total + s.gall[q]
            parts.append(jnp.sum(jnp.where(pick, total, 0.0), axis=0, keepdims=True))
        return jnp.concatenate(parts, axis=1)

    def position(shape, dim, both, start):
        r = lax.broadcasted_iota(jnp.int32, shape, dim) + start
        if both:
            core, r = r // TOK, lax.rem(r, TOK)
        else:
            core = c
        return r + (r // BLK) * BLK + core * BLK

    def decay(later, earlier):
        gap = later - earlier
        keep = gap >= 0
        return jnp.where(keep, jnp.exp(jnp.where(keep, gap, 0).astype(F32) * log_rate), 0.0)

    own_rows = pl.ds(pl.multiple_of(y * HALF, HALF), HALF)

    gall = s.gall
    gall[me] = gp[...]

    def g_gain(j, i, dev, q):
        return remote(gall.at[q], gall.at[q], s.g_s.at[j, i], s.g_r.at[j, i], dev)

    for i in peers:
        g_gain(0, i, zdev[i], me).start()
    w_send(0)
    for n in range(NCH):
        w_local(n, z).start()
    cot_local = pltpu.make_async_copy(cot_in, s.cot.at[z], s.ol.at[0])
    cot_local.start()
    for i in peers:
        g_gain(0, i, zdev[i], place(x, zdn[i], c)).wait_recv()
    for i in range(ZN):
        g_gain(1, i, xdev, place(x, zdn[i], c)).start()
    for i in range(ZN):
        g_gain(2, i, cdev, place(x, zdn[i], c)).start()
    for i in range(ZN):
        g_gain(1, i, xdev, place(1 - x, zdn[i], c)).wait_recv()
        g_gain(2, ZN + i, cdev, place(1 - x, zdn[i], c)).start()
    for i in range(8):
        xx = x if i < ZN else 1 - x
        g_gain(2, i, cdev, place(xx, zdn[i % ZN], 1 - c)).wait_recv()
    for i in peers:
        g_gain(0, i, zdev[i], me).wait_send()
    for i in range(ZN):
        g_gain(1, i, xdev, place(x, zdn[i], c)).wait_send()
    for i in range(8):
        xx = x if i < ZN else 1 - x
        g_gain(2, i, cdev, place(xx, zdn[i % ZN], c)).wait_send()

    for n in range(4):
        w_own(n)
    tokens = tok[...].astype(F32)
    n_first, _ = normed(tokens)
    s.first[z] = (n_first * gain_row(0)).astype(BF)
    ag_send(s.first, 0, False)
    for n in range(1, 4):
        w_send(n)
    pump_z(0)
    ag_forward(s.first, 0, 1)
    pump_x(0)
    ag_forward(s.first, 0, 2)
    ag_forward(s.first, 0, 3)
    pump_z(1)
    ag_wait(s.first, 0, False)
    cot_local.wait()
    ag_send(s.cot, 1, False)
    for n in range(4, NCH):
        w_send(n)
        w_own(n)

    qkv, swish = s.qkv, s.swish

    def columns(n, t):
        return W[n, :, :, pl.ds(pl.multiple_of(t * 256, 256), 256)].reshape(D, 256)

    w_fin(0)

    def project_qk(t):
        scale = jnp.where(t == 1, 0.0625, 1.0)
        out = nn(s.first[...].reshape(TOK, D), columns(0, t)) * scale
        qkv[c, :, pl.ds(pl.multiple_of(t * 256, 256), 256)] = out.astype(BF)

    loop(2, project_qk)
    pump_z(2)
    pump_x(1)
    w_fin(1)

    def project_v(t):
        out = nn(s.first[...].reshape(TOK, D), columns(1, t))
        qkv[c, :, pl.ds(pl.multiple_of(512 + t * 256, 256), 256)] = out.astype(BF)

    loop(2, project_v)

    def kv_copy(cc):
        blk = qkv.at[cc, :, pl.ds(256, 768)]
        return remote(blk, blk, s.kv_s.at[0], s.kv_r.at[0], cdev)

    kv_copy(c).start()
    pump_z(3)
    pump_x(2)
    kv_copy(1 - c).wait_recv()

    def all_keys():
        return qkv[:, :, 256:512].reshape(2 * TOK, 256)

    def all_values():
        return qkv[:, :, 512:1024].reshape(2 * TOK, CH)

    def retain(h):
        rows = pl.ds(pl.multiple_of(h * 256, 256), 256)
        later = position((256, 2 * TOK), 0, False, h * 256)
        earlier = position((256, 2 * TOK), 1, True, 0)
        scores = nt(qkv[c, rows, 0:256], all_keys()) * decay(later, earlier)
        s.ret[rows, :] = nn(scores.astype(BF), all_values())

    loop(2, retain)
    w_fin(2)

    def project_s(t):
        out = nn(s.first[...].reshape(TOK, D), columns(2, t))
        swish[:, pl.ds(pl.multiple_of(t * 256, 256), 256)] = out

    loop(2, project_s)
    gain_g = group_gain()

    def gate(h):
        rows = pl.ds(pl.multiple_of(h * BLK, BLK), BLK)
        n, _ = normed(s.ret[rows, :])
        w = swish[rows, :]
        YB[3, rows, :] = (n * gain_g * (w / (1.0 + jnp.exp(-w)))).astype(BF)

    loop(ZN, gate)
    pump_x(3)
    w_fin(3)

    rs_a(0, 0, (3,))
    rs_b(
        0,
        0,
        (3,),
        {
            0: (lambda: ag_forward(s.cot, 1, 1), lambda: pump_z(4)),
            1: (lambda: ag_forward(s.cot, 1, 2), lambda: pump_x(4)),
            2: (lambda: ag_forward(s.cot, 1, 3), lambda: pump_z(5)),
            3: (lambda: pump_x(5), lambda: pump_z(6)),
        },
    )
    rs_c(0, 0)
    hidden = tok[own_rows, :].astype(F32) + s.rsum[...]
    s.hidden[...] = hidden
    n_second, _ = normed(hidden)
    s.second[z, own_rows, :] = (n_second * gain_row(1)).astype(BF)
    ag_send(s.second, 2, True)
    ag_forward(s.second, 2, 1)
    ag_forward(s.second, 2, 2)
    ag_forward(s.second, 2, 3)
    pump_x(6)
    for n in range(4, NCH):
        w_fin(n)
    ag_wait(s.cot, 1, False)
    ag_wait(s.second, 2, True)

    tmp = s.tmp

    def feed(t):
        cols = pl.ds(pl.multiple_of(t * 256, 256), 256)
        sec = s.second[...].reshape(TOK, D)
        tmp[0] = nn(sec, columns(4, t))
        tmp[1] = nn(sec, columns(5, t))
        tmp[2] = nn(s.cot[...].reshape(TOK, D), columns(6, t))

        def act(h):
            rows = pl.ds(pl.multiple_of(h * HALF, HALF), HALF)
            a, u, gm = tmp[0, rows, :], tmp[1, rows, :], tmp[2, rows, :]
            root = 0.7978845608028654
            th = jnp.tanh(root * (a + 0.044715 * (a * a * a)))
            half = 0.5 * (1.0 + th)
            gelu = a * half
            slope = half + 0.5 * a * (1.0 - th * th) * (root * (1.0 + 0.134145 * (a * a)))
            YB[6, rows, cols] = (gelu * u).astype(BF)
            YB[4, rows, cols] = (gm * u * slope).astype(BF)
            YB[5, rows, cols] = (gm * gelu).astype(BF)

        loop(TOK // HALF, act)

    loop(2, feed)
    rs_done(0, 0)
    rs_a(1, 0, (4, 5))
    rs_b(
        1,
        0,
        (4, 5),
        {
            0: (lambda: transpose(s.second),),
            1: (lambda: grad_a(4, True),),
            2: (lambda: grad_a(5, True),),
            3: (lambda: transpose(s.cot),),
            4: (lambda: grad_a(6, True),),
        },
    )
    rs_c(1, 0)
    n_second, rstd = normed(s.hidden[...])
    g_in = s.rsum[...]
    s.vec[1:2, :] = jnp.sum(g_in * n_second, axis=0, keepdims=True)
    ghid = s.cot[z, own_rows, :].astype(F32) + norm_back(n_second, rstd, g_in * gain_row(1))
    s.ghid[...] = ghid
    s.hlow[z, own_rows, :] = ghid.astype(BF)
    ag_send(s.hlow, 3, True)
    ag_forward(s.hlow, 3, 1)
    grad_b(4, True)
    ag_forward(s.hlow, 3, 2)
    ag_forward(s.hlow, 3, 3)
    grad_b(5, True)
    grad_b(6, True)
    rs_a(2, 1, (6,))
    ag_wait(s.hlow, 3, True)

    def back_gated(t):
        tmp[t] = nn(s.hlow[...].reshape(TOK, D), columns(3, t))

    loop(2, back_gated)

    def back_gate(h, total):
        rows = pl.ds(pl.multiple_of(h * BLK, BLK), BLK)
        n, rstd = normed(s.ret[rows, :])
        w, g = swish[rows, :], jnp.concatenate([tmp[0, rows, :], tmp[1, rows, :]], axis=1)
        sig = 1.0 / (1.0 + jnp.exp(-w))
        silu = w * sig
        YB[2, rows, :] = (g * (n * gain_g) * (sig * (1.0 + w * (1.0 - sig)))).astype(BF)
        gs = g * silu
        s.dr[rows, :] = norm_back(n, rstd, gs * gain_g).astype(BF)
        return total + jnp.sum(gs * n, axis=0, keepdims=True)

    transpose(s.hlow)
    grad_a(3, True)
    group = lax.fori_loop(0, ZN, back_gate, jnp.zeros((1, CH), F32))
    s.vec[2:3, 0:CH] = group

    def back_keys(core, h):
        rows = pl.ds(pl.multiple_of(h * 256, 256), 256)
        keys, values = qkv[core, rows, 256:512], qkv[core, rows, 512:1024]
        query = qkv[c, :, 0:256]
        r = lax.broadcasted_iota(jnp.int32, (256, TOK), 0) + h * 256
        earlier = r + (r // BLK) * BLK + core * BLK
        table = decay(position((256, TOK), 1, False, 0), earlier)
        weights = (nt(keys, query) * table).astype(BF)
        slopes = (nt(values, s.dr[...]) * table).astype(BF)
        return rows, nn(slopes, query), nn(weights, s.dr[...])

    def back_other(h):
        rows, dk, dv = back_keys(1 - c, h)
        s.dkv_s[rows, 0:256] = dk.astype(BF)
        s.dkv_s[rows, 256:768] = dv.astype(BF)

    def back_own(h):
        rows, dk, dv = back_keys(c, h)
        tmp[0, rows, :] = dk
        tmp[1, rows, :] = dv[:, 0:256]
        tmp[2, rows, :] = dv[:, 256:512]

    loop(2, back_other)
    dkv_copy = remote(s.dkv_s, s.dkv_r, s.kv_s.at[1], s.kv_r.at[1], cdev)
    dkv_copy.start()
    loop(2, back_own)

    def back_query(h):
        rows = pl.ds(pl.multiple_of(h * 256, 256), 256)
        later = position((256, 2 * TOK), 0, False, h * 256)
        earlier = position((256, 2 * TOK), 1, True, 0)
        slopes = nt(s.dr[rows, :], all_values()) * decay(later, earlier)
        YB[0, rows, 0:256] = nn(slopes.astype(BF), all_keys()).astype(BF)

    loop(2, back_query)
    dkv_copy.wait_recv()

    def back_sum(h):
        rows = pl.ds(pl.multiple_of(h * BLK, BLK), BLK)
        other = s.dkv_r[rows, :].astype(F32)
        YB[0, rows, 256:512] = ((tmp[0, rows, :] + other[:, 0:256]) * 0.0625).astype(BF)
        YB[1, rows, 0:256] = (tmp[1, rows, :] + other[:, 256:512]).astype(BF)
        YB[1, rows, 256:512] = (tmp[2, rows, :] + other[:, 512:768]).astype(BF)

    loop(ZN, back_sum)

    rs_done(1, 0)
    rs_a(3, 0, (0, 1, 2))
    rs_b(2, 1, (6,), {})
    for n in (4, 5, 6):
        grad_sent(n)
    rs_b(
        3,
        0,
        (0, 1, 2),
        {
            0: (lambda: transpose(s.first), lambda: grad_a(0, False)),
            1: (lambda: grad_a(1, False),),
            2: (lambda: grad_a(2, False),),
            3: (lambda: grad_b(0, False),),
            4: (lambda: grad_b(1, False),),
        },
    )
    rs_c(3, 0)
    n_first, rstd = normed(tok[own_rows, :].astype(F32))
    g_in = s.rsum[...]
    s.vec[0:1, :] = jnp.sum(g_in * n_first, axis=0, keepdims=True)
    g_tok = s.ghid[...] + norm_back(n_first, rstd, g_in * gain_row(0))
    s.ostage[0] = g_tok.astype(BF)

    def out_copies(j, dst):
        there = dst.at[own_rows]
        return (
            remote(s.ostage.at[j], there, s.o_s.at[j], s.o_r.at[j], ydev),
            pltpu.make_async_copy(s.ostage.at[j], there, s.ol.at[1 + j]),
        )

    for copy in out_copies(0, gtok_o):
        copy.start()
    grad_b(2, False)
    grad_b(3, False)
    rs_c(2, 1)
    s.ostage[1] = (s.hidden[...] + s.rsum[...]).astype(BF)
    for copy in out_copies(1, res_o):
        copy.start()

    vec = s.vec

    def v_copy(j, dst, dev):
        return remote(vec, dst, s.v_s.at[j], s.v_r.at[j], dev)

    vec[3:8, :] = jnp.zeros((5, D), F32)
    vec[2:3, CH:D] = jnp.zeros((1, D - CH), F32)
    for j, (dst, dev) in enumerate(((s.vrc, cdev), (s.vrx, xdev), (s.vry, ydev))):
        copy = v_copy(j, dst, dev)
        copy.start()
        copy.wait()
        if j < 2:
            vec[...] = vec[...] + dst[...]
        else:
            vec[0:2, :] = vec[0:2, :] + dst[0:2, :]
    s.vz[z] = vec[...]
    for i in peers:
        remote(vec, s.vz.at[z], s.v_s.at[2 + i], s.v_r.at[2 + i], zdev[i]).start()
    for i in peers:
        there = s.vz.at[zdn[i]]
        copy = remote(there, there, s.v_s.at[2 + i], s.v_r.at[2 + i], zdev[i])
        copy.wait_recv()
    for i in peers:
        remote(vec, s.vz.at[z], s.v_s.at[2 + i], s.v_r.at[2 + i], zdev[i]).wait_send()
    vz = s.vz
    vec_o[0:2, :] = ((vz[0, 0:2, :] + vz[1, 0:2, :]) + vz[2, 0:2, :]) + vz[3, 0:2, :]
    vec_o[2:4, :] = jnp.zeros((2, D), F32)
    for zz in range(ZN):
        vec_o[4 + zz : 5 + zz, :] = vz[zz, 2:3, :]

    for j, dst in enumerate((gtok_o, res_o)):
        there = dst.at[pl.ds(pl.multiple_of((1 - y) * HALF, HALF), HALF)]
        a, b = out_copies(j, dst)
        a.wait_send()
        b.wait()
        remote(s.ostage.at[j], there, s.o_s.at[j], s.o_r.at[j], ydev).wait_recv()
    for n in range(4):
        grad_sent(n)
    for n in range(NCH):
        grad_done(n)
    loop(NCH, w_done)
    kv_copy(c).wait_send()
    dkv_copy.wait_send()
    for ia, (buf, own) in enumerate(((s.first, False), (s.cot, False), (s.second, True), (s.hlow, True))):
        ag_done(buf, ia, own)
    rs_done(2, 1)
    rs_done(3, 0)


def pieces(tokens, w_query, w_key, w_value, w_swish, w_output, w_gelu, w_up, w_down, gain_first, gain_second, gain_group, decay_rate, cotangent):
    me = lax.axis_index("fsdp") * 8 + lax.axis_index("ctx")
    pk = jnp.concatenate([w_query, w_key, w_value, w_swish, w_output], axis=2).transpose(1, 0, 2)
    lane = lax.broadcasted_iota(jnp.int32, (ZN, BLK), 1) // 32
    spread = jnp.where(lane == lax.rem(me, 4), jnp.tile(gain_group.astype(F32), (1, 4)), 0.0)
    gp = jnp.concatenate(
        [gain_first.astype(F32)[None], gain_second.astype(F32)[None], spread, jnp.zeros((2, BLK), F32)], axis=0
    )
    return (tokens[0], gp, jnp.log(decay_rate), cotangent[0], pk, w_gelu, w_up, w_down)


def fused(*args):
    shapes = [
        jax.ShapeDtypeStruct((BLK, D), BF),
        jax.ShapeDtypeStruct((BLK, D), BF),
        jax.ShapeDtypeStruct((4, ZN, BLK, CH), BF),
        jax.ShapeDtypeStruct((3, BLK, D), BF),
        jax.ShapeDtypeStruct((8, D), F32),
    ]
    hbm = pl.BlockSpec(memory_space=pl.ANY)
    vmem = pl.BlockSpec(memory_space=pltpu.VMEM)
    smem = pl.BlockSpec(memory_space=pltpu.SMEM)
    scratch = [pltpu.VMEM(*v) for v in SCRATCH.values()]
    for name, shape in SEMS.items():
        scratch.append(pltpu.SemaphoreType.REGULAR if shape is None else pltpu.SemaphoreType.DMA(shape))
    result, g_tok, gwa, gwf, vec = pl.pallas_call(
        kernel,
        out_shape=shapes,
        in_specs=[vmem, vmem, smem, hbm, hbm, hbm, hbm, hbm],
        out_specs=[hbm, hbm, hbm, hbm, vmem],
        scratch_shapes=scratch,
        compiler_params=pltpu.CompilerParams(collective_id=0, has_side_effects=True, vmem_limit_bytes=VLIM),
    )(*pieces(*args))
    me = lax.axis_index("fsdp") * 8 + lax.axis_index("ctx")
    swap = gwa.transpose(0, 2, 1, 3).astype(F32)
    gwf = gwf.astype(F32)
    g_first = lax.dynamic_slice(vec[0], (me * BLK,), (BLK,))
    g_second = lax.dynamic_slice(vec[1], (me * BLK,), (BLK,))
    g_group = lax.dynamic_slice(vec, (4, me * 32), (4, 32))
    return (
        result[None].astype(F32),
        g_tok[None].astype(F32),
        swap[0, :, :, 0:256],
        swap[0, :, :, 256:512],
        swap[1],
        swap[2],
        swap[3],
        gwf[0],
        gwf[1],
        gwf[2],
        g_first,
        g_second,
        g_group,
    )


highest_precision = lax.Precision.HIGHEST


def prefix(part, axis, combine, identity):
    place = lax.axis_index(axis)
    gathered = jax.tree.map(lambda a: lax.all_gather(a, axis), part)
    state = jax.tree.map(lambda a, e: jnp.zeros_like(a) + jnp.asarray(e, a.dtype), part, identity)

    def one(turn, state):
        return combine(
            state, jax.tree.map(lambda a: lax.dynamic_index_in_dim(a, turn, 0, False), gathered)
        )

    return lax.fori_loop(0, place, one, state)


def entering_2(value, axis, combine, identity):
    devices, mine = (lax.axis_size(axis), lax.axis_index(axis))
    everything = jax.tree.map(
        lambda part, kind: lax.all_gather(part.astype(kind), axis),
        value,
        jax.tree.map(lambda a: jnp.bfloat16 if a.dtype == jnp.float32 else a.dtype, value),
    )
    start = jax.tree.map(
        lambda part, zero: jnp.broadcast_to(jnp.asarray(zero, part.dtype), part.shape),
        value,
        identity,
    )

    def turn(k, before):
        at = devices - 1 - k
        reached = at > mine
        new = combine(
            before, jax.tree.map(lambda part, own: part[at].astype(own.dtype), everything, value)
        )
        return jax.tree.map(lambda a, b: jnp.where(reached, a, b), new, before)

    return lax.fori_loop(0, devices, turn, start)


def norm_rows(values, gain):
    center = values - jnp.mean(values, axis=-1, keepdims=True)
    spread = jnp.mean(center * center, axis=-1, keepdims=True)
    return center * lax.rsqrt(spread + 1e-05) * gain


def entry_weights(length, log_rate):
    position = jnp.arange(length).astype(jnp.float32)
    return jnp.exp((position[:, None] + 1.0) * log_rate[None, :])


def exit_weights(length, log_rate):
    position = jnp.arange(length).astype(jnp.float32)
    return jnp.exp((length - 1.0 - position)[:, None] * log_rate[None, :])


def decay_matrix(length, log_rate):
    position = jnp.arange(length).astype(jnp.float32)
    distance = position[:, None] - position[None, :]
    causal = distance >= 0.0
    return jnp.where(
        causal[None], jnp.exp(jnp.where(causal, distance, 0.0)[None] * log_rate[:, None, None]), 0.0
    )


def retain_out(query_block, key_block_rows, value_block_rows, retention_state, log_rate):
    length = query_block.shape[1]
    scores = (
        jnp.einsum("sthk,sqhk->shtq", query_block, key_block_rows, precision=highest_precision)
        * decay_matrix(length, log_rate)[None]
    )
    within = jnp.einsum("shtq,sqhv->sthv", scores, value_block_rows, precision=highest_precision)
    carried_state = jnp.einsum(
        "sthk,shkv->sthv",
        query_block * entry_weights(length, log_rate)[None, :, :, None],
        retention_state,
        precision=highest_precision,
    )
    return within + carried_state


def retain_low(query_low, key_low, query_wide, value_wide, retention_state, log_rate):
    length = query_low.shape[1]
    raw_scores = jnp.einsum(
        "sthk,sqhk->shtq", query_low, key_low, preferred_element_type=jnp.float32
    )
    scores = raw_scores * decay_matrix(length, log_rate)[None]
    within = jnp.einsum("shtq,sqhv->sthv", scores, value_wide, precision=highest_precision)
    carried_state = jnp.einsum(
        "sthk,shkv->sthv",
        query_wide * entry_weights(length, log_rate)[None, :, :, None],
        retention_state,
        precision=highest_precision,
    )
    return within + carried_state


def own_states(key_block_rows, value_block_rows, log_rate):
    length = key_block_rows.shape[1]
    return jnp.einsum(
        "sthk,sthv->shkv",
        key_block_rows * exit_weights(length, log_rate)[None, :, :, None],
        value_block_rows,
        precision=highest_precision,
    )


def combine_states(earlier, later):
    return (earlier[0] * later[0], later[0][None, :, None, None] * earlier[1] + later[1])


def gate_section(retained, swish_in, gain):
    return norm_rows(retained, gain) * jax.nn.silu(swish_in)


def mlp_section(act_gelu, act_up):
    return jax.nn.gelu(act_gelu) * act_up


def general(
    tokens,
    w_query,
    w_key,
    w_value,
    w_swish,
    w_output,
    w_gelu,
    w_up,
    w_down,
    gain_first,
    gain_second,
    gain_group,
    decay_rate,
    cotangent,
):
    f32 = jnp.float32
    bf16 = jnp.bfloat16
    gathered = (
        lax.all_gather(w_query, ("fsdp", "ctx"), axis=0, tiled=True),
        lax.all_gather(w_key, ("fsdp", "ctx"), axis=0, tiled=True),
        lax.all_gather(w_value, ("fsdp", "ctx"), axis=0, tiled=True),
        lax.all_gather(w_swish, ("fsdp", "ctx"), axis=0, tiled=True),
        lax.all_gather(w_output, ("fsdp", "ctx"), axis=0, tiled=True),
        lax.all_gather(w_gelu, ("fsdp", "ctx"), axis=0, tiled=True),
        lax.all_gather(w_up, ("fsdp", "ctx"), axis=0, tiled=True),
        lax.all_gather(w_down, ("fsdp", "ctx"), axis=0, tiled=True),
        lax.all_gather(gain_first, ("fsdp", "ctx"), axis=0, tiled=True),
        lax.all_gather(gain_second, ("fsdp", "ctx"), axis=0, tiled=True),
        lax.all_gather(gain_group, ("fsdp", "ctx"), axis=1, tiled=True),
    )
    (
        full_query,
        full_key,
        full_value,
        full_swish,
        full_output,
        full_gelu,
        full_up,
        full_down,
        full_first,
        full_second,
        full_group,
    ) = gathered
    log_rate = jnp.log(decay_rate)
    piece = tokens.shape[1]
    key_scale = full_query.shape[2] ** (-0.5)
    factor = jnp.exp(piece * log_rate)
    inputs = tokens.astype(f32)
    first_gain = full_first.astype(f32)
    second_gain = full_second.astype(f32)
    group_gain = full_group.astype(f32)
    first_low = norm_rows(inputs, first_gain).astype(bf16)
    query_block = jnp.einsum(
        "spd,dhk->sphk", first_low, full_query, preferred_element_type=f32
    ).astype(bf16)
    key_block_rows = (
        jnp.einsum("spd,dhk->sphk", first_low, full_key, preferred_element_type=f32) * key_scale
    ).astype(bf16)
    value_block_rows = jnp.einsum(
        "spd,dhv->sphv", first_low, full_value, preferred_element_type=f32
    ).astype(bf16)
    swish_in = jnp.einsum("spd,dhv->sphv", first_low, full_swish, preferred_element_type=f32)
    query_wide = query_block.astype(f32)
    key_wide = key_block_rows.astype(f32)
    value_wide = value_block_rows.astype(f32)
    local_state = own_states(key_wide, value_wide, log_rate)
    identity = (jnp.ones_like(factor), jnp.zeros_like(local_state))
    _, entering = prefix((factor, local_state), "ctx", combine_states, identity)
    retained = retain_low(query_block, key_block_rows, query_wide, value_wide, entering, log_rate)
    gated = gate_section(retained, swish_in, group_gain).astype(bf16)
    attn_terms = jnp.einsum("sphv,dhv->spd", gated, full_output, preferred_element_type=f32)
    hidden = inputs + lax.psum(attn_terms, "tp")
    second_low = norm_rows(hidden, second_gain).astype(bf16)
    act_gelu = jnp.einsum("spd,df->spf", second_low, full_gelu, preferred_element_type=f32)
    act_up = jnp.einsum("spd,df->spf", second_low, full_up, preferred_element_type=f32)
    mixed = mlp_section(act_gelu, act_up).astype(bf16)
    mlp_terms = jnp.einsum("spf,df->spd", mixed, full_down, preferred_element_type=f32)
    result = hidden + lax.psum(mlp_terms.astype(jnp.bfloat16), "tp").astype(jnp.float32)
    back_query, back_key, back_value, back_swish, back_output, back_gelu, back_up, back_down = gathered[:8]
    grad_mixed = jnp.einsum("spd,df->spf", cotangent, back_down, preferred_element_type=f32)
    grad_down = jnp.einsum("spd,spf->df", cotangent, mixed, preferred_element_type=f32).astype(bf16)
    _, pull_mlp = jax.vjp(mlp_section, act_gelu, act_up)
    grad_act_gelu, grad_act_up = pull_mlp(grad_mixed)
    gelu_low = grad_act_gelu.astype(bf16)
    up_low = grad_act_up.astype(bf16)
    grad_gelu = jnp.einsum("spd,spf->df", second_low, gelu_low, preferred_element_type=f32).astype(bf16)
    grad_up = jnp.einsum("spd,spf->df", second_low, up_low, preferred_element_type=f32).astype(bf16)
    second_terms = jnp.einsum(
        "spf,df->spd", gelu_low, back_gelu, preferred_element_type=f32
    ) + jnp.einsum("spf,df->spd", up_low, back_up, preferred_element_type=f32)
    grad_second_in = lax.psum(second_terms, "tp")
    _, pull_second = jax.vjp(norm_rows, hidden, second_gain)
    hidden_from_norm, grad_second = pull_second(grad_second_in)
    grad_hidden = cotangent.astype(f32) + hidden_from_norm
    hidden_low = grad_hidden.astype(bf16)
    grad_gated = jnp.einsum("spd,dhv->sphv", hidden_low, back_output, preferred_element_type=f32)
    grad_output = jnp.einsum("spd,sphv->dhv", hidden_low, gated, preferred_element_type=f32).astype(bf16)
    _, pull_gate = jax.vjp(gate_section, retained, swish_in, group_gain)
    grad_retained, grad_swish_in, grad_group = pull_gate(grad_gated)
    swish_low = grad_swish_in.astype(bf16)
    entry_grad = jnp.einsum(
        "sthk,sthv->shkv",
        query_wide * entry_weights(piece, log_rate)[None, :, :, None],
        grad_retained,
        precision=highest_precision,
    )
    _, later_grad = entering_2((factor, entry_grad), "ctx", combine_states, identity)
    _, pull_retain = jax.vjp(
        lambda rows_q, rows_k, rows_v: (
            retain_out(rows_q, rows_k, rows_v, entering, log_rate),
            own_states(rows_k, rows_v, log_rate),
        ),
        query_wide,
        key_wide,
        value_wide,
    )
    grad_query_act, grad_key_act, grad_value_act = pull_retain((grad_retained, later_grad))
    query_low = grad_query_act.astype(bf16)
    key_low = (grad_key_act.astype(bf16).astype(f32) * key_scale).astype(bf16)
    value_low = grad_value_act.astype(bf16)
    grad_query = jnp.einsum("spd,sphk->dhk", first_low, query_low, preferred_element_type=f32).astype(bf16)
    grad_key = jnp.einsum("spd,sphk->dhk", first_low, key_low, preferred_element_type=f32).astype(bf16)
    grad_value = jnp.einsum("spd,sphv->dhv", first_low, value_low, preferred_element_type=f32).astype(bf16)
    grad_swish = jnp.einsum("spd,sphv->dhv", first_low, swish_low, preferred_element_type=f32).astype(bf16)
    first_terms = jnp.einsum("sphk,dhk->spd", query_low, back_query, preferred_element_type=f32)
    first_terms = first_terms + jnp.einsum(
        "sphk,dhk->spd", key_low, back_key, preferred_element_type=f32
    )
    first_terms = first_terms + jnp.einsum(
        "sphv,dhv->spd", value_low, back_value, preferred_element_type=f32
    )
    first_terms = first_terms + jnp.einsum(
        "sphv,dhv->spd", swish_low, back_swish, preferred_element_type=f32
    )
    grad_first_in = lax.psum(first_terms.astype(jnp.bfloat16), "tp").astype(jnp.float32)
    _, pull_first = jax.vjp(norm_rows, inputs, first_gain)
    tokens_from_norm, grad_first = pull_first(grad_first_in)
    grad_tokens = grad_hidden + tokens_from_norm
    owned = tuple(
        lax.psum_scatter(g, ("fsdp", "ctx"), scatter_dimension=0, tiled=True).astype(f32)
        for g in (grad_query, grad_key, grad_value, grad_swish, grad_output, grad_gelu, grad_up, grad_down, grad_first, grad_second)
    ) + (lax.psum_scatter(grad_group, ("fsdp", "ctx"), scatter_dimension=1, tiled=True),)
    return (
        result,
        grad_tokens,
        owned[0],
        owned[1],
        owned[2],
        owned[3],
        owned[4],
        owned[5],
        owned[6],
        owned[7],
        owned[8],
        owned[9],
        owned[10],
    )


def solution(mesh):
    wide, flat = P(("fsdp", "ctx"), "tp", None), P(("fsdp", "ctx"), "tp")
    tok, row, group = P("fsdp", "ctx", None), P(("fsdp", "ctx")), P("tp", ("fsdp", "ctx"))
    in_specs = (tok,) + (wide,) * 5 + (flat,) * 3 + (row, row, group, P("tp"), tok)
    out_specs = (tok, tok) + (wide,) * 5 + (flat,) * 3 + (row, row, group)
    sizes = (mesh.shape["fsdp"], mesh.shape["ctx"], mesh.shape["tp"])
    local = fused if sizes == (2, 2 * ZN, 2) else general
    return jax.shard_map(local, mesh=mesh, in_specs=in_specs, out_specs=out_specs, check_vma=False)
```

```python
import types

import jax
import jax.numpy as jnp
from jax import lax
from jax.experimental import pallas as pl
from jax.experimental.pallas import tpu as pltpu
from jax.sharding import PartitionSpec as P

MESH = pl.DeviceIdType.MESH
BF = jnp.bfloat16
F32 = jnp.float32

ZN = 4
BLK = 128
HALF = 64
TOK = ZN * BLK
D = 2048
CH = 512
NCH = 7
NC = 4
AC = 4
AR = HALF // AC
SETS = 4
VW = 640
VLIM = 62 * 2**20


def nt(a, b):
    return lax.dot_general(a, b, (((1,), (1,)), ((), ())), preferred_element_type=F32)


def nn(a, b):
    return lax.dot_general(a, b, (((1,), (0,)), ((), ())), preferred_element_type=F32)


def normed(v):
    center = v - jnp.mean(v, axis=-1, keepdims=True)
    rstd = lax.rsqrt(jnp.mean(center * center, axis=-1, keepdims=True) + 1e-05)
    return center * rstd, rstd


def norm_back(n, rstd, g):
    return rstd * (
        g - jnp.mean(g, axis=-1, keepdims=True) - n * jnp.mean(g * n, axis=-1, keepdims=True)
    )


def remote(src, dst, ss, rs, dev):
    return pltpu.make_async_remote_copy(src, dst, ss, rs, device_id=dev, device_id_type=MESH)


SCRATCH = dict(
    gall=((16, 8, 128), F32),
    W=((NCH, 16, BLK, CH), BF),
    first=((ZN, BLK, D), BF),
    cot=((ZN, BLK, D), BF),
    second=((ZN, BLK, D), BF),
    hlow=((ZN, BLK, D), BF),
    XT=((16, BLK, TOK), BF),
    qkv=((2, TOK, 1024), BF),
    swish=((TOK, CH), F32),
    ret=((TOK, CH), F32),
    dr=((TOK, CH), BF),
    YB=((NCH, TOK, CH), BF),
    dkv_s=((TOK, 768), BF),
    dkv_r=((TOK, 768), BF),
    tmp=((3, TOK, 256), F32),
    ysend=((2, NC, ZN, HALF, CH), BF),
    yrecv=((2, NC, ZN, HALF, CH), BF),
    zsend=((2, NC, ZN, HALF, CH), BF),
    zrecv=((2, NC, ZN + 1, HALF, CH), BF),
    hidden=((HALF, D), F32),
    ghid=((HALF, D), F32),
    rsum=((HALF, D), F32),
    ostage=((2, HALF, D), BF),
    gcs=((2, ZN, BLK, CH), BF),
    gcr=((SETS, 2, ZN, BLK, CH), BF),
    gxs=((SETS, ZN, BLK, CH), BF),
    gxr=((SETS, ZN, BLK, CH), BF),
    gzs=((SETS, ZN, BLK, CH), BF),
    vec=((8, VW), F32),
    vrc=((8, VW), F32),
    vrx=((8, VW), F32),
    vry=((8, VW), F32),
    vz=((ZN, 8, VW), F32),
)
SEMS = dict(
    g_s=(3, 8), g_r=(3, 8),
    wz_s=(NCH, 3), wz_r=(NCH, 3), wx_s=(NCH, 4), wx_r=(NCH, 4), wc_s=(NCH, 8), wc_r=(NCH, 8), wl=(NCH,),
    az_s=(4, AC, 2, ZN), az_r=(4, AC, ZN), ay_s=(4, AC, ZN), ay_r=(4, AC, ZN),
    ry_s=(4, NC), ry_r=(4, NC), rz_s=(4, NC, ZN), rz_r=(4, NC, ZN + 1),
    kv_s=(2,), kv_r=(2,),
    gc_s=(NCH, 2), gc_r=(NCH, 2), gx_s=(NCH,), gx_r=(NCH,), gz_s=(NCH, 3), gz_r=(NCH, 3), gl=(NCH,),
    v_s=(6,), v_r=(6,), o_s=(2,), o_r=(2,), ol=(4,),
    credit=None,
)
NAMES = list(SCRATCH) + list(SEMS)


def kernel(tok, gp, lr, cot_in, pk, wg, wu, wd, res_o, gtok_o, gwa_o, gwf_o, vec_o, *scratch):
    s = types.SimpleNamespace(**dict(zip(NAMES, scratch)))
    W, YB, XT = s.W, s.YB, s.XT
    x, k, y = lax.axis_index("fsdp"), lax.axis_index("ctx"), lax.axis_index("tp")
    z, c = k // 2, k % 2
    zup = [lax.rem(z + i, ZN) for i in range(ZN)]
    zdn = [lax.rem(z + ZN - i, ZN) for i in range(ZN)]
    zdev = [(x, zup[i] * 2 + c, y) for i in range(ZN)]
    updev, dndev = zdev[1], zdev[ZN - 1]
    xdev, ydev, cdev = (1 - x, k, y), (x, k, 1 - y), (x, z * 2 + 1 - c, y)
    peers = range(1, ZN)

    def place(xx, zz, cc):
        return xx * 8 + zz * 2 + cc

    me = place(x, z, c)
    log_rate = lr[z]

    def loop(n, f):
        def step(i, carry):
            f(i)
            return carry

        lax.fori_loop(0, n, step, 0)

    barrier = pltpu.get_barrier_semaphore()
    for dev in zdev[1:] + [xdev, ydev, cdev]:
        pl.semaphore_signal(barrier, inc=1, device_id=dev, device_id_type=MESH)
    pl.semaphore_wait(barrier, 6)

    def w_src(n, zz):
        if n < 4:
            return pk.at[zz, :, pl.ds(n * CH, CH)]
        return (wg, wu, wd)[n - 4].at[:, pl.ds(pl.multiple_of(zz * CH, CH), CH)]

    def w_local(n, zz):
        return pltpu.make_async_copy(w_src(n, zz), W.at[n, me], s.wl.at[n])

    def w_piece(n, i):
        remote(w_src(n, zup[i]), W.at[n, me], s.wz_s.at[n, i - 1], s.wz_r.at[n, i - 1], zdev[i]).start()

    def w_send(n):
        for i in peers:
            w_piece(n, i)

    def w_z(n, i):
        blk = W.at[n, place(x, zdn[i], c)]
        return remote(blk, blk, s.wz_s.at[n, i - 1], s.wz_r.at[n, i - 1], zdev[i])

    def w_x(n, j, xx):
        blk = W.at[n, place(xx, zdn[j], c)]
        return remote(blk, blk, s.wx_s.at[n, j], s.wx_r.at[n, j], xdev)

    def w_c(n, j, cc):
        xx = x if j < 4 else 1 - x
        blk = W.at[n, place(xx, zdn[j % 4], cc)]
        return remote(blk, blk, s.wc_s.at[n, j], s.wc_r.at[n, j], cdev)

    def w_own(n):
        pltpu.make_async_copy(W.at[n, me], W.at[n, me], s.wl.at[n]).wait()
        w_x(n, 0, x).start()
        w_c(n, 0, c).start()

    def pump_z(n):
        for i in peers:
            w_z(n, i).wait_recv()
            w_x(n, i, x).start()
            w_c(n, i, c).start()

    def pump_x(n):
        for j in range(ZN):
            w_x(n, j, 1 - x).wait_recv()
            w_c(n, ZN + j, c).start()

    def w_fin(n):
        for j in range(8):
            w_c(n, j, 1 - c).wait_recv()

    def w_done(n):
        for i in peers:
            w_z(n, i).wait_send()
        for j in range(ZN):
            w_x(n, j, x).wait_send()
        for j in range(8):
            w_c(n, j, c).wait_send()

    def a_rows(yy, ch):
        return pl.ds(pl.multiple_of(yy * HALF + ch * AR, AR), AR)

    def a_z(buf, ia, ch, zz, way):
        blk = buf.at[zz, a_rows(y, ch)]
        return remote(blk, blk, s.az_s.at[ia, ch, way, zz], s.az_r.at[ia, ch, zz], (updev, dndev)[way])

    def a_y(buf, ia, ch, zz, yy):
        blk = buf.at[zz, a_rows(yy, ch)]
        return remote(blk, blk, s.ay_s.at[ia, ch, zz], s.ay_r.at[ia, ch, zz], ydev)

    def ag_sends(buf, ia, ch, zz, do):
        pl.when((zz <= z) & (z < ZN - 1))(lambda: do(a_z(buf, ia, ch, zz, 0)))
        pl.when((zz >= z) & (z > 0))(lambda: do(a_z(buf, ia, ch, zz, 1)))

    def ag_send(buf, ia, own):
        def f(ch):
            ag_sends(buf, ia, ch, z, lambda copy: copy.start())
            if own:
                a_y(buf, ia, ch, z, y).start()

        loop(AC, f)

    def ag_forward(buf, ia, d):
        def f(ch):
            def pass_on(zz):
                a_z(buf, ia, ch, zz, 0).wait_recv()
                ag_sends(buf, ia, ch, zz, lambda copy: copy.start())
                a_y(buf, ia, ch, zz, y).start()

            pl.when(z >= d)(lambda: pass_on(z - d))
            pl.when(z + d < ZN)(lambda: pass_on(z + d))

        loop(AC, f)

    def ag_wait(buf, ia, own):
        def f(ch):
            for i in range(0 if own else 1, ZN):
                a_y(buf, ia, ch, zdn[i], 1 - y).wait_recv()

        loop(AC, f)

    def ag_done(buf, ia, own):
        def f(ch):
            for i in range(ZN):
                ag_sends(buf, ia, ch, zdn[i], lambda copy: copy.wait_send())
                if own or i > 0:
                    a_y(buf, ia, ch, zdn[i], y).wait_send()

        loop(AC, f)

    def product(chunks, j, yy):
        total = None
        for n in chunks:
            rows = [YB[n, pl.ds(pl.multiple_of(zz * BLK + yy * HALF, HALF), HALF), :] for zz in range(ZN)]
            lhs = jnp.concatenate(rows, axis=0)
            rhs = W[n, pl.ds(j * 4, 4)].reshape(CH, CH)
            part = nt(lhs, rhs)
            total = part if total is None else total + part
        return total.reshape(ZN, HALF, CH)

    def r_y(ir, b, j):
        return remote(s.ysend.at[b, j], s.yrecv.at[b, j], s.ry_s.at[ir, j], s.ry_r.at[ir, j], ydev)

    def r_z(ir, b, j, d, way):
        slot = d if way == 0 else jnp.where(d == z - 1, ZN, d)
        return remote(
            s.zsend.at[b, j, d], s.zrecv.at[b, j, slot], s.rz_s.at[ir, j, d], s.rz_r.at[ir, j, slot], (updev, dndev)[way]
        )

    def r_arrived(ir, b, j, slot):
        there = s.zrecv.at[b, j, slot]
        remote(there, there, s.rz_s.at[ir, j, 0], s.rz_r.at[ir, j, slot], updev).wait_recv()

    def rs_a(ir, b, chunks):
        def f(j):
            s.ysend[b, j] = product(chunks, j, 1 - y).astype(BF)
            r_y(ir, b, j).start()

        loop(NC, f)

    def r_pass(ir, b, j, level):
        def go(dests, way):
            for d in dests:
                if level > 0:
                    r_arrived(ir, b, j, d)
                    s.zsend[b, j, d] = (s.zsend[b, j, d].astype(F32) + s.zrecv[b, j, d].astype(F32)).astype(BF)
                r_z(ir, b, j, d, way).start()

        pl.when(z == level)(lambda: go(range(ZN - 1, level, -1), 0))
        pl.when(z == ZN - 1 - level)(lambda: go(range(ZN - 1 - level), 1))

    def rs_y(ir, b, chunks, j):
        own = product(chunks, j, y)
        r_y(ir, b, j).wait_recv()
        s.zsend[b, j] = (own + s.yrecv[b, j].astype(F32)).astype(BF)
        r_pass(ir, b, j, 0)

    def rs_c(ir, b):
        def f(j):
            cols = pl.ds(pl.multiple_of(j * CH, CH), CH)
            s.rsum[:, cols] = s.zsend[b, j, z].astype(F32)

            def add(slot):
                r_arrived(ir, b, j, slot)
                s.rsum[:, cols] = s.rsum[:, cols] + s.zrecv[b, j, slot].astype(F32)

            pl.when(z > 0)(lambda: add(z))
            pl.when(z < ZN - 1)(lambda: add(ZN))

        loop(NC, f)

    def rs_done(ir, b):
        def f(j):
            r_y(ir, b, j).wait_send()
            for i in peers:
                r_z(ir, b, j, zdn[i], 0).wait_send()

        loop(NC, f)

    def transpose(buf):
        def f(q):
            cols = pl.ds(pl.multiple_of(q * BLK, BLK), BLK)
            XT[q] = buf[:, :, cols].reshape(TOK, BLK).T

        loop(16, f)

    def grad_rows(n, xx, cc):
        lhs = jnp.concatenate([XT[place(xx, zz, cc)] for zz in range(ZN)], axis=0)
        return nn(lhs, YB[n]).reshape(ZN, BLK, CH)

    def g_c(n, xx):
        return remote(s.gcs.at[xx], s.gcr.at[n % SETS, xx], s.gc_s.at[n, xx], s.gc_r.at[n, xx], cdev)

    def g_x(n):
        return remote(s.gxs.at[n % SETS], s.gxr.at[n % SETS], s.gx_s.at[n], s.gx_r.at[n], xdev)

    def g_dst(n):
        if n < 4:
            return gwa_o.at[n, z]
        return gwf_o.at[n - 4, :, pl.ds(pl.multiple_of(z * CH, CH), CH)]

    def g_z(n, i):
        return remote(s.gzs.at[n % SETS, zup[i]], g_dst(n), s.gz_s.at[n, i - 1], s.gz_r.at[n, i - 1], zdev[i])

    def g_local(n):
        return pltpu.make_async_copy(s.gzs.at[n % SETS, z], g_dst(n), s.gl.at[n])

    def grad_a(n, first_use):
        b = n % SETS

        def f(t):
            xx = (1 - x) * (1 - t) + x * t
            s.gcs[xx] = grad_rows(n, xx, 1 - c).astype(BF)
            g_c(n, xx).start()

        loop(2, f)
        own = grad_rows(n, 1 - x, c)
        g_c(n, 1 - x).wait_recv()
        if not first_use:
            pl.semaphore_wait(s.credit.at[b], 1)
        s.gxs[b] = (own + s.gcr[b, 1 - x].astype(F32)).astype(BF)
        g_x(n).start()
        own = grad_rows(n, x, c)
        g_c(n, x).wait_recv()
        s.gzs[b] = (own + s.gcr[b, x].astype(F32)).astype(BF)
        for xx in range(2):
            g_c(n, xx).wait_send()

    def grad_b(n, more):
        b = n % SETS
        g_x(n).wait_recv()
        s.gzs[b] = (s.gzs[b].astype(F32) + s.gxr[b].astype(F32)).astype(BF)
        for i in peers:
            g_z(n, i).start()
        g_local(n).start()
        g_x(n).wait_send()
        if more:
            pl.semaphore_signal(s.credit.at[b], inc=1, device_id=xdev, device_id_type=MESH)

    def grad_sent(n):
        for i in peers:
            g_z(n, i).wait_send()
        g_local(n).wait()

    def grad_done(n):
        for i in peers:
            g_z(n, i).wait_recv()

    def gain_row(r):
        return jnp.concatenate([s.gall[q, r : r + 1, :] for q in range(16)], axis=1)

    def group_gain():
        pick = lax.broadcasted_iota(jnp.int32, (8, 128), 0) == 2 + z
        parts = []
        for r in range(4):
            total = s.gall[4 * r]
            for q in range(4 * r + 1, 4 * r + 4):
                total = total + s.gall[q]
            parts.append(jnp.sum(jnp.where(pick, total, 0.0), axis=0, keepdims=True))
        return jnp.concatenate(parts, axis=1)

    def packed(row):
        return jnp.concatenate([row[:, 256 * q : 256 * q + 256] for q in range(D // 256)], axis=0)

    def position(shape, dim, both, start):
        r = lax.broadcasted_iota(jnp.int32, shape, dim) + start
        if both:
            core, r = r // TOK, lax.rem(r, TOK)
        else:
            core = c
        return r + (r // BLK) * BLK + core * BLK

    def decay(later, earlier):
        gap = later - earlier
        keep = gap >= 0
        return jnp.where(keep, jnp.exp(jnp.where(keep, gap, 0).astype(F32) * log_rate), 0.0)

    own_rows = pl.ds(pl.multiple_of(y * HALF, HALF), HALF)

    gall = s.gall
    gall[me] = gp[...]

    def g_gain(j, i, dev, q):
        return remote(gall.at[q], gall.at[q], s.g_s.at[j, i], s.g_r.at[j, i], dev)

    for i in peers:
        g_gain(0, i, zdev[i], me).start()
    w_send(0)
    for n in range(NCH):
        w_local(n, z).start()
    cot_local = pltpu.make_async_copy(cot_in, s.cot.at[z], s.ol.at[0])
    cot_local.start()
    for i in peers:
        g_gain(0, i, zdev[i], place(x, zdn[i], c)).wait_recv()
    for i in range(ZN):
        g_gain(1, i, xdev, place(x, zdn[i], c)).start()
    for i in range(ZN):
        g_gain(2, i, cdev, place(x, zdn[i], c)).start()
    for i in range(ZN):
        g_gain(1, i, xdev, place(1 - x, zdn[i], c)).wait_recv()
        g_gain(2, ZN + i, cdev, place(1 - x, zdn[i], c)).start()
    for i in range(8):
        xx = x if i < ZN else 1 - x
        g_gain(2, i, cdev, place(xx, zdn[i % ZN], 1 - c)).wait_recv()
    for i in peers:
        g_gain(0, i, zdev[i], me).wait_send()
    for i in range(ZN):
        g_gain(1, i, xdev, place(x, zdn[i], c)).wait_send()
    for i in range(8):
        xx = x if i < ZN else 1 - x
        g_gain(2, i, cdev, place(xx, zdn[i % ZN], c)).wait_send()
    vec = s.vec
    vec[...] = jnp.zeros((8, VW), F32)
    gain_g = group_gain()
    tmp, qkv, swish = s.tmp, s.qkv, s.swish

    def columns(n, t):
        return W[n, :, :, pl.ds(pl.multiple_of(t * 256, 256), 256)].reshape(D, 256)

    def all_keys():
        return qkv[:, :, 256:512].reshape(2 * TOK, 256)

    def all_values():
        return qkv[:, :, 512:1024].reshape(2 * TOK, CH)

    def out_copies(j, dst):
        there = dst.at[own_rows]
        return (
            remote(s.ostage.at[j], there, s.o_s.at[j], s.o_r.at[j], ydev),
            pltpu.make_async_copy(s.ostage.at[j], there, s.ol.at[1 + j]),
        )

    tokens = tok[...].astype(F32)
    n_first, _ = normed(tokens)
    s.first[z] = (n_first * gain_row(0)).astype(BF)
    ag_send(s.first, 0, False)
    ag_forward(s.first, 0, 1)
    w_own(3)
    w_own(1)
    w_own(0)
    pump_z(0)
    w_send(3)
    ag_forward(s.first, 0, 2)
    w_send(1)
    w_own(2)
    pump_x(0)
    pump_z(3)
    w_send(2)
    ag_forward(s.first, 0, 3)
    ag_wait(s.first, 0, False)
    pump_z(1)
    cot_local.wait()
    ag_send(s.cot, 1, False)
    w_fin(0)

    def project_qk(t):
        scale = jnp.where(t == 1, 0.0625, 1.0)
        out = nn(s.first[...].reshape(TOK, D), columns(0, t)) * scale
        qkv[c, :, pl.ds(pl.multiple_of(t * 256, 256), 256)] = out.astype(BF)

    loop(2, project_qk)
    pump_x(1)
    w_send(5)
    pump_z(2)
    w_fin(1)

    def project_v(t):
        out = nn(s.first[...].reshape(TOK, D), columns(1, t))
        qkv[c, :, pl.ds(pl.multiple_of(512 + t * 256, 256), 256)] = out.astype(BF)

    loop(2, project_v)

    def kv_copy(cc):
        blk = qkv.at[cc, :, pl.ds(256, 768)]
        return remote(blk, blk, s.kv_s.at[0], s.kv_r.at[0], cdev)

    kv_copy(c).start()
    w_own(4)
    pump_x(3)
    kv_copy(1 - c).wait_recv()

    def retain(h):
        rows = pl.ds(pl.multiple_of(h * 256, 256), 256)
        later = position((256, 2 * TOK), 0, False, h * 256)
        earlier = position((256, 2 * TOK), 1, True, 0)
        scores = nt(qkv[c, rows, 0:256], all_keys()) * decay(later, earlier)
        s.ret[rows, :] = nn(scores.astype(BF), all_values())

    loop(2, retain)
    pump_x(2)
    w_send(6)
    ag_forward(s.cot, 1, 1)
    w_fin(2)

    def project_s(t):
        out = nn(s.first[...].reshape(TOK, D), columns(2, t))
        swish[:, pl.ds(pl.multiple_of(t * 256, 256), 256)] = out

    loop(2, project_s)
    def gate(h):
        rows = pl.ds(pl.multiple_of(h * BLK, BLK), BLK)
        n, _ = normed(s.ret[rows, :])
        w = swish[rows, :]
        YB[3, rows, :] = (n * gain_g * (w / (1.0 + jnp.exp(-w)))).astype(BF)

    loop(ZN, gate)
    w_own(5)
    w_own(6)
    w_fin(3)
    rs_a(0, 0, (3,))
    w_send(4)
    rs_y(0, 0, (3,), 0)
    rs_y(0, 0, (3,), 1)
    ag_forward(s.cot, 1, 2)
    pump_z(6)
    r_pass(0, 0, 0, 1)
    r_pass(0, 0, 1, 1)
    rs_y(0, 0, (3,), 2)
    r_pass(0, 0, 2, 1)
    r_pass(0, 0, 0, 2)
    pump_z(4)
    rs_y(0, 0, (3,), 3)
    ag_forward(s.cot, 1, 3)
    r_pass(0, 0, 3, 1)
    r_pass(0, 0, 1, 2)
    pump_z(5)
    r_pass(0, 0, 2, 2)
    r_pass(0, 0, 3, 2)
    rs_c(0, 0)
    hidden = tok[own_rows, :].astype(F32) + s.rsum[...]
    s.hidden[...] = hidden
    n_second, _ = normed(hidden)
    s.second[z, own_rows, :] = (n_second * gain_row(1)).astype(BF)
    ag_send(s.second, 2, True)
    ag_forward(s.second, 2, 1)
    pump_x(6)
    ag_wait(s.cot, 1, False)
    ag_forward(s.second, 2, 2)
    ag_forward(s.second, 2, 3)
    pump_x(5)
    pump_x(4)
    ag_wait(s.second, 2, True)
    for n in range(4, NCH):
        w_fin(n)

    def feed(t):
        cols = pl.ds(pl.multiple_of(t * 256, 256), 256)
        sec = s.second[...].reshape(TOK, D)
        tmp[0] = nn(sec, columns(4, t))
        tmp[1] = nn(sec, columns(5, t))
        tmp[2] = nn(s.cot[...].reshape(TOK, D), columns(6, t))

        def act(h):
            rows = pl.ds(pl.multiple_of(h * HALF, HALF), HALF)
            a, u, gm = tmp[0, rows, :], tmp[1, rows, :], tmp[2, rows, :]
            root = 0.7978845608028654
            th = jnp.tanh(root * (a + 0.044715 * (a * a * a)))
            half = 0.5 * (1.0 + th)
            gelu = a * half
            slope = half + 0.5 * a * (1.0 - th * th) * (root * (1.0 + 0.134145 * (a * a)))
            YB[6, rows, cols] = (gelu * u).astype(BF)
            YB[4, rows, cols] = (gm * u * slope).astype(BF)
            YB[5, rows, cols] = (gm * gelu).astype(BF)

        loop(TOK // HALF, act)

    loop(2, feed)
    rs_done(0, 0)
    rs_a(1, 0, (4, 5))
    rs_y(1, 0, (4, 5), 0)
    r_pass(1, 0, 0, 1)
    transpose(s.second)
    rs_a(2, 1, (6,))
    rs_y(1, 0, (4, 5), 1)
    grad_a(5, True)
    r_pass(1, 0, 1, 1)
    rs_y(1, 0, (4, 5), 2)
    r_pass(1, 0, 2, 1)
    rs_y(1, 0, (4, 5), 3)
    r_pass(1, 0, 0, 2)
    r_pass(1, 0, 1, 2)
    r_pass(1, 0, 3, 1)
    r_pass(1, 0, 2, 2)
    rs_y(2, 1, (6,), 0)
    r_pass(1, 0, 3, 2)
    rs_c(1, 0)
    n_second, rstd = normed(s.hidden[...])
    g_in = s.rsum[...]
    vec[:, 256:512] = packed(jnp.sum(g_in * n_second, axis=0, keepdims=True))
    ghid = s.cot[z, own_rows, :].astype(F32) + norm_back(n_second, rstd, g_in * gain_row(1))
    s.ghid[...] = ghid
    s.hlow[z, own_rows, :] = ghid.astype(BF)
    ag_send(s.hlow, 3, True)
    r_pass(2, 1, 0, 1)
    grad_a(4, True)
    transpose(s.cot)
    rs_y(2, 1, (6,), 1)
    grad_a(6, True)
    ag_forward(s.hlow, 3, 1)
    r_pass(2, 1, 1, 1)
    ag_forward(s.hlow, 3, 2)
    grad_b(4, True)
    ag_forward(s.hlow, 3, 3)
    rs_y(2, 1, (6,), 2)
    grad_b(5, True)
    rs_y(2, 1, (6,), 3)
    grad_b(6, True)
    ag_wait(s.hlow, 3, True)
    transpose(s.hlow)
    grad_a(3, True)
    def back_gated(t):
        tmp[t] = nn(s.hlow[...].reshape(TOK, D), columns(3, t))

    loop(2, back_gated)

    def back_gate(h, total):
        rows = pl.ds(pl.multiple_of(h * BLK, BLK), BLK)
        n, rstd = normed(s.ret[rows, :])
        w, g = swish[rows, :], jnp.concatenate([tmp[0, rows, :], tmp[1, rows, :]], axis=1)
        sig = 1.0 / (1.0 + jnp.exp(-w))
        silu = w * sig
        YB[2, rows, :] = (g * (n * gain_g) * (sig * (1.0 + w * (1.0 - sig)))).astype(BF)
        gs = g * silu
        s.dr[rows, :] = norm_back(n, rstd, gs * gain_g).astype(BF)
        return total + jnp.sum(gs * n, axis=0, keepdims=True)

    group = lax.fori_loop(0, ZN, back_gate, jnp.zeros((1, CH), F32))
    vec[0:4, 512:VW] = jnp.concatenate([group[:, 128 * q : 128 * q + 128] for q in range(4)], axis=0)

    r_pass(2, 1, 0, 2)
    def back_keys(core, h):
        rows = pl.ds(pl.multiple_of(h * 256, 256), 256)
        keys, values = qkv[core, rows, 256:512], qkv[core, rows, 512:1024]
        query = qkv[c, :, 0:256]
        r = lax.broadcasted_iota(jnp.int32, (256, TOK), 0) + h * 256
        earlier = r + (r // BLK) * BLK + core * BLK
        table = decay(position((256, TOK), 1, False, 0), earlier)
        weights = (nt(keys, query) * table).astype(BF)
        slopes = (nt(values, s.dr[...]) * table).astype(BF)
        return rows, nn(slopes, query), nn(weights, s.dr[...])

    def back_other(h):
        rows, dk, dv = back_keys(1 - c, h)
        s.dkv_s[rows, 0:256] = dk.astype(BF)
        s.dkv_s[rows, 256:768] = dv.astype(BF)

    def back_own(h):
        rows, dk, dv = back_keys(c, h)
        tmp[0, rows, :] = dk
        tmp[1, rows, :] = dv[:, 0:256]
        tmp[2, rows, :] = dv[:, 256:512]

    loop(2, back_other)
    dkv_copy = remote(s.dkv_s, s.dkv_r, s.kv_s.at[1], s.kv_r.at[1], cdev)
    dkv_copy.start()
    loop(2, back_own)

    def back_query(h):
        rows = pl.ds(pl.multiple_of(h * 256, 256), 256)
        later = position((256, 2 * TOK), 0, False, h * 256)
        earlier = position((256, 2 * TOK), 1, True, 0)
        slopes = nt(s.dr[rows, :], all_values()) * decay(later, earlier)
        YB[0, rows, 0:256] = nn(slopes.astype(BF), all_keys()).astype(BF)

    loop(2, back_query)
    dkv_copy.wait_recv()

    def back_sum(h):
        rows = pl.ds(pl.multiple_of(h * BLK, BLK), BLK)
        other = s.dkv_r[rows, :].astype(F32)
        YB[0, rows, 256:512] = ((tmp[0, rows, :] + other[:, 0:256]) * 0.0625).astype(BF)
        YB[1, rows, 0:256] = (tmp[1, rows, :] + other[:, 256:512]).astype(BF)
        YB[1, rows, 256:512] = (tmp[2, rows, :] + other[:, 512:768]).astype(BF)

    loop(ZN, back_sum)

    grad_b(3, False)
    transpose(s.first)
    r_pass(2, 1, 2, 1)
    rs_done(1, 0)
    rs_a(3, 0, (0, 1, 2))
    r_pass(2, 1, 3, 1)
    grad_sent(5)
    grad_a(1, False)
    rs_y(3, 0, (0, 1, 2), 0)
    grad_sent(4)
    grad_a(0, False)
    rs_y(3, 0, (0, 1, 2), 1)
    grad_sent(6)
    grad_a(2, False)
    r_pass(3, 0, 0, 1)
    r_pass(3, 0, 1, 1)
    r_pass(2, 1, 1, 2)
    r_pass(3, 0, 0, 2)
    r_pass(2, 1, 2, 2)
    rs_y(3, 0, (0, 1, 2), 2)
    r_pass(3, 0, 2, 1)
    rs_y(3, 0, (0, 1, 2), 3)
    r_pass(3, 0, 1, 2)
    r_pass(2, 1, 3, 2)
    rs_c(2, 1)
    s.ostage[1] = (s.hidden[...] + s.rsum[...]).astype(BF)
    for copy in out_copies(1, res_o):
        copy.start()
    grad_b(1, False)
    r_pass(3, 0, 3, 1)
    r_pass(3, 0, 2, 2)
    r_pass(3, 0, 3, 2)
    rs_c(3, 0)
    n_first, rstd = normed(tok[own_rows, :].astype(F32))
    g_in = s.rsum[...]
    vec[:, 0:256] = packed(jnp.sum(g_in * n_first, axis=0, keepdims=True))
    g_tok = s.ghid[...] + norm_back(n_first, rstd, g_in * gain_row(0))
    s.ostage[0] = g_tok.astype(BF)

    for copy in out_copies(0, gtok_o):
        copy.start()
    grad_b(0, False)
    def v_copy(j, dst, dev):
        return remote(vec, dst, s.v_s.at[j], s.v_r.at[j], dev)

    v_copy(0, s.vrc, cdev).start()
    v_copy(0, s.vrc, cdev).wait()
    vec[...] = vec[...] + s.vrc[...]
    v_copy(1, s.vrx, xdev).start()
    v_copy(1, s.vrx, xdev).wait()
    vec[...] = vec[...] + s.vrx[...]
    v_copy(2, s.vry, ydev).start()
    grad_b(2, False)
    v_copy(2, s.vry, ydev).wait()
    vec[:, 0:512] = vec[:, 0:512] + s.vry[:, 0:512]
    vz = s.vz
    vz[z] = vec[...]
    for i in peers:
        v_copy(2 + i, vz.at[z], zdev[i]).start()
    for i in peers:
        there = vz.at[zdn[i]]
        remote(there, there, s.v_s.at[2 + i], s.v_r.at[2 + i], zdev[i]).wait_recv()
    for i in peers:
        v_copy(2 + i, vz.at[z], zdev[i]).wait_send()
    vec_o[:, 0:512] = ((vz[0, :, 0:512] + vz[1, :, 0:512]) + vz[2, :, 0:512]) + vz[3, :, 0:512]
    for zz in range(ZN):
        vec_o[:, 512 + 128 * zz : 640 + 128 * zz] = vz[zz, :, 512:VW]
    for j, dst in enumerate((gtok_o, res_o)):
        there = dst.at[pl.ds(pl.multiple_of((1 - y) * HALF, HALF), HALF)]
        a, b = out_copies(j, dst)
        a.wait_send()
        b.wait()
        remote(s.ostage.at[j], there, s.o_s.at[j], s.o_r.at[j], ydev).wait_recv()
    for n in range(4):
        grad_sent(n)
    for n in range(NCH):
        grad_done(n)
    loop(NCH, w_done)
    kv_copy(c).wait_send()
    dkv_copy.wait_send()
    for ia, (buf, own) in enumerate(((s.first, False), (s.cot, False), (s.second, True), (s.hlow, True))):
        ag_done(buf, ia, own)
    rs_done(2, 1)
    rs_done(3, 0)


def finish_kernel(gwa, gwf, res, gtok, vec, o_res, o_tok, o_q, o_k, o_v, o_s, o_o, o_g, o_u, o_d, o_first, o_second, o_group):
    o_res[0] = res[...].astype(F32)
    o_tok[0] = gtok[...].astype(F32)
    for n, out in enumerate((o_g, o_u, o_d)):
        out[...] = gwf[n].astype(F32)
    both = jnp.swapaxes(gwa[0].astype(F32), 0, 1)
    o_q[...] = both[:, :, 0:256]
    o_k[...] = both[:, :, 256:512]
    for n, out in enumerate((o_v, o_s, o_o)):
        out[...] = jnp.swapaxes(gwa[n + 1].astype(F32), 0, 1)
    me = lax.axis_index("fsdp") * 8 + lax.axis_index("ctx")
    quarter = lax.rem(me, 4)

    def row(r, start, stop):
        block = vec[:, start:stop]
        return jnp.sum(jnp.where(lax.broadcasted_iota(jnp.int32, block.shape, 0) == r, block, 0.0), axis=0, keepdims=True)

    for out, start in ((o_first, 0), (o_second, 256)):
        pair = row(me // 2, start, start + 256)
        out[...] = jnp.where(lax.rem(me, 2) == 0, pair[:, 0:128], pair[:, 128:256])
    for zz in range(ZN):
        line = row(me // 4, 512 + 128 * zz, 640 + 128 * zz)
        total = jnp.zeros((1, 32), F32)
        for q in range(4):
            total = total + jnp.where(quarter == q, line[:, 32 * q : 32 * q + 32], 0.0)
        o_group[zz : zz + 1, :] = total


def finish(res, gtok, gwa, gwf, vec):
    steps = 2
    rows = BLK // steps
    flat = pl.BlockSpec((rows, D), lambda i: (i, 0))
    deep = pl.BlockSpec((1, rows, D), lambda i: (0, i, 0))
    narrow = pl.BlockSpec((rows, ZN, 256), lambda i: (i, 0, 0))
    wide = pl.BlockSpec((rows, ZN, CH), lambda i: (i, 0, 0))

    def whole(*shape):
        return pl.BlockSpec(shape, lambda i: (0,) * len(shape))

    def f32(*shape):
        return jax.ShapeDtypeStruct(shape, F32)

    outs = pl.pallas_call(
        finish_kernel,
        grid=(steps,),
        in_specs=[
            pl.BlockSpec((4, ZN, rows, CH), lambda i: (0, 0, i, 0)),
            pl.BlockSpec((3, rows, D), lambda i: (0, i, 0)),
            flat,
            flat,
            whole(8, 1024),
        ],
        out_specs=[deep, deep, narrow, narrow, wide, wide, wide, flat, flat, flat, whole(1, BLK), whole(1, BLK), whole(ZN, 32)],
        out_shape=[f32(1, BLK, D)] * 2
        + [f32(BLK, ZN, 256)] * 2
        + [f32(BLK, ZN, CH)] * 3
        + [f32(BLK, D)] * 3
        + [f32(1, BLK)] * 2
        + [f32(ZN, 32)],
        compiler_params=pltpu.CompilerParams(vmem_limit_bytes=VLIM),
    )(gwa, gwf, res, gtok, vec)
    return tuple(outs[:10]) + (outs[10].reshape(BLK), outs[11].reshape(BLK), outs[12])


def start_kernel(q, k, v, sw, o, g_first, g_second, g_group, rate, pk, gp, lr):
    for ref, at in ((q, 0), (k, 256), (v, 512), (sw, 1024), (o, 1536)):
        pk[:, :, at : at + ref.shape[2]] = jnp.swapaxes(ref[...], 0, 1)
    me = lax.axis_index("fsdp") * 8 + lax.axis_index("ctx")
    quarter = lax.rem(me, 4)
    gp[...] = jnp.zeros((8, BLK), F32)
    gp[0:1, :] = g_first[...].astype(F32)
    gp[1:2, :] = g_second[...].astype(F32)
    lane = lax.broadcasted_iota(jnp.int32, (ZN, BLK), 1) // 32
    wide = jnp.concatenate([g_group[...].astype(F32)] * 4, axis=1)
    gp[2:6, :] = jnp.where(lane == quarter, wide, 0.0)
    lr[...] = jnp.log(rate[...])


def begin(w_query, w_key, w_value, w_swish, w_output, gain_first, gain_second, gain_group, decay_rate):
    steps = 2
    rows = BLK // steps
    narrow = pl.BlockSpec((rows, ZN, 256), lambda i: (i, 0, 0))
    wide = pl.BlockSpec((rows, ZN, CH), lambda i: (i, 0, 0))

    def whole(*shape):
        return pl.BlockSpec(shape, lambda i: (0,) * len(shape))

    pk, gp, lr = pl.pallas_call(
        start_kernel,
        grid=(steps,),
        in_specs=[narrow, narrow, wide, wide, wide, whole(1, BLK), whole(1, BLK), whole(ZN, 32), whole(1, ZN)],
        out_specs=[pl.BlockSpec((ZN, rows, 4 * CH), lambda i: (0, i, 0)), whole(8, BLK), whole(1, ZN)],
        out_shape=[
            jax.ShapeDtypeStruct((ZN, BLK, 4 * CH), BF),
            jax.ShapeDtypeStruct((8, BLK), F32),
            jax.ShapeDtypeStruct((1, ZN), F32),
        ],
        compiler_params=pltpu.CompilerParams(vmem_limit_bytes=VLIM),
    )(w_query, w_key, w_value, w_swish, w_output, gain_first[None], gain_second[None], gain_group, decay_rate[None])
    return pk, gp, lr[0]


def fused(
    tokens, w_query, w_key, w_value, w_swish, w_output, w_gelu, w_up, w_down, gain_first, gain_second, gain_group, decay_rate, cotangent
):
    pk, gp, lr = begin(w_query, w_key, w_value, w_swish, w_output, gain_first, gain_second, gain_group, decay_rate)
    shapes = [
        jax.ShapeDtypeStruct((BLK, D), BF),
        jax.ShapeDtypeStruct((BLK, D), BF),
        jax.ShapeDtypeStruct((4, ZN, BLK, CH), BF),
        jax.ShapeDtypeStruct((3, BLK, D), BF),
        jax.ShapeDtypeStruct((8, 1024), F32),
    ]
    hbm = pl.BlockSpec(memory_space=pl.ANY)
    vmem = pl.BlockSpec(memory_space=pltpu.VMEM)
    smem = pl.BlockSpec(memory_space=pltpu.SMEM)
    scratch = [pltpu.VMEM(*v) for v in SCRATCH.values()]
    for shape in SEMS.values():
        scratch.append(pltpu.SemaphoreType.REGULAR((3,)) if shape is None else pltpu.SemaphoreType.DMA(shape))
    result, g_tok, gwa, gwf, vec = pl.pallas_call(
        kernel,
        out_shape=shapes,
        in_specs=[vmem, vmem, smem, hbm, hbm, hbm, hbm, hbm],
        out_specs=[hbm, hbm, hbm, hbm, vmem],
        scratch_shapes=scratch,
        compiler_params=pltpu.CompilerParams(collective_id=0, has_side_effects=True, vmem_limit_bytes=VLIM),
    )(tokens[0], gp, lr, cotangent[0], pk, w_gelu, w_up, w_down)
    return finish(result, g_tok, gwa, gwf, vec)


highest_precision = lax.Precision.HIGHEST


def prefix(part, axis, combine, identity):
    place = lax.axis_index(axis)
    gathered = jax.tree.map(lambda a: lax.all_gather(a, axis), part)
    state = jax.tree.map(lambda a, e: jnp.zeros_like(a) + jnp.asarray(e, a.dtype), part, identity)

    def one(turn, state):
        return combine(
            state, jax.tree.map(lambda a: lax.dynamic_index_in_dim(a, turn, 0, False), gathered)
        )

    return lax.fori_loop(0, place, one, state)


def entering_2(value, axis, combine, identity):
    devices, mine = (lax.axis_size(axis), lax.axis_index(axis))
    everything = jax.tree.map(
        lambda part, kind: lax.all_gather(part.astype(kind), axis),
        value,
        jax.tree.map(lambda a: jnp.bfloat16 if a.dtype == jnp.float32 else a.dtype, value),
    )
    start = jax.tree.map(
        lambda part, zero: jnp.broadcast_to(jnp.asarray(zero, part.dtype), part.shape),
        value,
        identity,
    )

    def turn(k, before):
        at = devices - 1 - k
        reached = at > mine
        new = combine(
            before, jax.tree.map(lambda part, own: part[at].astype(own.dtype), everything, value)
        )
        return jax.tree.map(lambda a, b: jnp.where(reached, a, b), new, before)

    return lax.fori_loop(0, devices, turn, start)


def norm_rows(values, gain):
    center = values - jnp.mean(values, axis=-1, keepdims=True)
    spread = jnp.mean(center * center, axis=-1, keepdims=True)
    return center * lax.rsqrt(spread + 1e-05) * gain


def entry_weights(length, log_rate):
    position = jnp.arange(length).astype(jnp.float32)
    return jnp.exp((position[:, None] + 1.0) * log_rate[None, :])


def exit_weights(length, log_rate):
    position = jnp.arange(length).astype(jnp.float32)
    return jnp.exp((length - 1.0 - position)[:, None] * log_rate[None, :])


def decay_matrix(length, log_rate):
    position = jnp.arange(length).astype(jnp.float32)
    distance = position[:, None] - position[None, :]
    causal = distance >= 0.0
    return jnp.where(
        causal[None], jnp.exp(jnp.where(causal, distance, 0.0)[None] * log_rate[:, None, None]), 0.0
    )


def retain_out(query_block, key_block_rows, value_block_rows, retention_state, log_rate):
    length = query_block.shape[1]
    scores = (
        jnp.einsum("sthk,sqhk->shtq", query_block, key_block_rows, precision=highest_precision)
        * decay_matrix(length, log_rate)[None]
    )
    within = jnp.einsum("shtq,sqhv->sthv", scores, value_block_rows, precision=highest_precision)
    carried_state = jnp.einsum(
        "sthk,shkv->sthv",
        query_block * entry_weights(length, log_rate)[None, :, :, None],
        retention_state,
        precision=highest_precision,
    )
    return within + carried_state


def retain_low(query_low, key_low, query_wide, value_wide, retention_state, log_rate):
    length = query_low.shape[1]
    raw_scores = jnp.einsum(
        "sthk,sqhk->shtq", query_low, key_low, preferred_element_type=jnp.float32
    )
    scores = raw_scores * decay_matrix(length, log_rate)[None]
    within = jnp.einsum("shtq,sqhv->sthv", scores, value_wide, precision=highest_precision)
    carried_state = jnp.einsum(
        "sthk,shkv->sthv",
        query_wide * entry_weights(length, log_rate)[None, :, :, None],
        retention_state,
        precision=highest_precision,
    )
    return within + carried_state


def own_states(key_block_rows, value_block_rows, log_rate):
    length = key_block_rows.shape[1]
    return jnp.einsum(
        "sthk,sthv->shkv",
        key_block_rows * exit_weights(length, log_rate)[None, :, :, None],
        value_block_rows,
        precision=highest_precision,
    )


def combine_states(earlier, later):
    return (earlier[0] * later[0], later[0][None, :, None, None] * earlier[1] + later[1])


def gate_section(retained, swish_in, gain):
    return norm_rows(retained, gain) * jax.nn.silu(swish_in)


def mlp_section(act_gelu, act_up):
    return jax.nn.gelu(act_gelu) * act_up


def general(
    tokens,
    w_query,
    w_key,
    w_value,
    w_swish,
    w_output,
    w_gelu,
    w_up,
    w_down,
    gain_first,
    gain_second,
    gain_group,
    decay_rate,
    cotangent,
):
    f32 = jnp.float32
    bf16 = jnp.bfloat16
    gathered = (
        lax.all_gather(w_query, ("fsdp", "ctx"), axis=0, tiled=True),
        lax.all_gather(w_key, ("fsdp", "ctx"), axis=0, tiled=True),
        lax.all_gather(w_value, ("fsdp", "ctx"), axis=0, tiled=True),
        lax.all_gather(w_swish, ("fsdp", "ctx"), axis=0, tiled=True),
        lax.all_gather(w_output, ("fsdp", "ctx"), axis=0, tiled=True),
        lax.all_gather(w_gelu, ("fsdp", "ctx"), axis=0, tiled=True),
        lax.all_gather(w_up, ("fsdp", "ctx"), axis=0, tiled=True),
        lax.all_gather(w_down, ("fsdp", "ctx"), axis=0, tiled=True),
        lax.all_gather(gain_first, ("fsdp", "ctx"), axis=0, tiled=True),
        lax.all_gather(gain_second, ("fsdp", "ctx"), axis=0, tiled=True),
        lax.all_gather(gain_group, ("fsdp", "ctx"), axis=1, tiled=True),
    )
    (
        full_query,
        full_key,
        full_value,
        full_swish,
        full_output,
        full_gelu,
        full_up,
        full_down,
        full_first,
        full_second,
        full_group,
    ) = gathered
    log_rate = jnp.log(decay_rate)
    piece = tokens.shape[1]
    key_scale = full_query.shape[2] ** (-0.5)
    factor = jnp.exp(piece * log_rate)
    inputs = tokens.astype(f32)
    first_gain = full_first.astype(f32)
    second_gain = full_second.astype(f32)
    group_gain = full_group.astype(f32)
    first_low = norm_rows(inputs, first_gain).astype(bf16)
    query_block = jnp.einsum(
        "spd,dhk->sphk", first_low, full_query, preferred_element_type=f32
    ).astype(bf16)
    key_block_rows = (
        jnp.einsum("spd,dhk->sphk", first_low, full_key, preferred_element_type=f32) * key_scale
    ).astype(bf16)
    value_block_rows = jnp.einsum(
        "spd,dhv->sphv", first_low, full_value, preferred_element_type=f32
    ).astype(bf16)
    swish_in = jnp.einsum("spd,dhv->sphv", first_low, full_swish, preferred_element_type=f32)
    query_wide = query_block.astype(f32)
    key_wide = key_block_rows.astype(f32)
    value_wide = value_block_rows.astype(f32)
    local_state = own_states(key_wide, value_wide, log_rate)
    identity = (jnp.ones_like(factor), jnp.zeros_like(local_state))
    _, entering = prefix((factor, local_state), "ctx", combine_states, identity)
    retained = retain_low(query_block, key_block_rows, query_wide, value_wide, entering, log_rate)
    gated = gate_section(retained, swish_in, group_gain).astype(bf16)
    attn_terms = jnp.einsum("sphv,dhv->spd", gated, full_output, preferred_element_type=f32)
    hidden = inputs + lax.psum(attn_terms, "tp")
    second_low = norm_rows(hidden, second_gain).astype(bf16)
    act_gelu = jnp.einsum("spd,df->spf", second_low, full_gelu, preferred_element_type=f32)
    act_up = jnp.einsum("spd,df->spf", second_low, full_up, preferred_element_type=f32)
    mixed = mlp_section(act_gelu, act_up).astype(bf16)
    mlp_terms = jnp.einsum("spf,df->spd", mixed, full_down, preferred_element_type=f32)
    result = hidden + lax.psum(mlp_terms.astype(jnp.bfloat16), "tp").astype(jnp.float32)
    back_query, back_key, back_value, back_swish, back_output, back_gelu, back_up, back_down = gathered[:8]
    grad_mixed = jnp.einsum("spd,df->spf", cotangent, back_down, preferred_element_type=f32)
    grad_down = jnp.einsum("spd,spf->df", cotangent, mixed, preferred_element_type=f32).astype(bf16)
    _, pull_mlp = jax.vjp(mlp_section, act_gelu, act_up)
    grad_act_gelu, grad_act_up = pull_mlp(grad_mixed)
    gelu_low = grad_act_gelu.astype(bf16)
    up_low = grad_act_up.astype(bf16)
    grad_gelu = jnp.einsum("spd,spf->df", second_low, gelu_low, preferred_element_type=f32).astype(bf16)
    grad_up = jnp.einsum("spd,spf->df", second_low, up_low, preferred_element_type=f32).astype(bf16)
    second_terms = jnp.einsum(
        "spf,df->spd", gelu_low, back_gelu, preferred_element_type=f32
    ) + jnp.einsum("spf,df->spd", up_low, back_up, preferred_element_type=f32)
    grad_second_in = lax.psum(second_terms, "tp")
    _, pull_second = jax.vjp(norm_rows, hidden, second_gain)
    hidden_from_norm, grad_second = pull_second(grad_second_in)
    grad_hidden = cotangent.astype(f32) + hidden_from_norm
    hidden_low = grad_hidden.astype(bf16)
    grad_gated = jnp.einsum("spd,dhv->sphv", hidden_low, back_output, preferred_element_type=f32)
    grad_output = jnp.einsum("spd,sphv->dhv", hidden_low, gated, preferred_element_type=f32).astype(bf16)
    _, pull_gate = jax.vjp(gate_section, retained, swish_in, group_gain)
    grad_retained, grad_swish_in, grad_group = pull_gate(grad_gated)
    swish_low = grad_swish_in.astype(bf16)
    entry_grad = jnp.einsum(
        "sthk,sthv->shkv",
        query_wide * entry_weights(piece, log_rate)[None, :, :, None],
        grad_retained,
        precision=highest_precision,
    )
    _, later_grad = entering_2((factor, entry_grad), "ctx", combine_states, identity)
    _, pull_retain = jax.vjp(
        lambda rows_q, rows_k, rows_v: (
            retain_out(rows_q, rows_k, rows_v, entering, log_rate),
            own_states(rows_k, rows_v, log_rate),
        ),
        query_wide,
        key_wide,
        value_wide,
    )
    grad_query_act, grad_key_act, grad_value_act = pull_retain((grad_retained, later_grad))
    query_low = grad_query_act.astype(bf16)
    key_low = (grad_key_act.astype(bf16).astype(f32) * key_scale).astype(bf16)
    value_low = grad_value_act.astype(bf16)
    grad_query = jnp.einsum("spd,sphk->dhk", first_low, query_low, preferred_element_type=f32).astype(bf16)
    grad_key = jnp.einsum("spd,sphk->dhk", first_low, key_low, preferred_element_type=f32).astype(bf16)
    grad_value = jnp.einsum("spd,sphv->dhv", first_low, value_low, preferred_element_type=f32).astype(bf16)
    grad_swish = jnp.einsum("spd,sphv->dhv", first_low, swish_low, preferred_element_type=f32).astype(bf16)
    first_terms = jnp.einsum("sphk,dhk->spd", query_low, back_query, preferred_element_type=f32)
    first_terms = first_terms + jnp.einsum(
        "sphk,dhk->spd", key_low, back_key, preferred_element_type=f32
    )
    first_terms = first_terms + jnp.einsum(
        "sphv,dhv->spd", value_low, back_value, preferred_element_type=f32
    )
    first_terms = first_terms + jnp.einsum(
        "sphv,dhv->spd", swish_low, back_swish, preferred_element_type=f32
    )
    grad_first_in = lax.psum(first_terms.astype(jnp.bfloat16), "tp").astype(jnp.float32)
    _, pull_first = jax.vjp(norm_rows, inputs, first_gain)
    tokens_from_norm, grad_first = pull_first(grad_first_in)
    grad_tokens = grad_hidden + tokens_from_norm
    owned = tuple(
        lax.psum_scatter(g, ("fsdp", "ctx"), scatter_dimension=0, tiled=True).astype(f32)
        for g in (grad_query, grad_key, grad_value, grad_swish, grad_output, grad_gelu, grad_up, grad_down, grad_first, grad_second)
    ) + (lax.psum_scatter(grad_group, ("fsdp", "ctx"), scatter_dimension=1, tiled=True),)
    return (
        result,
        grad_tokens,
        owned[0],
        owned[1],
        owned[2],
        owned[3],
        owned[4],
        owned[5],
        owned[6],
        owned[7],
        owned[8],
        owned[9],
        owned[10],
    )


def solution(mesh):
    wide, flat = P(("fsdp", "ctx"), "tp", None), P(("fsdp", "ctx"), "tp")
    tok, row, group = P("fsdp", "ctx", None), P(("fsdp", "ctx")), P("tp", ("fsdp", "ctx"))
    in_specs = (tok,) + (wide,) * 5 + (flat,) * 3 + (row, row, group, P("tp"), tok)
    out_specs = (tok, tok) + (wide,) * 5 + (flat,) * 3 + (row, row, group)
    sizes = (mesh.shape["fsdp"], mesh.shape["ctx"], mesh.shape["tp"])
    local = fused if sizes == (2, 2 * ZN, 2) else general
    return jax.shard_map(local, mesh=mesh, in_specs=in_specs, out_specs=out_specs, check_vma=False)
```

```python
import types

import jax
import jax.numpy as jnp
from jax import lax
from jax.experimental import pallas as pl
from jax.experimental.pallas import tpu as pltpu
from jax.sharding import PartitionSpec as P

MESH = pl.DeviceIdType.MESH
BF = jnp.bfloat16
F32 = jnp.float32

ZN = 4
BLK = 128
ROOT = 0.7978845608028654
HR = 32
HALF = 64
TOK = ZN * BLK
D = 2048
CH = 512
NCH = 7
NC = 2
RC = D // NC
RB = 16 // NC
AC = 4
AR = HALF // AC
SETS = 4
VW = 640
VLIM = 62 * 2**20


def nt(a, b):
    return lax.dot_general(a, b, (((1,), (1,)), ((), ())), preferred_element_type=F32)


def nn(a, b):
    return lax.dot_general(a, b, (((1,), (0,)), ((), ())), preferred_element_type=F32)


def normed(v):
    center = v - jnp.mean(v, axis=-1, keepdims=True)
    rstd = lax.rsqrt(jnp.mean(center * center, axis=-1, keepdims=True) + 1e-05)
    return center * rstd, rstd


def norm_back(n, rstd, g):
    return rstd * (
        g - jnp.mean(g, axis=-1, keepdims=True) - n * jnp.mean(g * n, axis=-1, keepdims=True)
    )


def remote(src, dst, ss, rs, dev):
    return pltpu.make_async_remote_copy(src, dst, ss, rs, device_id=dev, device_id_type=MESH)


SCRATCH = dict(
    gall=((16, 8, 128), F32),
    W=((NCH, 16, BLK, CH), BF),
    first=((ZN, BLK, D), BF),
    cot=((ZN, BLK, D), BF),
    second=((ZN, BLK, D), BF),
    hlow=((ZN, BLK, D), BF),
    XT=((16, BLK, TOK), BF),
    qkv=((2, TOK, 1024), BF),
    swish=((TOK, CH), F32),
    ret=((TOK, CH), F32),
    dr=((TOK, CH), BF),
    YB=((NCH, TOK, CH), BF),
    dkv_s=((TOK, 768), BF),
    dkv_r=((TOK, 768), BF),
    tmp=((5, TOK, 256), F32),
    ysend=((2, 2, NC, ZN, HR, RC), BF),
    yrecv=((2, 2, NC, ZN, HR, RC), BF),
    zsend=((2, 2, NC, ZN, HR, RC), BF),
    zrecv=((2, 2, NC, ZN + 1, HR, RC), BF),
    hidden=((HALF, D), F32),
    ghid=((HALF, D), F32),
    rsum=((HALF, D), F32),
    ostage=((2, HALF, D), BF),
    gcs=((2, ZN, BLK, CH), BF),
    gcr=((SETS, 2, ZN, BLK, CH), BF),
    gxs=((SETS, ZN, BLK, CH), BF),
    gxr=((SETS, ZN, BLK, CH), BF),
    gzs=((SETS, ZN, BLK, CH), BF),
    vec=((8, VW), F32),
    vrc=((8, VW), F32),
    vrx=((8, VW), F32),
    vry=((8, VW), F32),
    vz=((ZN, 8, VW), F32),
)
SEMS = dict(
    g_s=(3, 8), g_r=(3, 8),
    wz_s=(NCH, 3), wz_r=(NCH, 3), wx_s=(NCH, 4), wx_r=(NCH, 4), wc_s=(NCH, 8), wc_r=(NCH, 8), wl=(NCH,),
    az_s=(4, AC, 2, ZN), az_r=(4, AC, ZN), ay_s=(4, AC, ZN), ay_r=(4, AC, ZN),
    ry_s=(4, 2, NC), ry_r=(4, 2, NC), rz_s=(4, 2, NC, ZN), rz_r=(4, 2, NC, ZN + 1),
    kv_s=(2,), kv_r=(2,),
    gc_s=(NCH, 2), gc_r=(NCH, 2), gx_s=(NCH,), gx_r=(NCH,), gz_s=(NCH, 3), gz_r=(NCH, 3), gl=(NCH,),
    v_s=(6,), v_r=(6,), o_s=(2, 2), o_r=(2, 2), ol=(1,), oo=(2, 2),
    credit=None,
)
NAMES = list(SCRATCH) + list(SEMS)


def kernel(tok, gp, lr, cot_in, pk, wg, wu, wd, res_o, gtok_o, gwa_o, gwf_o, vec_o, *scratch):
    s = types.SimpleNamespace(**dict(zip(NAMES, scratch)))
    W, YB, XT = s.W, s.YB, s.XT
    x, k, y = lax.axis_index("fsdp"), lax.axis_index("ctx"), lax.axis_index("tp")
    z, c = k // 2, k % 2
    zup = [lax.rem(z + i, ZN) for i in range(ZN)]
    zdn = [lax.rem(z + ZN - i, ZN) for i in range(ZN)]
    zdev = [(x, zup[i] * 2 + c, y) for i in range(ZN)]
    updev, dndev = zdev[1], zdev[ZN - 1]
    xdev, ydev, cdev = (1 - x, k, y), (x, k, 1 - y), (x, z * 2 + 1 - c, y)
    peers = range(1, ZN)

    def place(xx, zz, cc):
        return xx * 8 + zz * 2 + cc

    me = place(x, z, c)
    log_rate = lr[z]

    def loop(n, f):
        def step(i, carry):
            f(i)
            return carry

        lax.fori_loop(0, n, step, 0)

    barrier = pltpu.get_barrier_semaphore()
    for dev in zdev[1:] + [xdev, ydev, cdev]:
        pl.semaphore_signal(barrier, inc=1, device_id=dev, device_id_type=MESH)
    pl.semaphore_wait(barrier, 6)

    def w_src(n, zz):
        if n < 4:
            return pk.at[zz, :, pl.ds(n * CH, CH)]
        return (wg, wu, wd)[n - 4].at[:, pl.ds(pl.multiple_of(zz * CH, CH), CH)]

    def w_local(n, zz):
        return pltpu.make_async_copy(w_src(n, zz), W.at[n, me], s.wl.at[n])

    def w_piece(n, i):
        remote(w_src(n, zup[i]), W.at[n, me], s.wz_s.at[n, i - 1], s.wz_r.at[n, i - 1], zdev[i]).start()

    def w_send(n):
        for i in peers:
            w_piece(n, i)

    def w_z(n, i):
        blk = W.at[n, place(x, zdn[i], c)]
        return remote(blk, blk, s.wz_s.at[n, i - 1], s.wz_r.at[n, i - 1], zdev[i])

    def w_x(n, j, xx):
        blk = W.at[n, place(xx, zdn[j], c)]
        return remote(blk, blk, s.wx_s.at[n, j], s.wx_r.at[n, j], xdev)

    def w_c(n, j, cc):
        xx = x if j < 4 else 1 - x
        blk = W.at[n, place(xx, zdn[j % 4], cc)]
        return remote(blk, blk, s.wc_s.at[n, j], s.wc_r.at[n, j], cdev)

    def w_own(n):
        pltpu.make_async_copy(W.at[n, me], W.at[n, me], s.wl.at[n]).wait()
        w_x(n, 0, x).start()
        w_c(n, 0, c).start()

    def pump_z(n, i):
        w_z(n, i).wait_recv()
        w_x(n, i, x).start()
        w_c(n, i, c).start()

    def pump_x(n, j):
        w_x(n, j, 1 - x).wait_recv()
        w_c(n, ZN + j, c).start()

    def w_fin(n):
        for j in range(8):
            w_c(n, j, 1 - c).wait_recv()

    def w_done(n):
        for i in peers:
            w_z(n, i).wait_send()
        for j in range(ZN):
            w_x(n, j, x).wait_send()
        for j in range(8):
            w_c(n, j, c).wait_send()

    def a_rows(yy, ch):
        return pl.ds(pl.multiple_of(yy * HALF + ch * AR, AR), AR)

    def a_z(buf, ia, ch, zz, way):
        blk = buf.at[zz, a_rows(y, ch)]
        return remote(blk, blk, s.az_s.at[ia, ch, way, zz], s.az_r.at[ia, ch, zz], (updev, dndev)[way])

    def a_y(buf, ia, ch, zz, yy):
        blk = buf.at[zz, a_rows(yy, ch)]
        return remote(blk, blk, s.ay_s.at[ia, ch, zz], s.ay_r.at[ia, ch, zz], ydev)

    def ag_sends(buf, ia, ch, zz, do):
        pl.when((zz <= z) & (z < ZN - 1))(lambda: do(a_z(buf, ia, ch, zz, 0)))
        pl.when((zz >= z) & (z > 0))(lambda: do(a_z(buf, ia, ch, zz, 1)))

    def ag_send(buf, ia, own, part):
        def f(at):
            ch = at + part * (AC // 2)
            ag_sends(buf, ia, ch, z, lambda copy: copy.start())
            if own:
                a_y(buf, ia, ch, z, y).start()

        loop(AC // 2, f)

    def ag_forward(buf, ia, d, part):
        def f(at):
            ch = at + part * (AC // 2)

            def pass_on(zz):
                a_z(buf, ia, ch, zz, 0).wait_recv()
                ag_sends(buf, ia, ch, zz, lambda copy: copy.start())
                a_y(buf, ia, ch, zz, y).start()

            pl.when(z >= d)(lambda: pass_on(z - d))
            pl.when(z + d < ZN)(lambda: pass_on(z + d))

        loop(AC // 2, f)

    def ag_wait(buf, ia, own, part):
        def f(at):
            ch = at + part * (AC // 2)
            for i in range(0 if own else 1, ZN):
                a_y(buf, ia, ch, zdn[i], 1 - y).wait_recv()

        loop(AC // 2, f)

    def ag_done(buf, ia, own):
        def f(ch):
            for i in range(ZN):
                ag_sends(buf, ia, ch, zdn[i], lambda copy: copy.wait_send())
                if own or i > 0:
                    a_y(buf, ia, ch, zdn[i], y).wait_send()

        loop(AC, f)

    def group_rows(buf, g):
        return jnp.concatenate([buf[zz, yy * HALF + g * HR : yy * HALF + g * HR + HR, :] for zz in range(ZN) for yy in range(2)], axis=0)

    def product(chunks, j, yy, g):
        total = None
        for n in chunks:
            rows = []
            for zz in range(ZN):
                at = (g * ZN + zz) * HALF + yy * HR if n > 3 else zz * BLK + yy * HALF + g * HR
                rows.append(YB[n, pl.ds(pl.multiple_of(at, HR), HR), :])
            lhs = jnp.concatenate(rows, axis=0)
            rhs = W[n, pl.ds(j * RB, RB)].reshape(RC, CH)
            part = nt(lhs, rhs)
            total = part if total is None else total + part
        return total.reshape(ZN, HR, RC)

    def r_y(ir, b, g, j):
        return remote(s.ysend.at[b, g, j], s.yrecv.at[b, g, j], s.ry_s.at[ir, g, j], s.ry_r.at[ir, g, j], ydev)

    def r_z(ir, b, g, j, d, way):
        slot = d if way == 0 else jnp.where(d == z - 1, ZN, d)
        return remote(
            s.zsend.at[b, g, j, d],
            s.zrecv.at[b, g, j, slot],
            s.rz_s.at[ir, g, j, d],
            s.rz_r.at[ir, g, j, slot],
            (updev, dndev)[way],
        )

    def r_arrived(ir, b, g, j, slot):
        there = s.zrecv.at[b, g, j, slot]
        remote(there, there, s.rz_s.at[ir, g, j, 0], s.rz_r.at[ir, g, j, slot], updev).wait_recv()

    def rs_a(ir, b, chunks, g):
        def f(j):
            s.ysend[b, g, j] = product(chunks, j, 1 - y, g).astype(BF)
            r_y(ir, b, g, j).start()

        loop(NC, f)

    def r_pass(ir, b, g, j, level):
        def go(dests, way):
            for d in dests:
                if level > 0:
                    r_arrived(ir, b, g, j, d)
                    s.zsend[b, g, j, d] = (s.zsend[b, g, j, d].astype(F32) + s.zrecv[b, g, j, d].astype(F32)).astype(BF)
                r_z(ir, b, g, j, d, way).start()

        pl.when(z == level)(lambda: go(range(ZN - 1, level, -1), 0))
        pl.when(z == ZN - 1 - level)(lambda: go(range(ZN - 1 - level), 1))

    def rs_y(ir, b, chunks, g, j):
        own = product(chunks, j, y, g)
        r_y(ir, b, g, j).wait_recv()
        s.zsend[b, g, j] = (own + s.yrecv[b, g, j].astype(F32)).astype(BF)
        r_pass(ir, b, g, j, 0)

    def rs_c(ir, b, g):
        mine = pl.ds(g * HR, HR)

        def f(j):
            cols = pl.ds(pl.multiple_of(j * RC, RC), RC)
            s.rsum[mine, cols] = s.zsend[b, g, j, z].astype(F32)

            def add(slot):
                r_arrived(ir, b, g, j, slot)
                s.rsum[mine, cols] = s.rsum[mine, cols] + s.zrecv[b, g, j, slot].astype(F32)

            pl.when(z > 0)(lambda: add(z))
            pl.when(z < ZN - 1)(lambda: add(ZN))

        loop(NC, f)
        return s.rsum[mine, :]

    def rs_done(ir, b, g):
        def f(j):
            r_y(ir, b, g, j).wait_send()
            for i in peers:
                r_z(ir, b, g, j, zdn[i], 0).wait_send()

        loop(NC, f)

    def transpose(buf, grouped):
        def f(q):
            cols = pl.ds(pl.multiple_of(q * BLK, BLK), BLK)
            if grouped:
                parts = []
                for g in range(2):
                    for zz in range(ZN):
                        for yy in range(2):
                            parts.append(buf[zz, yy * HALF + g * HR : yy * HALF + g * HR + HR, cols])
                XT[q] = jnp.concatenate(parts, axis=0).T
            else:
                XT[q] = buf[:, :, cols].reshape(TOK, BLK).T

        loop(16, f)

    def grad_rows(n, xx, cc):
        lhs = jnp.concatenate([XT[place(xx, zz, cc)] for zz in range(ZN)], axis=0)
        return nn(lhs, YB[n]).reshape(ZN, BLK, CH)

    def g_c(n, xx):
        return remote(s.gcs.at[xx], s.gcr.at[n % SETS, xx], s.gc_s.at[n, xx], s.gc_r.at[n, xx], cdev)

    def g_x(n):
        return remote(s.gxs.at[n % SETS], s.gxr.at[n % SETS], s.gx_s.at[n], s.gx_r.at[n], xdev)

    def g_dst(n):
        if n < 4:
            return gwa_o.at[n, z]
        return gwf_o.at[n - 4, :, pl.ds(pl.multiple_of(z * CH, CH), CH)]

    def g_z(n, i):
        return remote(s.gzs.at[n % SETS, zup[i]], g_dst(n), s.gz_s.at[n, i - 1], s.gz_r.at[n, i - 1], zdev[i])

    def g_local(n):
        return pltpu.make_async_copy(s.gzs.at[n % SETS, z], g_dst(n), s.gl.at[n])

    def grad_a(n, first_use):
        b = n % SETS

        def f(t):
            xx = (1 - x) * (1 - t) + x * t
            s.gcs[xx] = grad_rows(n, xx, 1 - c).astype(BF)
            g_c(n, xx).start()

        loop(2, f)
        own = grad_rows(n, 1 - x, c)
        g_c(n, 1 - x).wait_recv()
        if not first_use:
            pl.semaphore_wait(s.credit.at[b], 1)
        s.gxs[b] = (own + s.gcr[b, 1 - x].astype(F32)).astype(BF)
        g_x(n).start()
        own = grad_rows(n, x, c)
        g_c(n, x).wait_recv()
        s.gzs[b] = (own + s.gcr[b, x].astype(F32)).astype(BF)
        for xx in range(2):
            g_c(n, xx).wait_send()

    def grad_b(n, more):
        b = n % SETS
        g_x(n).wait_recv()
        s.gzs[b] = (s.gzs[b].astype(F32) + s.gxr[b].astype(F32)).astype(BF)
        for i in peers:
            g_z(n, i).start()
        g_local(n).start()
        g_x(n).wait_send()
        if more:
            pl.semaphore_signal(s.credit.at[b], inc=1, device_id=xdev, device_id_type=MESH)

    def grad_sent(n):
        for i in peers:
            g_z(n, i).wait_send()
        g_local(n).wait()

    def grad_done(n):
        for i in peers:
            g_z(n, i).wait_recv()

    def gain_row(r):
        return jnp.concatenate([s.gall[q, r : r + 1, :] for q in range(16)], axis=1)

    def group_gain():
        pick = lax.broadcasted_iota(jnp.int32, (8, 128), 0) == 2 + z
        parts = []
        for r in range(4):
            total = s.gall[4 * r]
            for q in range(4 * r + 1, 4 * r + 4):
                total = total + s.gall[q]
            parts.append(jnp.sum(jnp.where(pick, total, 0.0), axis=0, keepdims=True))
        return jnp.concatenate(parts, axis=1)

    def packed(row):
        return jnp.concatenate([row[:, 256 * q : 256 * q + 256] for q in range(D // 256)], axis=0)

    def position(shape, dim, both, start):
        r = lax.broadcasted_iota(jnp.int32, shape, dim) + start
        if both:
            core, r = r // TOK, lax.rem(r, TOK)
        else:
            core = c
        return r + (r // BLK) * BLK + core * BLK

    def decay(later, earlier):
        gap = later - earlier
        keep = gap >= 0
        return jnp.where(keep, jnp.exp(jnp.where(keep, gap, 0).astype(F32) * log_rate), 0.0)

    def own_rows(g):
        return pl.ds(pl.multiple_of(y * HALF + g * HR, HR), HR)

    gall = s.gall
    gall[me] = gp[...]

    def g_gain(j, i, dev, q):
        return remote(gall.at[q], gall.at[q], s.g_s.at[j, i], s.g_r.at[j, i], dev)

    for i in peers:
        g_gain(0, i, zdev[i], me).start()
    w_send(0)
    for n in range(NCH):
        w_local(n, z).start()
    cot_local = pltpu.make_async_copy(cot_in, s.cot.at[z], s.ol.at[0])
    cot_local.start()
    for i in peers:
        g_gain(0, i, zdev[i], place(x, zdn[i], c)).wait_recv()
    for i in range(ZN):
        g_gain(1, i, xdev, place(x, zdn[i], c)).start()
    for i in range(ZN):
        g_gain(2, i, cdev, place(x, zdn[i], c)).start()
    for i in range(ZN):
        g_gain(1, i, xdev, place(1 - x, zdn[i], c)).wait_recv()
        g_gain(2, ZN + i, cdev, place(1 - x, zdn[i], c)).start()
    for i in range(8):
        xx = x if i < ZN else 1 - x
        g_gain(2, i, cdev, place(xx, zdn[i % ZN], 1 - c)).wait_recv()
    for i in peers:
        g_gain(0, i, zdev[i], me).wait_send()
    for i in range(ZN):
        g_gain(1, i, xdev, place(x, zdn[i], c)).wait_send()
    for i in range(8):
        xx = x if i < ZN else 1 - x
        g_gain(2, i, cdev, place(xx, zdn[i % ZN], c)).wait_send()
    vec = s.vec
    vec[...] = jnp.zeros((8, VW), F32)
    gain_g = group_gain()
    tmp, qkv, swish = s.tmp, s.qkv, s.swish

    def columns(n, t):
        return W[n, :, :, pl.ds(pl.multiple_of(t * 256, 256), 256)].reshape(D, 256)

    def all_keys():
        return qkv[:, :, 256:512].reshape(2 * TOK, 256)

    def all_values():
        return qkv[:, :, 512:1024].reshape(2 * TOK, CH)

    def out_copies(j, g, dst):
        here, there = s.ostage.at[j, pl.ds(g * HR, HR)], dst.at[own_rows(g)]
        return (
            remote(here, there, s.o_s.at[j, g], s.o_r.at[j, g], ydev),
            pltpu.make_async_copy(here, there, s.oo.at[j, g]),
        )

    pump_z(0, 1)
    tokens = tok[...].astype(F32)
    n_first, _ = normed(tokens)
    s.first[z] = (n_first * gain_row(0)).astype(BF)
    for part in range(2):
        ag_send(s.first, 0, False, part)
    ag_forward(s.first, 0, 1, 0)
    pump_z(0, 2)
    w_own(6)
    w_own(1)
    w_own(0)
    ag_forward(s.first, 0, 1, 1)
    ag_forward(s.first, 0, 2, 0)
    ag_forward(s.first, 0, 3, 0)
    w_send(3)
    pump_z(0, 3)
    w_send(1)
    w_own(3)
    w_own(2)
    w_own(4)
    pump_x(0, 0)
    pump_x(0, 1)
    ag_forward(s.first, 0, 2, 1)
    pump_z(3, 1)
    w_send(2)
    pump_z(3, 2)
    pump_z(1, 1)
    pump_z(1, 2)
    pump_x(3, 0)
    pump_x(3, 1)
    pump_z(3, 3)
    cot_local.wait()
    for part in range(2):
        ag_send(s.cot, 1, False, part)
    pump_x(1, 0)
    pump_x(1, 1)
    pump_x(0, 2)
    pump_x(0, 3)
    pump_z(1, 3)
    w_send(5)
    ag_forward(s.first, 0, 3, 1)
    for part in range(2):
        ag_wait(s.first, 0, False, part)
    pump_z(2, 1)
    w_send(4)
    pump_z(2, 2)
    w_fin(0)

    def project_qk(t):
        scale = jnp.where(t == 1, 0.0625, 1.0)
        out = nn(s.first[...].reshape(TOK, D), columns(0, t)) * scale
        qkv[c, :, pl.ds(pl.multiple_of(t * 256, 256), 256)] = out.astype(BF)

    loop(2, project_qk)
    pump_x(1, 2)
    pump_x(1, 3)
    w_fin(1)

    def project_v(t):
        out = nn(s.first[...].reshape(TOK, D), columns(1, t))
        qkv[c, :, pl.ds(pl.multiple_of(512 + t * 256, 256), 256)] = out.astype(BF)

    loop(2, project_v)

    def kv_copy(cc):
        blk = qkv.at[cc, :, pl.ds(256, 768)]
        return remote(blk, blk, s.kv_s.at[0], s.kv_r.at[0], cdev)

    kv_copy(c).start()
    pump_z(2, 3)
    ag_forward(s.cot, 1, 1, 0)
    ag_forward(s.cot, 1, 1, 1)
    pump_x(2, 0)
    pump_x(2, 1)
    kv_copy(1 - c).wait_recv()

    def retain(h):
        rows = pl.ds(pl.multiple_of(h * 256, 256), 256)
        later = position((256, 2 * TOK), 0, False, h * 256)
        earlier = position((256, 2 * TOK), 1, True, 0)
        scores = nt(qkv[c, rows, 0:256], all_keys()) * decay(later, earlier)
        s.ret[rows, :] = nn(scores.astype(BF), all_values())

    loop(2, retain)
    pump_x(3, 2)
    pump_x(3, 3)
    w_send(6)
    pump_x(2, 2)
    pump_x(2, 3)
    w_fin(2)

    def project_s(t):
        out = nn(s.first[...].reshape(TOK, D), columns(2, t))
        swish[:, pl.ds(pl.multiple_of(t * 256, 256), 256)] = out

    loop(2, project_s)
    def gate(h):
        rows = pl.ds(pl.multiple_of(h * BLK, BLK), BLK)
        n, _ = normed(s.ret[rows, :])
        w = swish[rows, :]
        YB[3, rows, :] = (n * gain_g * (w / (1.0 + jnp.exp(-w)))).astype(BF)

    loop(ZN, gate)
    w_own(5)
    pump_z(5, 1)
    w_fin(3)
    rs_a(0, 0, (3,), 0)
    rs_y(0, 0, (3,), 0, 0)
    rs_a(0, 0, (3,), 1)
    pump_z(5, 2)
    pump_z(5, 3)
    pump_z(4, 1)
    rs_y(0, 0, (3,), 0, 1)
    ag_forward(s.cot, 1, 2, 0)
    rs_y(0, 0, (3,), 1, 0)
    r_pass(0, 0, 1, 0, 1)
    rs_y(0, 0, (3,), 1, 1)
    pump_z(6, 1)
    ag_forward(s.cot, 1, 2, 1)
    r_pass(0, 0, 1, 1, 1)
    pump_z(4, 2)
    pump_x(5, 0)
    pump_x(5, 1)
    ag_forward(s.cot, 1, 3, 0)
    pump_z(6, 2)
    pump_z(4, 3)
    pump_x(6, 0)
    pump_x(6, 1)
    r_pass(0, 0, 0, 0, 1)
    r_pass(0, 0, 1, 0, 2)
    r_pass(0, 0, 1, 1, 2)
    pump_x(5, 2)
    pump_x(5, 3)
    pump_x(4, 0)
    pump_x(4, 1)
    r_pass(0, 0, 0, 1, 1)
    pump_z(6, 3)
    r_pass(0, 0, 0, 0, 2)
    ag_forward(s.cot, 1, 3, 1)
    hidden = tok[own_rows(1), :].astype(F32) + rs_c(0, 0, 1)
    s.hidden[32:64, :] = hidden
    n_second, _ = normed(hidden)
    s.second[z, own_rows(1), :] = (n_second * gain_row(1)).astype(BF)
    ag_send(s.second, 2, True, 1)
    r_pass(0, 0, 0, 1, 2)
    ag_forward(s.second, 2, 1, 1)
    hidden = tok[own_rows(0), :].astype(F32) + rs_c(0, 0, 0)
    s.hidden[0:32, :] = hidden
    n_second, _ = normed(hidden)
    s.second[z, own_rows(0), :] = (n_second * gain_row(1)).astype(BF)
    ag_send(s.second, 2, True, 0)
    ag_forward(s.second, 2, 2, 1)
    pump_x(6, 2)
    pump_x(6, 3)
    for part in range(2):
        ag_wait(s.cot, 1, False, part)
    ag_forward(s.second, 2, 1, 0)
    ag_forward(s.second, 2, 3, 1)
    pump_x(4, 2)
    pump_x(4, 3)
    w_fin(4)
    w_fin(5)

    def feed(g):
        rows_g = pl.ds(g * 256, 256)

        def tile(t):
            sec = group_rows(s.second, g)
            cols = pl.ds(pl.multiple_of(t * 256, 256), 256)
            tmp[2 * t, rows_g, :] = nn(sec, columns(4, t))
            tmp[2 * t + 1, rows_g, :] = nn(sec, columns(5, t))

            def act(h):
                rows = pl.ds(pl.multiple_of(g * 256 + h * HALF, HALF), HALF)
                a, u = tmp[2 * t, rows, :], tmp[2 * t + 1, rows, :]
                th = jnp.tanh(ROOT * (a + 0.044715 * (a * a * a)))
                half = 0.5 * (1.0 + th)
                gelu = a * half
                slope = half + 0.5 * a * (1.0 - th * th) * (ROOT * (1.0 + 0.134145 * (a * a)))
                YB[6, rows, cols] = (gelu * u).astype(BF)
                tmp[2 * t, rows, :] = u * slope
                tmp[2 * t + 1, rows, :] = gelu

            loop(4, act)

        loop(2, tile)

    w_fin(6)

    def feed_back(g):
        rows_g = pl.ds(g * 256, 256)

        def tile(t):
            cols = pl.ds(pl.multiple_of(t * 256, 256), 256)
            tmp[4, rows_g, :] = nn(group_rows(s.cot, g), columns(6, t))

            def act(h):
                rows = pl.ds(pl.multiple_of(g * 256 + h * HALF, HALF), HALF)
                gm = tmp[4, rows, :]
                YB[4, rows, cols] = (gm * tmp[2 * t, rows, :]).astype(BF)
                YB[5, rows, cols] = (gm * tmp[2 * t + 1, rows, :]).astype(BF)

            loop(4, act)

        loop(2, tile)

    ag_forward(s.second, 2, 2, 0)
    ag_wait(s.second, 2, True, 1)
    ag_forward(s.second, 2, 3, 0)
    feed(1)
    feed_back(1)
    rs_done(0, 0, 1)
    rs_a(1, 0, (4, 5), 1)
    ag_wait(s.second, 2, True, 0)
    feed(0)
    transpose(s.second, True)
    feed_back(0)
    rs_done(0, 0, 0)
    rs_a(1, 0, (4, 5), 0)
    rs_y(1, 0, (4, 5), 1, 0)
    grad_a(4, True)
    r_pass(1, 0, 1, 0, 1)
    rs_a(2, 1, (6,), 1)
    rs_y(1, 0, (4, 5), 1, 1)
    rs_y(1, 0, (4, 5), 0, 0)
    r_pass(1, 0, 1, 1, 1)
    r_pass(1, 0, 1, 0, 2)
    grad_a(5, True)
    r_pass(1, 0, 1, 1, 2)
    r_pass(1, 0, 0, 0, 1)
    rs_y(1, 0, (4, 5), 0, 1)
    g_in = rs_c(1, 0, 1)
    n_second, rstd = normed(s.hidden[32:64, :])
    vec[:, 256:512] = vec[:, 256:512] + packed(jnp.sum(g_in * n_second, axis=0, keepdims=True))
    ghid = s.cot[z, own_rows(1), :].astype(F32) + norm_back(n_second, rstd, g_in * gain_row(1))
    s.ghid[32:64, :] = ghid
    s.hlow[z, own_rows(1), :] = ghid.astype(BF)
    ag_send(s.hlow, 3, True, 1)
    r_pass(1, 0, 0, 0, 2)
    r_pass(1, 0, 0, 1, 1)
    rs_y(2, 1, (6,), 1, 0)
    transpose(s.cot, True)
    r_pass(1, 0, 0, 1, 2)
    ag_forward(s.hlow, 3, 1, 1)
    g_in = rs_c(1, 0, 0)
    n_second, rstd = normed(s.hidden[0:32, :])
    vec[:, 256:512] = vec[:, 256:512] + packed(jnp.sum(g_in * n_second, axis=0, keepdims=True))
    ghid = s.cot[z, own_rows(0), :].astype(F32) + norm_back(n_second, rstd, g_in * gain_row(1))
    s.ghid[0:32, :] = ghid
    s.hlow[z, own_rows(0), :] = ghid.astype(BF)
    ag_send(s.hlow, 3, True, 0)
    rs_y(2, 1, (6,), 1, 1)
    r_pass(2, 1, 1, 0, 1)
    grad_a(6, True)
    ag_forward(s.hlow, 3, 2, 1)
    ag_forward(s.hlow, 3, 1, 0)
    ag_forward(s.hlow, 3, 3, 1)
    r_pass(2, 1, 1, 1, 1)
    ag_forward(s.hlow, 3, 2, 0)
    grad_b(5, True)
    ag_forward(s.hlow, 3, 3, 0)
    rs_a(2, 1, (6,), 0)
    grad_b(6, True)
    ag_wait(s.hlow, 3, True, 1)
    ag_wait(s.hlow, 3, True, 0)
    r_pass(2, 1, 1, 0, 2)
    transpose(s.hlow, False)
    grad_a(3, True)
    rs_y(2, 1, (6,), 0, 0)
    grad_b(4, True)
    def back_gated(g):
        def tile(t):
            out = nn(group_rows(s.hlow, g), columns(3, t))
            for q in range(8):
                tmp[t, q * HALF + g * HR : q * HALF + g * HR + HR, :] = out[q * HR : q * HR + HR]

        loop(2, tile)

        def back_gate(h, total):
            rows = pl.ds(pl.multiple_of(h * HALF + g * HR, HR), HR)
            n, rstd = normed(s.ret[rows, :])
            w, g_out = swish[rows, :], jnp.concatenate([tmp[0, rows, :], tmp[1, rows, :]], axis=1)
            sig = 1.0 / (1.0 + jnp.exp(-w))
            silu = w * sig
            YB[2, rows, :] = (g_out * (n * gain_g) * (sig * (1.0 + w * (1.0 - sig)))).astype(BF)
            gs = g_out * silu
            s.dr[rows, :] = norm_back(n, rstd, gs * gain_g).astype(BF)
            return total + jnp.sum(gs * n, axis=0, keepdims=True)

        group = lax.fori_loop(0, 8, back_gate, jnp.zeros((1, CH), F32))
        vec[0:4, 512:VW] = vec[0:4, 512:VW] + jnp.concatenate([group[:, 128 * q : 128 * q + 128] for q in range(4)], axis=0)

    back_gated(0)
    transpose(s.first, False)
    back_gated(1)
    def back_keys(core, h):
        rows = pl.ds(pl.multiple_of(h * 256, 256), 256)
        keys, values = qkv[core, rows, 256:512], qkv[core, rows, 512:1024]
        query = qkv[c, :, 0:256]
        r = lax.broadcasted_iota(jnp.int32, (256, TOK), 0) + h * 256
        earlier = r + (r // BLK) * BLK + core * BLK
        table = decay(position((256, TOK), 1, False, 0), earlier)
        weights = (nt(keys, query) * table).astype(BF)
        slopes = (nt(values, s.dr[...]) * table).astype(BF)
        return rows, nn(slopes, query), nn(weights, s.dr[...])

    def back_other(h):
        rows, dk, dv = back_keys(1 - c, h)
        s.dkv_s[rows, 0:256] = dk.astype(BF)
        s.dkv_s[rows, 256:768] = dv.astype(BF)

    def back_own(h):
        rows, dk, dv = back_keys(c, h)
        tmp[0, rows, :] = dk
        tmp[1, rows, :] = dv[:, 0:256]
        tmp[2, rows, :] = dv[:, 256:512]

    loop(2, back_other)
    dkv_copy = remote(s.dkv_s, s.dkv_r, s.kv_s.at[1], s.kv_r.at[1], cdev)
    dkv_copy.start()
    loop(2, back_own)

    r_pass(2, 1, 0, 0, 1)
    grad_b(3, False)
    r_pass(2, 1, 1, 1, 2)
    def back_query(h):
        rows = pl.ds(pl.multiple_of(h * 256, 256), 256)
        later = position((256, 2 * TOK), 0, False, h * 256)
        earlier = position((256, 2 * TOK), 1, True, 0)
        slopes = nt(s.dr[rows, :], all_values()) * decay(later, earlier)
        YB[0, rows, 0:256] = nn(slopes.astype(BF), all_keys()).astype(BF)

    loop(2, back_query)
    dkv_copy.wait_recv()

    def back_sum(h):
        rows = pl.ds(pl.multiple_of(h * BLK, BLK), BLK)
        other = s.dkv_r[rows, :].astype(F32)
        YB[0, rows, 256:512] = ((tmp[0, rows, :] + other[:, 0:256]) * 0.0625).astype(BF)
        YB[1, rows, 0:256] = (tmp[1, rows, :] + other[:, 256:512]).astype(BF)
        YB[1, rows, 256:512] = (tmp[2, rows, :] + other[:, 512:768]).astype(BF)

    loop(ZN, back_sum)

    rs_done(1, 0, 0)
    rs_a(3, 0, (0, 1, 2), 0)
    rs_done(1, 0, 1)
    rs_a(3, 0, (0, 1, 2), 1)
    rs_y(2, 1, (6,), 0, 1)
    grad_sent(5)
    grad_a(1, False)
    r_pass(2, 1, 0, 0, 2)
    rs_y(3, 0, (0, 1, 2), 0, 0)
    rs_y(3, 0, (0, 1, 2), 0, 1)
    r_pass(3, 0, 0, 0, 1)
    r_pass(2, 1, 0, 1, 1)
    grad_b(1, False)
    rs_y(3, 0, (0, 1, 2), 1, 0)
    r_pass(2, 1, 0, 1, 2)
    rs_y(3, 0, (0, 1, 2), 1, 1)
    s.ostage[1, 32:64, :] = (s.hidden[32:64, :] + rs_c(2, 1, 1)).astype(BF)
    for copy in out_copies(1, 1, res_o):
        copy.start()
    grad_sent(4)
    grad_a(0, False)
    r_pass(3, 0, 0, 1, 1)
    grad_sent(6)
    grad_a(2, False)
    r_pass(3, 0, 0, 0, 2)
    r_pass(3, 0, 1, 0, 1)
    r_pass(3, 0, 1, 1, 1)
    s.ostage[1, 0:32, :] = (s.hidden[0:32, :] + rs_c(2, 1, 0)).astype(BF)
    for copy in out_copies(1, 0, res_o):
        copy.start()
    r_pass(3, 0, 0, 1, 2)
    r_pass(3, 0, 1, 0, 2)
    g_in = rs_c(3, 0, 0)
    n_first, rstd = normed(tok[own_rows(0), :].astype(F32))
    vec[:, 0:256] = vec[:, 0:256] + packed(jnp.sum(g_in * n_first, axis=0, keepdims=True))
    g_tok = s.ghid[0:32, :] + norm_back(n_first, rstd, g_in * gain_row(0))
    s.ostage[0, 0:32, :] = g_tok.astype(BF)
    grad_b(0, False)
    r_pass(3, 0, 1, 1, 2)
    grad_b(2, False)
    g_in = rs_c(3, 0, 1)
    n_first, rstd = normed(tok[own_rows(1), :].astype(F32))
    vec[:, 0:256] = vec[:, 0:256] + packed(jnp.sum(g_in * n_first, axis=0, keepdims=True))
    g_tok = s.ghid[32:64, :] + norm_back(n_first, rstd, g_in * gain_row(0))
    s.ostage[0, 32:64, :] = g_tok.astype(BF)
    def v_copy(j, dst, dev):
        return remote(vec, dst, s.v_s.at[j], s.v_r.at[j], dev)

    v_copy(0, s.vrc, cdev).start()
    v_copy(0, s.vrc, cdev).wait()
    vec[...] = vec[...] + s.vrc[...]
    v_copy(1, s.vrx, xdev).start()
    v_copy(1, s.vrx, xdev).wait()
    vec[...] = vec[...] + s.vrx[...]
    v_copy(2, s.vry, ydev).start()
    for copy in out_copies(0, 0, gtok_o):
        copy.start()
    for copy in out_copies(0, 1, gtok_o):
        copy.start()
    v_copy(2, s.vry, ydev).wait()
    vec[:, 0:512] = vec[:, 0:512] + s.vry[:, 0:512]
    vz = s.vz
    vz[z] = vec[...]
    for i in peers:
        v_copy(2 + i, vz.at[z], zdev[i]).start()
    for i in peers:
        there = vz.at[zdn[i]]
        remote(there, there, s.v_s.at[2 + i], s.v_r.at[2 + i], zdev[i]).wait_recv()
    for i in peers:
        v_copy(2 + i, vz.at[z], zdev[i]).wait_send()
    vec_o[:, 0:512] = ((vz[0, :, 0:512] + vz[1, :, 0:512]) + vz[2, :, 0:512]) + vz[3, :, 0:512]
    for zz in range(ZN):
        vec_o[:, 512 + 128 * zz : 640 + 128 * zz] = vz[zz, :, 512:VW]
    for j, dst in enumerate((gtok_o, res_o)):
        for g in range(2):
            there = dst.at[pl.ds(pl.multiple_of((1 - y) * HALF + g * HR, HR), HR)]
            a, b = out_copies(j, g, dst)
            a.wait_send()
            b.wait()
            remote(there, there, s.o_s.at[j, g], s.o_r.at[j, g], ydev).wait_recv()
    for n in range(4):
        grad_sent(n)
    for n in range(NCH):
        grad_done(n)
    loop(NCH, w_done)
    kv_copy(c).wait_send()
    dkv_copy.wait_send()
    for ia, (buf, own) in enumerate(((s.first, False), (s.cot, False), (s.second, True), (s.hlow, True))):
        ag_done(buf, ia, own)
    for g in range(2):
        rs_done(2, 1, g)
        rs_done(3, 0, g)


def finish_kernel(gwa, gwf, res, gtok, vec, o_res, o_tok, o_q, o_k, o_v, o_s, o_o, o_g, o_u, o_d, o_first, o_second, o_group):
    o_res[0] = res[...].astype(F32)
    o_tok[0] = gtok[...].astype(F32)
    for n, out in enumerate((o_g, o_u, o_d)):
        out[...] = gwf[n].astype(F32)
    both = jnp.swapaxes(gwa[0].astype(F32), 0, 1)
    o_q[...] = both[:, :, 0:256]
    o_k[...] = both[:, :, 256:512]
    for n, out in enumerate((o_v, o_s, o_o)):
        out[...] = jnp.swapaxes(gwa[n + 1].astype(F32), 0, 1)
    me = lax.axis_index("fsdp") * 8 + lax.axis_index("ctx")
    quarter = lax.rem(me, 4)

    def row(r, start, stop):
        block = vec[:, start:stop]
        return jnp.sum(jnp.where(lax.broadcasted_iota(jnp.int32, block.shape, 0) == r, block, 0.0), axis=0, keepdims=True)

    for out, start in ((o_first, 0), (o_second, 256)):
        pair = row(me // 2, start, start + 256)
        out[...] = jnp.where(lax.rem(me, 2) == 0, pair[:, 0:128], pair[:, 128:256])
    for zz in range(ZN):
        line = row(me // 4, 512 + 128 * zz, 640 + 128 * zz)
        total = jnp.zeros((1, 32), F32)
        for q in range(4):
            total = total + jnp.where(quarter == q, line[:, 32 * q : 32 * q + 32], 0.0)
        o_group[zz : zz + 1, :] = total


def finish(res, gtok, gwa, gwf, vec):
    steps = 2
    rows = BLK // steps
    flat = pl.BlockSpec((rows, D), lambda i: (i, 0))
    deep = pl.BlockSpec((1, rows, D), lambda i: (0, i, 0))
    narrow = pl.BlockSpec((rows, ZN, 256), lambda i: (i, 0, 0))
    wide = pl.BlockSpec((rows, ZN, CH), lambda i: (i, 0, 0))

    def whole(*shape):
        return pl.BlockSpec(shape, lambda i: (0,) * len(shape))

    def f32(*shape):
        return jax.ShapeDtypeStruct(shape, F32)

    outs = pl.pallas_call(
        finish_kernel,
        grid=(steps,),
        in_specs=[
            pl.BlockSpec((4, ZN, rows, CH), lambda i: (0, 0, i, 0)),
            pl.BlockSpec((3, rows, D), lambda i: (0, i, 0)),
            flat,
            flat,
            whole(8, 1024),
        ],
        out_specs=[deep, deep, narrow, narrow, wide, wide, wide, flat, flat, flat, whole(1, BLK), whole(1, BLK), whole(ZN, 32)],
        out_shape=[f32(1, BLK, D)] * 2
        + [f32(BLK, ZN, 256)] * 2
        + [f32(BLK, ZN, CH)] * 3
        + [f32(BLK, D)] * 3
        + [f32(1, BLK)] * 2
        + [f32(ZN, 32)],
        compiler_params=pltpu.CompilerParams(vmem_limit_bytes=VLIM),
    )(gwa, gwf, res, gtok, vec)
    return tuple(outs[:10]) + (outs[10].reshape(BLK), outs[11].reshape(BLK), outs[12])


def start_kernel(q, k, v, sw, o, g_first, g_second, g_group, rate, pk, gp, lr):
    for ref, at in ((q, 0), (k, 256), (v, 512), (sw, 1024), (o, 1536)):
        pk[:, :, at : at + ref.shape[2]] = jnp.swapaxes(ref[...], 0, 1)
    me = lax.axis_index("fsdp") * 8 + lax.axis_index("ctx")
    quarter = lax.rem(me, 4)
    gp[...] = jnp.zeros((8, BLK), F32)
    gp[0:1, :] = g_first[...].astype(F32)
    gp[1:2, :] = g_second[...].astype(F32)
    lane = lax.broadcasted_iota(jnp.int32, (ZN, BLK), 1) // 32
    wide = jnp.concatenate([g_group[...].astype(F32)] * 4, axis=1)
    gp[2:6, :] = jnp.where(lane == quarter, wide, 0.0)
    lr[...] = jnp.log(rate[...])


def begin(w_query, w_key, w_value, w_swish, w_output, gain_first, gain_second, gain_group, decay_rate):
    steps = 2
    rows = BLK // steps
    narrow = pl.BlockSpec((rows, ZN, 256), lambda i: (i, 0, 0))
    wide = pl.BlockSpec((rows, ZN, CH), lambda i: (i, 0, 0))

    def whole(*shape):
        return pl.BlockSpec(shape, lambda i: (0,) * len(shape))

    pk, gp, lr = pl.pallas_call(
        start_kernel,
        grid=(steps,),
        in_specs=[narrow, narrow, wide, wide, wide, whole(1, BLK), whole(1, BLK), whole(ZN, 32), whole(1, ZN)],
        out_specs=[pl.BlockSpec((ZN, rows, 4 * CH), lambda i: (0, i, 0)), whole(8, BLK), whole(1, ZN)],
        out_shape=[
            jax.ShapeDtypeStruct((ZN, BLK, 4 * CH), BF),
            jax.ShapeDtypeStruct((8, BLK), F32),
            jax.ShapeDtypeStruct((1, ZN), F32),
        ],
        compiler_params=pltpu.CompilerParams(vmem_limit_bytes=VLIM),
    )(w_query, w_key, w_value, w_swish, w_output, gain_first[None], gain_second[None], gain_group, decay_rate[None])
    return pk, gp, lr[0]


def fused(
    tokens, w_query, w_key, w_value, w_swish, w_output, w_gelu, w_up, w_down, gain_first, gain_second, gain_group, decay_rate, cotangent
):
    pk, gp, lr = begin(w_query, w_key, w_value, w_swish, w_output, gain_first, gain_second, gain_group, decay_rate)
    shapes = [
        jax.ShapeDtypeStruct((BLK, D), BF),
        jax.ShapeDtypeStruct((BLK, D), BF),
        jax.ShapeDtypeStruct((4, ZN, BLK, CH), BF),
        jax.ShapeDtypeStruct((3, BLK, D), BF),
        jax.ShapeDtypeStruct((8, 1024), F32),
    ]
    hbm = pl.BlockSpec(memory_space=pl.ANY)
    vmem = pl.BlockSpec(memory_space=pltpu.VMEM)
    smem = pl.BlockSpec(memory_space=pltpu.SMEM)
    scratch = [pltpu.VMEM(*v) for v in SCRATCH.values()]
    for shape in SEMS.values():
        scratch.append(pltpu.SemaphoreType.REGULAR((3,)) if shape is None else pltpu.SemaphoreType.DMA(shape))
    result, g_tok, gwa, gwf, vec = pl.pallas_call(
        kernel,
        out_shape=shapes,
        in_specs=[vmem, vmem, smem, hbm, hbm, hbm, hbm, hbm],
        out_specs=[hbm, hbm, hbm, hbm, vmem],
        scratch_shapes=scratch,
        compiler_params=pltpu.CompilerParams(collective_id=0, has_side_effects=True, vmem_limit_bytes=VLIM),
    )(tokens[0], gp, lr, cotangent[0], pk, w_gelu, w_up, w_down)
    return finish(result, g_tok, gwa, gwf, vec)


highest_precision = lax.Precision.HIGHEST


def prefix(part, axis, combine, identity):
    place = lax.axis_index(axis)
    gathered = jax.tree.map(lambda a: lax.all_gather(a, axis), part)
    state = jax.tree.map(lambda a, e: jnp.zeros_like(a) + jnp.asarray(e, a.dtype), part, identity)

    def one(turn, state):
        return combine(
            state, jax.tree.map(lambda a: lax.dynamic_index_in_dim(a, turn, 0, False), gathered)
        )

    return lax.fori_loop(0, place, one, state)


def entering_2(value, axis, combine, identity):
    devices, mine = (lax.axis_size(axis), lax.axis_index(axis))
    everything = jax.tree.map(
        lambda part, kind: lax.all_gather(part.astype(kind), axis),
        value,
        jax.tree.map(lambda a: jnp.bfloat16 if a.dtype == jnp.float32 else a.dtype, value),
    )
    start = jax.tree.map(
        lambda part, zero: jnp.broadcast_to(jnp.asarray(zero, part.dtype), part.shape),
        value,
        identity,
    )

    def turn(k, before):
        at = devices - 1 - k
        reached = at > mine
        new = combine(
            before, jax.tree.map(lambda part, own: part[at].astype(own.dtype), everything, value)
        )
        return jax.tree.map(lambda a, b: jnp.where(reached, a, b), new, before)

    return lax.fori_loop(0, devices, turn, start)


def norm_rows(values, gain):
    center = values - jnp.mean(values, axis=-1, keepdims=True)
    spread = jnp.mean(center * center, axis=-1, keepdims=True)
    return center * lax.rsqrt(spread + 1e-05) * gain


def entry_weights(length, log_rate):
    position = jnp.arange(length).astype(jnp.float32)
    return jnp.exp((position[:, None] + 1.0) * log_rate[None, :])


def exit_weights(length, log_rate):
    position = jnp.arange(length).astype(jnp.float32)
    return jnp.exp((length - 1.0 - position)[:, None] * log_rate[None, :])


def decay_matrix(length, log_rate):
    position = jnp.arange(length).astype(jnp.float32)
    distance = position[:, None] - position[None, :]
    causal = distance >= 0.0
    return jnp.where(
        causal[None], jnp.exp(jnp.where(causal, distance, 0.0)[None] * log_rate[:, None, None]), 0.0
    )


def retain_out(query_block, key_block_rows, value_block_rows, retention_state, log_rate):
    length = query_block.shape[1]
    scores = (
        jnp.einsum("sthk,sqhk->shtq", query_block, key_block_rows, precision=highest_precision)
        * decay_matrix(length, log_rate)[None]
    )
    within = jnp.einsum("shtq,sqhv->sthv", scores, value_block_rows, precision=highest_precision)
    carried_state = jnp.einsum(
        "sthk,shkv->sthv",
        query_block * entry_weights(length, log_rate)[None, :, :, None],
        retention_state,
        precision=highest_precision,
    )
    return within + carried_state


def retain_low(query_low, key_low, query_wide, value_wide, retention_state, log_rate):
    length = query_low.shape[1]
    raw_scores = jnp.einsum(
        "sthk,sqhk->shtq", query_low, key_low, preferred_element_type=jnp.float32
    )
    scores = raw_scores * decay_matrix(length, log_rate)[None]
    within = jnp.einsum("shtq,sqhv->sthv", scores, value_wide, precision=highest_precision)
    carried_state = jnp.einsum(
        "sthk,shkv->sthv",
        query_wide * entry_weights(length, log_rate)[None, :, :, None],
        retention_state,
        precision=highest_precision,
    )
    return within + carried_state


def own_states(key_block_rows, value_block_rows, log_rate):
    length = key_block_rows.shape[1]
    return jnp.einsum(
        "sthk,sthv->shkv",
        key_block_rows * exit_weights(length, log_rate)[None, :, :, None],
        value_block_rows,
        precision=highest_precision,
    )


def combine_states(earlier, later):
    return (earlier[0] * later[0], later[0][None, :, None, None] * earlier[1] + later[1])


def gate_section(retained, swish_in, gain):
    return norm_rows(retained, gain) * jax.nn.silu(swish_in)


def mlp_section(act_gelu, act_up):
    return jax.nn.gelu(act_gelu) * act_up


def general(
    tokens,
    w_query,
    w_key,
    w_value,
    w_swish,
    w_output,
    w_gelu,
    w_up,
    w_down,
    gain_first,
    gain_second,
    gain_group,
    decay_rate,
    cotangent,
):
    f32 = jnp.float32
    bf16 = jnp.bfloat16
    gathered = (
        lax.all_gather(w_query, ("fsdp", "ctx"), axis=0, tiled=True),
        lax.all_gather(w_key, ("fsdp", "ctx"), axis=0, tiled=True),
        lax.all_gather(w_value, ("fsdp", "ctx"), axis=0, tiled=True),
        lax.all_gather(w_swish, ("fsdp", "ctx"), axis=0, tiled=True),
        lax.all_gather(w_output, ("fsdp", "ctx"), axis=0, tiled=True),
        lax.all_gather(w_gelu, ("fsdp", "ctx"), axis=0, tiled=True),
        lax.all_gather(w_up, ("fsdp", "ctx"), axis=0, tiled=True),
        lax.all_gather(w_down, ("fsdp", "ctx"), axis=0, tiled=True),
        lax.all_gather(gain_first, ("fsdp", "ctx"), axis=0, tiled=True),
        lax.all_gather(gain_second, ("fsdp", "ctx"), axis=0, tiled=True),
        lax.all_gather(gain_group, ("fsdp", "ctx"), axis=1, tiled=True),
    )
    (
        full_query,
        full_key,
        full_value,
        full_swish,
        full_output,
        full_gelu,
        full_up,
        full_down,
        full_first,
        full_second,
        full_group,
    ) = gathered
    log_rate = jnp.log(decay_rate)
    piece = tokens.shape[1]
    key_scale = full_query.shape[2] ** (-0.5)
    factor = jnp.exp(piece * log_rate)
    inputs = tokens.astype(f32)
    first_gain = full_first.astype(f32)
    second_gain = full_second.astype(f32)
    group_gain = full_group.astype(f32)
    first_low = norm_rows(inputs, first_gain).astype(bf16)
    query_block = jnp.einsum(
        "spd,dhk->sphk", first_low, full_query, preferred_element_type=f32
    ).astype(bf16)
    key_block_rows = (
        jnp.einsum("spd,dhk->sphk", first_low, full_key, preferred_element_type=f32) * key_scale
    ).astype(bf16)
    value_block_rows = jnp.einsum(
        "spd,dhv->sphv", first_low, full_value, preferred_element_type=f32
    ).astype(bf16)
    swish_in = jnp.einsum("spd,dhv->sphv", first_low, full_swish, preferred_element_type=f32)
    query_wide = query_block.astype(f32)
    key_wide = key_block_rows.astype(f32)
    value_wide = value_block_rows.astype(f32)
    local_state = own_states(key_wide, value_wide, log_rate)
    identity = (jnp.ones_like(factor), jnp.zeros_like(local_state))
    _, entering = prefix((factor, local_state), "ctx", combine_states, identity)
    retained = retain_low(query_block, key_block_rows, query_wide, value_wide, entering, log_rate)
    gated = gate_section(retained, swish_in, group_gain).astype(bf16)
    attn_terms = jnp.einsum("sphv,dhv->spd", gated, full_output, preferred_element_type=f32)
    hidden = inputs + lax.psum(attn_terms, "tp")
    second_low = norm_rows(hidden, second_gain).astype(bf16)
    act_gelu = jnp.einsum("spd,df->spf", second_low, full_gelu, preferred_element_type=f32)
    act_up = jnp.einsum("spd,df->spf", second_low, full_up, preferred_element_type=f32)
    mixed = mlp_section(act_gelu, act_up).astype(bf16)
    mlp_terms = jnp.einsum("spf,df->spd", mixed, full_down, preferred_element_type=f32)
    result = hidden + lax.psum(mlp_terms.astype(jnp.bfloat16), "tp").astype(jnp.float32)
    back_query, back_key, back_value, back_swish, back_output, back_gelu, back_up, back_down = gathered[:8]
    grad_mixed = jnp.einsum("spd,df->spf", cotangent, back_down, preferred_element_type=f32)
    grad_down = jnp.einsum("spd,spf->df", cotangent, mixed, preferred_element_type=f32).astype(bf16)
    _, pull_mlp = jax.vjp(mlp_section, act_gelu, act_up)
    grad_act_gelu, grad_act_up = pull_mlp(grad_mixed)
    gelu_low = grad_act_gelu.astype(bf16)
    up_low = grad_act_up.astype(bf16)
    grad_gelu = jnp.einsum("spd,spf->df", second_low, gelu_low, preferred_element_type=f32).astype(bf16)
    grad_up = jnp.einsum("spd,spf->df", second_low, up_low, preferred_element_type=f32).astype(bf16)
    second_terms = jnp.einsum(
        "spf,df->spd", gelu_low, back_gelu, preferred_element_type=f32
    ) + jnp.einsum("spf,df->spd", up_low, back_up, preferred_element_type=f32)
    grad_second_in = lax.psum(second_terms, "tp")
    _, pull_second = jax.vjp(norm_rows, hidden, second_gain)
    hidden_from_norm, grad_second = pull_second(grad_second_in)
    grad_hidden = cotangent.astype(f32) + hidden_from_norm
    hidden_low = grad_hidden.astype(bf16)
    grad_gated = jnp.einsum("spd,dhv->sphv", hidden_low, back_output, preferred_element_type=f32)
    grad_output = jnp.einsum("spd,sphv->dhv", hidden_low, gated, preferred_element_type=f32).astype(bf16)
    _, pull_gate = jax.vjp(gate_section, retained, swish_in, group_gain)
    grad_retained, grad_swish_in, grad_group = pull_gate(grad_gated)
    swish_low = grad_swish_in.astype(bf16)
    entry_grad = jnp.einsum(
        "sthk,sthv->shkv",
        query_wide * entry_weights(piece, log_rate)[None, :, :, None],
        grad_retained,
        precision=highest_precision,
    )
    _, later_grad = entering_2((factor, entry_grad), "ctx", combine_states, identity)
    _, pull_retain = jax.vjp(
        lambda rows_q, rows_k, rows_v: (
            retain_out(rows_q, rows_k, rows_v, entering, log_rate),
            own_states(rows_k, rows_v, log_rate),
        ),
        query_wide,
        key_wide,
        value_wide,
    )
    grad_query_act, grad_key_act, grad_value_act = pull_retain((grad_retained, later_grad))
    query_low = grad_query_act.astype(bf16)
    key_low = (grad_key_act.astype(bf16).astype(f32) * key_scale).astype(bf16)
    value_low = grad_value_act.astype(bf16)
    grad_query = jnp.einsum("spd,sphk->dhk", first_low, query_low, preferred_element_type=f32).astype(bf16)
    grad_key = jnp.einsum("spd,sphk->dhk", first_low, key_low, preferred_element_type=f32).astype(bf16)
    grad_value = jnp.einsum("spd,sphv->dhv", first_low, value_low, preferred_element_type=f32).astype(bf16)
    grad_swish = jnp.einsum("spd,sphv->dhv", first_low, swish_low, preferred_element_type=f32).astype(bf16)
    first_terms = jnp.einsum("sphk,dhk->spd", query_low, back_query, preferred_element_type=f32)
    first_terms = first_terms + jnp.einsum(
        "sphk,dhk->spd", key_low, back_key, preferred_element_type=f32
    )
    first_terms = first_terms + jnp.einsum(
        "sphv,dhv->spd", value_low, back_value, preferred_element_type=f32
    )
    first_terms = first_terms + jnp.einsum(
        "sphv,dhv->spd", swish_low, back_swish, preferred_element_type=f32
    )
    grad_first_in = lax.psum(first_terms.astype(jnp.bfloat16), "tp").astype(jnp.float32)
    _, pull_first = jax.vjp(norm_rows, inputs, first_gain)
    tokens_from_norm, grad_first = pull_first(grad_first_in)
    grad_tokens = grad_hidden + tokens_from_norm
    owned = tuple(
        lax.psum_scatter(g, ("fsdp", "ctx"), scatter_dimension=0, tiled=True).astype(f32)
        for g in (grad_query, grad_key, grad_value, grad_swish, grad_output, grad_gelu, grad_up, grad_down, grad_first, grad_second)
    ) + (lax.psum_scatter(grad_group, ("fsdp", "ctx"), scatter_dimension=1, tiled=True),)
    return (
        result,
        grad_tokens,
        owned[0],
        owned[1],
        owned[2],
        owned[3],
        owned[4],
        owned[5],
        owned[6],
        owned[7],
        owned[8],
        owned[9],
        owned[10],
    )


def solution(mesh):
    wide, flat = P(("fsdp", "ctx"), "tp", None), P(("fsdp", "ctx"), "tp")
    tok, row, group = P("fsdp", "ctx", None), P(("fsdp", "ctx")), P("tp", ("fsdp", "ctx"))
    in_specs = (tok,) + (wide,) * 5 + (flat,) * 3 + (row, row, group, P("tp"), tok)
    out_specs = (tok, tok) + (wide,) * 5 + (flat,) * 3 + (row, row, group)
    sizes = (mesh.shape["fsdp"], mesh.shape["ctx"], mesh.shape["tp"])
    local = fused if sizes == (2, 2 * ZN, 2) else general
    return jax.shard_map(local, mesh=mesh, in_specs=in_specs, out_specs=out_specs, check_vma=False)
```

```python
import types

import jax
import jax.numpy as jnp
from jax import lax
from jax.experimental import pallas as pl
from jax.experimental.pallas import tpu as pltpu
from jax.sharding import PartitionSpec as P

MESH = pl.DeviceIdType.MESH
BF = jnp.bfloat16
F32 = jnp.float32

ZN = 4
BLK = 128
ROOT = 0.7978845608028654
HR = 32
HALF = 64
TOK = ZN * BLK
D = 2048
CH = 512
NCH = 7
NC = 2
RC = D // NC
RB = 16 // NC
AC = 4
AR = HALF // AC
SETS = 4
VW = 640
VLIM = 62 * 2**20


def nt(a, b):
    return lax.dot_general(a, b, (((1,), (1,)), ((), ())), preferred_element_type=F32)


def nn(a, b):
    return lax.dot_general(a, b, (((1,), (0,)), ((), ())), preferred_element_type=F32)


def normed(v):
    center = v - jnp.mean(v, axis=-1, keepdims=True)
    rstd = lax.rsqrt(jnp.mean(center * center, axis=-1, keepdims=True) + 1e-05)
    return center * rstd, rstd


def norm_back(n, rstd, g):
    return rstd * (
        g - jnp.mean(g, axis=-1, keepdims=True) - n * jnp.mean(g * n, axis=-1, keepdims=True)
    )


def remote(src, dst, ss, rs, dev):
    return pltpu.make_async_remote_copy(src, dst, ss, rs, device_id=dev, device_id_type=MESH)


SCRATCH = dict(
    gall=((16, 8, 128), F32),
    W=((NCH, 16, BLK, CH), BF),
    first=((ZN, BLK, D), BF),
    cot=((ZN, BLK, D), BF),
    second=((ZN, BLK, D), BF),
    hlow=((ZN, BLK, D), BF),
    XT=((16, BLK, TOK), BF),
    qkv=((2, TOK, 1024), BF),
    swish=((TOK, CH), F32),
    ret=((TOK, CH), F32),
    dr=((TOK, CH), BF),
    YB=((NCH, TOK, CH), BF),
    dkv_s=((TOK, 768), BF),
    dkv_r=((TOK, 768), BF),
    tmp=((5, TOK, 256), F32),
    ysend=((2, 2, NC, ZN, HR, RC), BF),
    yrecv=((2, 2, NC, ZN, HR, RC), BF),
    zsend=((2, 2, NC, ZN, HR, RC), BF),
    zrecv=((2, 2, NC, ZN + 1, HR, RC), BF),
    hidden=((HALF, D), F32),
    ghid=((HALF, D), F32),
    rsum=((HALF, D), F32),
    ostage=((2, HALF, D), BF),
    gcs=((2, ZN, BLK, CH), BF),
    gcr=((SETS, 2, ZN, BLK, CH), BF),
    gxs=((SETS, ZN, BLK, CH), BF),
    gxr=((SETS, ZN, BLK, CH), BF),
    gzs=((SETS, ZN, BLK, CH), BF),
    vec=((8, VW), F32),
    vrc=((8, VW), F32),
    vrx=((8, VW), F32),
    vry=((8, VW), F32),
    vz=((ZN, 8, VW), F32),
)
SEMS = dict(
    g_s=(3, 8), g_r=(3, 8),
    wz_s=(NCH, 3), wz_r=(NCH, 3), wx_s=(NCH, 4), wx_r=(NCH, 4), wc_s=(NCH, 8), wc_r=(NCH, 8), wl=(NCH,),
    az_s=(4, AC, 2, ZN), az_r=(4, AC, ZN), ay_s=(4, AC, ZN), ay_r=(4, AC, ZN),
    ry_s=(4, 2, NC), ry_r=(4, 2, NC), rz_s=(4, 2, NC, ZN), rz_r=(4, 2, NC, ZN + 1),
    kv_s=(2,), kv_r=(2,),
    gc_s=(NCH, 2), gc_r=(NCH, 2), gx_s=(NCH,), gx_r=(NCH,), gz_s=(NCH, 3), gz_r=(NCH, 3), gl=(NCH,),
    v_s=(6,), v_r=(6,), o_s=(2, 2), o_r=(2, 2), ol=(1,), oo=(2, 2),
    credit=None,
)
NAMES = list(SCRATCH) + list(SEMS)


def kernel(tok, gp, lr, cot_in, pk, wg, wu, wd, res_o, gtok_o, gwa_o, gwf_o, vec_o, *scratch):
    s = types.SimpleNamespace(**dict(zip(NAMES, scratch)))
    W, YB, XT = s.W, s.YB, s.XT
    x, k, y = lax.axis_index("fsdp"), lax.axis_index("ctx"), lax.axis_index("tp")
    z, c = k // 2, k % 2
    zup = [lax.rem(z + i, ZN) for i in range(ZN)]
    zdn = [lax.rem(z + ZN - i, ZN) for i in range(ZN)]
    zdev = [(x, zup[i] * 2 + c, y) for i in range(ZN)]
    updev, dndev = zdev[1], zdev[ZN - 1]
    xdev, ydev, cdev = (1 - x, k, y), (x, k, 1 - y), (x, z * 2 + 1 - c, y)
    peers = range(1, ZN)

    def place(xx, zz, cc):
        return xx * 8 + zz * 2 + cc

    me = place(x, z, c)
    log_rate = lr[z]

    def loop(n, f):
        def step(i, carry):
            f(i)
            return carry

        lax.fori_loop(0, n, step, 0)

    barrier = pltpu.get_barrier_semaphore()
    for dev in zdev[1:] + [xdev, ydev, cdev]:
        pl.semaphore_signal(barrier, inc=1, device_id=dev, device_id_type=MESH)
    pl.semaphore_wait(barrier, 6)

    def w_src(n, zz):
        if n < 4:
            return pk.at[zz, :, pl.ds(n * CH, CH)]
        return (wg, wu, wd)[n - 4].at[:, pl.ds(pl.multiple_of(zz * CH, CH), CH)]

    def w_local(n, zz):
        return pltpu.make_async_copy(w_src(n, zz), W.at[n, me], s.wl.at[n])

    def w_piece(n, i):
        remote(w_src(n, zup[i]), W.at[n, me], s.wz_s.at[n, i - 1], s.wz_r.at[n, i - 1], zdev[i]).start()

    def w_send(n):
        for i in peers:
            w_piece(n, i)

    def w_z(n, i):
        blk = W.at[n, place(x, zdn[i], c)]
        return remote(blk, blk, s.wz_s.at[n, i - 1], s.wz_r.at[n, i - 1], zdev[i])

    def w_x(n, j, xx):
        blk = W.at[n, place(xx, zdn[j], c)]
        return remote(blk, blk, s.wx_s.at[n, j], s.wx_r.at[n, j], xdev)

    def w_c(n, j, cc):
        xx = x if j < 4 else 1 - x
        blk = W.at[n, place(xx, zdn[j % 4], cc)]
        return remote(blk, blk, s.wc_s.at[n, j], s.wc_r.at[n, j], cdev)

    def w_own(n):
        pltpu.make_async_copy(W.at[n, me], W.at[n, me], s.wl.at[n]).wait()
        w_x(n, 0, x).start()
        w_c(n, 0, c).start()

    def pump_z(n, i):
        w_z(n, i).wait_recv()
        w_x(n, i, x).start()
        w_c(n, i, c).start()

    def pump_x(n, j):
        w_x(n, j, 1 - x).wait_recv()
        w_c(n, ZN + j, c).start()

    def w_fin(n):
        for j in range(8):
            w_c(n, j, 1 - c).wait_recv()

    def w_done(n):
        for i in peers:
            w_z(n, i).wait_send()
        for j in range(ZN):
            w_x(n, j, x).wait_send()
        for j in range(8):
            w_c(n, j, c).wait_send()

    def a_rows(yy, ch):
        return pl.ds(pl.multiple_of(yy * HALF + ch * AR, AR), AR)

    def a_z(buf, ia, ch, zz, way):
        blk = buf.at[zz, a_rows(y, ch)]
        return remote(blk, blk, s.az_s.at[ia, ch, way, zz], s.az_r.at[ia, ch, zz], (updev, dndev)[way])

    def a_y(buf, ia, ch, zz, yy):
        blk = buf.at[zz, a_rows(yy, ch)]
        return remote(blk, blk, s.ay_s.at[ia, ch, zz], s.ay_r.at[ia, ch, zz], ydev)

    def ag_sends(buf, ia, ch, zz, do):
        pl.when((zz <= z) & (z < ZN - 1))(lambda: do(a_z(buf, ia, ch, zz, 0)))
        pl.when((zz >= z) & (z > 0))(lambda: do(a_z(buf, ia, ch, zz, 1)))

    def ag_send(buf, ia, own, part):
        def f(at):
            ch = at + part * (AC // 2)
            ag_sends(buf, ia, ch, z, lambda copy: copy.start())
            if own:
                a_y(buf, ia, ch, z, y).start()

        loop(AC // 2, f)

    def ag_forward(buf, ia, d, part):
        def f(at):
            ch = at + part * (AC // 2)

            def pass_on(zz):
                a_z(buf, ia, ch, zz, 0).wait_recv()
                ag_sends(buf, ia, ch, zz, lambda copy: copy.start())
                a_y(buf, ia, ch, zz, y).start()

            pl.when(z >= d)(lambda: pass_on(z - d))
            pl.when(z + d < ZN)(lambda: pass_on(z + d))

        loop(AC // 2, f)

    def ag_wait(buf, ia, own, part):
        def f(at):
            ch = at + part * (AC // 2)
            for i in range(0 if own else 1, ZN):
                a_y(buf, ia, ch, zdn[i], 1 - y).wait_recv()

        loop(AC // 2, f)

    def ag_done(buf, ia, own):
        def f(ch):
            for i in range(ZN):
                ag_sends(buf, ia, ch, zdn[i], lambda copy: copy.wait_send())
                if own or i > 0:
                    a_y(buf, ia, ch, zdn[i], y).wait_send()

        loop(AC, f)

    def group_rows(buf, g):
        return jnp.concatenate([buf[zz, yy * HALF + g * HR : yy * HALF + g * HR + HR, :] for zz in range(ZN) for yy in range(2)], axis=0)

    def product(chunks, j, yy, g):
        total = None
        for n in chunks:
            rows = []
            for zz in range(ZN):
                at = (g * ZN + zz) * HALF + yy * HR if n > 3 else zz * BLK + yy * HALF + g * HR
                rows.append(YB[n, pl.ds(pl.multiple_of(at, HR), HR), :])
            lhs = jnp.concatenate(rows, axis=0)
            rhs = W[n, pl.ds(j * RB, RB)].reshape(RC, CH)
            part = nt(lhs, rhs)
            total = part if total is None else total + part
        return total.reshape(ZN, HR, RC)

    def r_y(ir, b, g, j):
        return remote(s.ysend.at[b, g, j], s.yrecv.at[b, g, j], s.ry_s.at[ir, g, j], s.ry_r.at[ir, g, j], ydev)

    def r_z(ir, b, g, j, d, way):
        slot = d if way == 0 else jnp.where(d == z - 1, ZN, d)
        return remote(
            s.zsend.at[b, g, j, d],
            s.zrecv.at[b, g, j, slot],
            s.rz_s.at[ir, g, j, d],
            s.rz_r.at[ir, g, j, slot],
            (updev, dndev)[way],
        )

    def r_arrived(ir, b, g, j, slot):
        there = s.zrecv.at[b, g, j, slot]
        remote(there, there, s.rz_s.at[ir, g, j, 0], s.rz_r.at[ir, g, j, slot], updev).wait_recv()

    def rs_a(ir, b, chunks, g):
        def f(j):
            s.ysend[b, g, j] = product(chunks, j, 1 - y, g).astype(BF)
            r_y(ir, b, g, j).start()

        loop(NC, f)

    def r_pass(ir, b, g, j, level):
        def go(dests, way):
            for d in dests:
                if level > 0:
                    r_arrived(ir, b, g, j, d)
                    s.zsend[b, g, j, d] = (s.zsend[b, g, j, d].astype(F32) + s.zrecv[b, g, j, d].astype(F32)).astype(BF)
                r_z(ir, b, g, j, d, way).start()

        pl.when(z == level)(lambda: go(range(ZN - 1, level, -1), 0))
        pl.when(z == ZN - 1 - level)(lambda: go(range(ZN - 1 - level), 1))

    def rs_y(ir, b, chunks, g, j):
        own = product(chunks, j, y, g)
        r_y(ir, b, g, j).wait_recv()
        s.zsend[b, g, j] = (own + s.yrecv[b, g, j].astype(F32)).astype(BF)
        r_pass(ir, b, g, j, 0)

    def rs_c(ir, b, g):
        mine = pl.ds(g * HR, HR)

        def f(j):
            cols = pl.ds(pl.multiple_of(j * RC, RC), RC)
            s.rsum[mine, cols] = s.zsend[b, g, j, z].astype(F32)

            def add(slot):
                r_arrived(ir, b, g, j, slot)
                s.rsum[mine, cols] = s.rsum[mine, cols] + s.zrecv[b, g, j, slot].astype(F32)

            pl.when(z > 0)(lambda: add(z))
            pl.when(z < ZN - 1)(lambda: add(ZN))

        loop(NC, f)
        return s.rsum[mine, :]

    def rs_done(ir, b, g):
        def f(j):
            r_y(ir, b, g, j).wait_send()
            for i in peers:
                r_z(ir, b, g, j, zdn[i], 0).wait_send()

        loop(NC, f)

    def transpose(buf, grouped):
        def f(q):
            cols = pl.ds(pl.multiple_of(q * BLK, BLK), BLK)
            if grouped:
                parts = []
                for g in range(2):
                    for zz in range(ZN):
                        for yy in range(2):
                            parts.append(buf[zz, yy * HALF + g * HR : yy * HALF + g * HR + HR, cols])
                XT[q] = jnp.concatenate(parts, axis=0).T
            else:
                XT[q] = buf[:, :, cols].reshape(TOK, BLK).T

        loop(16, f)

    def grad_rows(n, xx, cc):
        lhs = jnp.concatenate([XT[place(xx, zz, cc)] for zz in range(ZN)], axis=0)
        return nn(lhs, YB[n]).reshape(ZN, BLK, CH)

    def g_c(n, xx):
        return remote(s.gcs.at[xx], s.gcr.at[n % SETS, xx], s.gc_s.at[n, xx], s.gc_r.at[n, xx], cdev)

    def g_x(n):
        return remote(s.gxs.at[n % SETS], s.gxr.at[n % SETS], s.gx_s.at[n], s.gx_r.at[n], xdev)

    def g_dst(n):
        if n < 4:
            return gwa_o.at[n, z]
        return gwf_o.at[n - 4, :, pl.ds(pl.multiple_of(z * CH, CH), CH)]

    def g_z(n, i):
        return remote(s.gzs.at[n % SETS, zup[i]], g_dst(n), s.gz_s.at[n, i - 1], s.gz_r.at[n, i - 1], zdev[i])

    def g_local(n):
        return pltpu.make_async_copy(s.gzs.at[n % SETS, z], g_dst(n), s.gl.at[n])

    def grad_a(n, first_use):
        b = n % SETS

        def f(t):
            xx = (1 - x) * (1 - t) + x * t
            s.gcs[xx] = grad_rows(n, xx, 1 - c).astype(BF)
            g_c(n, xx).start()

        loop(2, f)
        own = grad_rows(n, 1 - x, c)
        g_c(n, 1 - x).wait_recv()
        if not first_use:
            pl.semaphore_wait(s.credit.at[b], 1)
        s.gxs[b] = (own + s.gcr[b, 1 - x].astype(F32)).astype(BF)
        g_x(n).start()
        own = grad_rows(n, x, c)
        g_c(n, x).wait_recv()
        s.gzs[b] = (own + s.gcr[b, x].astype(F32)).astype(BF)
        for xx in range(2):
            g_c(n, xx).wait_send()

    def grad_b(n, more):
        b = n % SETS
        g_x(n).wait_recv()
        s.gzs[b] = (s.gzs[b].astype(F32) + s.gxr[b].astype(F32)).astype(BF)
        for i in peers:
            g_z(n, i).start()
        g_local(n).start()
        g_x(n).wait_send()
        if more:
            pl.semaphore_signal(s.credit.at[b], inc=1, device_id=xdev, device_id_type=MESH)

    def grad_sent(n):
        for i in peers:
            g_z(n, i).wait_send()
        g_local(n).wait()

    def grad_done(n):
        for i in peers:
            g_z(n, i).wait_recv()

    def gain_row(r):
        return jnp.concatenate([s.gall[q, r : r + 1, :] for q in range(16)], axis=1)

    def group_gain():
        pick = lax.broadcasted_iota(jnp.int32, (8, 128), 0) == 2 + z
        parts = []
        for r in range(4):
            total = s.gall[4 * r]
            for q in range(4 * r + 1, 4 * r + 4):
                total = total + s.gall[q]
            parts.append(jnp.sum(jnp.where(pick, total, 0.0), axis=0, keepdims=True))
        return jnp.concatenate(parts, axis=1)

    def packed(row):
        return jnp.concatenate([row[:, 256 * q : 256 * q + 256] for q in range(D // 256)], axis=0)

    def position(shape, dim, both, start):
        r = lax.broadcasted_iota(jnp.int32, shape, dim) + start
        if both:
            core, r = r // TOK, lax.rem(r, TOK)
        else:
            core = c
        return r + (r // BLK) * BLK + core * BLK

    def decay(later, earlier):
        gap = later - earlier
        keep = gap >= 0
        return jnp.where(keep, jnp.exp(jnp.where(keep, gap, 0).astype(F32) * log_rate), 0.0)

    def own_rows(g):
        return pl.ds(pl.multiple_of(y * HALF + g * HR, HR), HR)

    gall = s.gall
    gall[me] = gp[...]

    def g_gain(j, i, dev, q):
        return remote(gall.at[q], gall.at[q], s.g_s.at[j, i], s.g_r.at[j, i], dev)

    for i in peers:
        g_gain(0, i, zdev[i], me).start()
    w_send(0)
    for n in range(NCH):
        w_local(n, z).start()
    cot_local = pltpu.make_async_copy(cot_in, s.cot.at[z], s.ol.at[0])
    cot_local.start()
    for i in peers:
        g_gain(0, i, zdev[i], place(x, zdn[i], c)).wait_recv()
    for i in range(ZN):
        g_gain(1, i, xdev, place(x, zdn[i], c)).start()
    for i in range(ZN):
        g_gain(2, i, cdev, place(x, zdn[i], c)).start()
    for i in range(ZN):
        g_gain(1, i, xdev, place(1 - x, zdn[i], c)).wait_recv()
        g_gain(2, ZN + i, cdev, place(1 - x, zdn[i], c)).start()
    for i in range(8):
        xx = x if i < ZN else 1 - x
        g_gain(2, i, cdev, place(xx, zdn[i % ZN], 1 - c)).wait_recv()
    for i in peers:
        g_gain(0, i, zdev[i], me).wait_send()
    for i in range(ZN):
        g_gain(1, i, xdev, place(x, zdn[i], c)).wait_send()
    for i in range(8):
        xx = x if i < ZN else 1 - x
        g_gain(2, i, cdev, place(xx, zdn[i % ZN], c)).wait_send()
    vec = s.vec
    vec[...] = jnp.zeros((8, VW), F32)
    gain_g = group_gain()
    tmp, qkv, swish = s.tmp, s.qkv, s.swish

    def columns(n, t):
        return W[n, :, :, pl.ds(pl.multiple_of(t * 256, 256), 256)].reshape(D, 256)

    def all_keys():
        return qkv[:, :, 256:512].reshape(2 * TOK, 256)

    def all_values():
        return qkv[:, :, 512:1024].reshape(2 * TOK, CH)

    def out_copies(j, g, dst):
        here, there = s.ostage.at[j, pl.ds(g * HR, HR)], dst.at[own_rows(g)]
        return (
            remote(here, there, s.o_s.at[j, g], s.o_r.at[j, g], ydev),
            pltpu.make_async_copy(here, there, s.oo.at[j, g]),
        )

    w_own(4)
    tokens = tok[...].astype(F32)
    n_first, _ = normed(tokens)
    s.first[z] = (n_first * gain_row(0)).astype(BF)
    for part in range(2):
        ag_send(s.first, 0, False, part)
    w_own(1)
    w_own(6)
    w_own(5)
    w_own(2)
    pump_z(0, 1)
    ag_forward(s.first, 0, 1, 0)
    w_send(1)
    w_own(0)
    ag_forward(s.first, 0, 1, 1)
    ag_forward(s.first, 0, 2, 0)
    pump_z(1, 1)
    pump_z(0, 2)
    pump_x(0, 0)
    pump_x(0, 1)
    w_send(2)
    pump_z(0, 3)
    ag_forward(s.first, 0, 2, 1)
    pump_x(0, 2)
    pump_x(0, 3)
    w_own(3)
    ag_forward(s.first, 0, 3, 0)
    w_send(3)
    pump_z(2, 1)
    pump_z(2, 2)
    pump_x(1, 0)
    pump_x(1, 1)
    pump_x(2, 0)
    pump_x(2, 1)
    pump_z(1, 2)
    pump_z(1, 3)
    cot_local.wait()
    for part in range(2):
        ag_send(s.cot, 1, False, part)
    ag_forward(s.first, 0, 3, 1)
    pump_z(2, 3)
    pump_z(3, 1)
    pump_z(3, 2)
    pump_x(1, 2)
    pump_x(1, 3)
    w_send(6)
    ag_forward(s.cot, 1, 1, 0)
    for part in range(2):
        ag_wait(s.first, 0, False, part)
    pump_x(2, 2)
    pump_x(2, 3)
    w_fin(0)

    def project_qk(t):
        scale = jnp.where(t == 1, 0.0625, 1.0)
        out = nn(s.first[...].reshape(TOK, D), columns(0, t)) * scale
        qkv[c, :, pl.ds(pl.multiple_of(t * 256, 256), 256)] = out.astype(BF)

    loop(2, project_qk)
    w_fin(1)

    def project_v(t):
        out = nn(s.first[...].reshape(TOK, D), columns(1, t))
        qkv[c, :, pl.ds(pl.multiple_of(512 + t * 256, 256), 256)] = out.astype(BF)

    loop(2, project_v)

    def kv_copy(cc):
        blk = qkv.at[cc, :, pl.ds(256, 768)]
        return remote(blk, blk, s.kv_s.at[0], s.kv_r.at[0], cdev)

    kv_copy(c).start()
    w_fin(2)

    def project_s(t):
        out = nn(s.first[...].reshape(TOK, D), columns(2, t))
        swish[:, pl.ds(pl.multiple_of(t * 256, 256), 256)] = out

    loop(2, project_s)
    pump_z(3, 3)
    kv_copy(1 - c).wait_recv()

    def retain(h):
        rows = pl.ds(pl.multiple_of(h * 256, 256), 256)
        later = position((256, 2 * TOK), 0, False, h * 256)
        earlier = position((256, 2 * TOK), 1, True, 0)
        scores = nt(qkv[c, rows, 0:256], all_keys()) * decay(later, earlier)
        s.ret[rows, :] = nn(scores.astype(BF), all_values())

    loop(2, retain)
    ag_forward(s.cot, 1, 1, 1)
    w_send(4)
    pump_x(3, 0)
    pump_x(3, 1)
    pump_x(3, 2)
    pump_x(3, 3)
    w_send(5)
    def gate(h):
        rows = pl.ds(pl.multiple_of(h * BLK, BLK), BLK)
        n, _ = normed(s.ret[rows, :])
        w = swish[rows, :]
        YB[3, rows, :] = (n * gain_g * (w / (1.0 + jnp.exp(-w)))).astype(BF)

    loop(ZN, gate)
    pump_z(6, 1)
    w_fin(3)
    rs_a(0, 0, (3,), 0)
    rs_a(0, 0, (3,), 1)
    ag_forward(s.cot, 1, 2, 0)
    pump_z(6, 2)
    pump_z(6, 3)
    pump_x(6, 0)
    pump_x(6, 1)
    rs_y(0, 0, (3,), 0, 0)
    ag_forward(s.cot, 1, 2, 1)
    rs_y(0, 0, (3,), 0, 1)
    r_pass(0, 0, 0, 0, 1)
    r_pass(0, 0, 0, 1, 1)
    pump_z(4, 1)
    pump_z(4, 2)
    rs_y(0, 0, (3,), 1, 0)
    rs_y(0, 0, (3,), 1, 1)
    ag_forward(s.cot, 1, 3, 0)
    r_pass(0, 0, 1, 0, 1)
    pump_z(4, 3)
    ag_forward(s.cot, 1, 3, 1)
    r_pass(0, 0, 0, 0, 2)
    r_pass(0, 0, 0, 1, 2)
    r_pass(0, 0, 1, 1, 1)
    pump_z(5, 1)
    hidden = tok[own_rows(0), :].astype(F32) + rs_c(0, 0, 0)
    s.hidden[0:32, :] = hidden
    n_second, _ = normed(hidden)
    s.second[z, own_rows(0), :] = (n_second * gain_row(1)).astype(BF)
    ag_send(s.second, 2, True, 0)
    pump_z(5, 2)
    r_pass(0, 0, 1, 0, 2)
    pump_z(5, 3)
    r_pass(0, 0, 1, 1, 2)
    pump_x(5, 0)
    pump_x(5, 1)
    pump_x(4, 0)
    pump_x(4, 1)
    pump_x(4, 2)
    pump_x(4, 3)
    for part in range(2):
        ag_wait(s.cot, 1, False, part)
    ag_forward(s.second, 2, 1, 0)
    hidden = tok[own_rows(1), :].astype(F32) + rs_c(0, 0, 1)
    s.hidden[32:64, :] = hidden
    n_second, _ = normed(hidden)
    s.second[z, own_rows(1), :] = (n_second * gain_row(1)).astype(BF)
    ag_send(s.second, 2, True, 1)
    ag_forward(s.second, 2, 2, 0)
    ag_forward(s.second, 2, 1, 1)
    ag_forward(s.second, 2, 3, 0)
    pump_x(5, 2)
    pump_x(5, 3)
    pump_x(6, 2)
    pump_x(6, 3)
    w_fin(4)
    w_fin(5)

    def feed(g):
        rows_g = pl.ds(g * 256, 256)

        def tile(t):
            sec = group_rows(s.second, g)
            cols = pl.ds(pl.multiple_of(t * 256, 256), 256)
            tmp[2 * t, rows_g, :] = nn(sec, columns(4, t))
            tmp[2 * t + 1, rows_g, :] = nn(sec, columns(5, t))

            def act(h):
                rows = pl.ds(pl.multiple_of(g * 256 + h * HALF, HALF), HALF)
                a, u = tmp[2 * t, rows, :], tmp[2 * t + 1, rows, :]
                th = jnp.tanh(ROOT * (a + 0.044715 * (a * a * a)))
                half = 0.5 * (1.0 + th)
                gelu = a * half
                slope = half + 0.5 * a * (1.0 - th * th) * (ROOT * (1.0 + 0.134145 * (a * a)))
                YB[6, rows, cols] = (gelu * u).astype(BF)
                tmp[2 * t, rows, :] = u * slope
                tmp[2 * t + 1, rows, :] = gelu

            loop(4, act)

        loop(2, tile)

    ag_forward(s.second, 2, 2, 1)
    w_fin(6)

    def feed_back(g):
        rows_g = pl.ds(g * 256, 256)

        def tile(t):
            cols = pl.ds(pl.multiple_of(t * 256, 256), 256)
            tmp[4, rows_g, :] = nn(group_rows(s.cot, g), columns(6, t))

            def act(h):
                rows = pl.ds(pl.multiple_of(g * 256 + h * HALF, HALF), HALF)
                gm = tmp[4, rows, :]
                YB[4, rows, cols] = (gm * tmp[2 * t, rows, :]).astype(BF)
                YB[5, rows, cols] = (gm * tmp[2 * t + 1, rows, :]).astype(BF)

            loop(4, act)

        loop(2, tile)

    ag_wait(s.second, 2, True, 0)
    ag_forward(s.second, 2, 3, 1)
    feed(0)
    feed_back(0)
    rs_done(0, 0, 0)
    rs_a(1, 0, (4, 5), 0)
    ag_wait(s.second, 2, True, 1)
    feed(1)
    transpose(s.second, True)
    feed_back(1)
    grad_a(4, True)
    rs_y(1, 0, (4, 5), 0, 0)
    rs_done(0, 0, 1)
    rs_a(1, 0, (4, 5), 1)
    rs_y(1, 0, (4, 5), 0, 1)
    r_pass(1, 0, 0, 0, 1)
    rs_a(2, 1, (6,), 1)
    grad_a(5, True)
    r_pass(1, 0, 0, 0, 2)
    rs_y(1, 0, (4, 5), 1, 0)
    r_pass(1, 0, 0, 1, 1)
    r_pass(1, 0, 0, 1, 2)
    r_pass(1, 0, 1, 0, 1)
    rs_y(1, 0, (4, 5), 1, 1)
    g_in = rs_c(1, 0, 0)
    n_second, rstd = normed(s.hidden[0:32, :])
    vec[:, 256:512] = vec[:, 256:512] + packed(jnp.sum(g_in * n_second, axis=0, keepdims=True))
    ghid = s.cot[z, own_rows(0), :].astype(F32) + norm_back(n_second, rstd, g_in * gain_row(1))
    s.ghid[0:32, :] = ghid
    s.hlow[z, own_rows(0), :] = ghid.astype(BF)
    ag_send(s.hlow, 3, True, 0)
    transpose(s.cot, True)
    r_pass(1, 0, 1, 0, 2)
    r_pass(1, 0, 1, 1, 1)
    rs_y(2, 1, (6,), 1, 0)
    r_pass(1, 0, 1, 1, 2)
    ag_forward(s.hlow, 3, 1, 0)
    g_in = rs_c(1, 0, 1)
    n_second, rstd = normed(s.hidden[32:64, :])
    vec[:, 256:512] = vec[:, 256:512] + packed(jnp.sum(g_in * n_second, axis=0, keepdims=True))
    ghid = s.cot[z, own_rows(1), :].astype(F32) + norm_back(n_second, rstd, g_in * gain_row(1))
    s.ghid[32:64, :] = ghid
    s.hlow[z, own_rows(1), :] = ghid.astype(BF)
    ag_send(s.hlow, 3, True, 1)
    r_pass(2, 1, 1, 0, 1)
    rs_y(2, 1, (6,), 1, 1)
    grad_a(6, True)
    ag_forward(s.hlow, 3, 2, 0)
    ag_forward(s.hlow, 3, 1, 1)
    r_pass(2, 1, 1, 1, 1)
    ag_forward(s.hlow, 3, 2, 1)
    grad_b(5, True)
    ag_forward(s.hlow, 3, 3, 0)
    grad_b(6, True)
    ag_forward(s.hlow, 3, 3, 1)
    ag_wait(s.hlow, 3, True, 0)
    rs_a(2, 1, (6,), 0)
    def back_gated(g):
        def tile(t):
            out = nn(group_rows(s.hlow, g), columns(3, t))
            for q in range(8):
                tmp[t, q * HALF + g * HR : q * HALF + g * HR + HR, :] = out[q * HR : q * HR + HR]

        loop(2, tile)

        def back_gate(h, total):
            rows = pl.ds(pl.multiple_of(h * HALF + g * HR, HR), HR)
            n, rstd = normed(s.ret[rows, :])
            w, g_out = swish[rows, :], jnp.concatenate([tmp[0, rows, :], tmp[1, rows, :]], axis=1)
            sig = 1.0 / (1.0 + jnp.exp(-w))
            silu = w * sig
            YB[2, rows, :] = (g_out * (n * gain_g) * (sig * (1.0 + w * (1.0 - sig)))).astype(BF)
            gs = g_out * silu
            s.dr[rows, :] = norm_back(n, rstd, gs * gain_g).astype(BF)
            return total + jnp.sum(gs * n, axis=0, keepdims=True)

        group = lax.fori_loop(0, 8, back_gate, jnp.zeros((1, CH), F32))
        vec[0:4, 512:VW] = vec[0:4, 512:VW] + jnp.concatenate([group[:, 128 * q : 128 * q + 128] for q in range(4)], axis=0)

    back_gated(0)
    grad_b(4, True)
    ag_wait(s.hlow, 3, True, 1)
    transpose(s.hlow, False)
    grad_a(3, True)
    rs_y(2, 1, (6,), 0, 0)
    back_gated(1)
    transpose(s.first, False)
    def back_keys(core, h):
        rows = pl.ds(pl.multiple_of(h * 256, 256), 256)
        keys, values = qkv[core, rows, 256:512], qkv[core, rows, 512:1024]
        query = qkv[c, :, 0:256]
        r = lax.broadcasted_iota(jnp.int32, (256, TOK), 0) + h * 256
        earlier = r + (r // BLK) * BLK + core * BLK
        table = decay(position((256, TOK), 1, False, 0), earlier)
        weights = (nt(keys, query) * table).astype(BF)
        slopes = (nt(values, s.dr[...]) * table).astype(BF)
        return rows, nn(slopes, query), nn(weights, s.dr[...])

    def back_other(h):
        rows, dk, dv = back_keys(1 - c, h)
        s.dkv_s[rows, 0:256] = dk.astype(BF)
        s.dkv_s[rows, 256:768] = dv.astype(BF)

    def back_own(h):
        rows, dk, dv = back_keys(c, h)
        tmp[0, rows, :] = dk
        tmp[1, rows, :] = dv[:, 0:256]
        tmp[2, rows, :] = dv[:, 256:512]

    loop(2, back_other)
    dkv_copy = remote(s.dkv_s, s.dkv_r, s.kv_s.at[1], s.kv_r.at[1], cdev)
    dkv_copy.start()
    loop(2, back_own)

    r_pass(2, 1, 0, 0, 1)
    def back_query(h):
        rows = pl.ds(pl.multiple_of(h * 256, 256), 256)
        later = position((256, 2 * TOK), 0, False, h * 256)
        earlier = position((256, 2 * TOK), 1, True, 0)
        slopes = nt(s.dr[rows, :], all_values()) * decay(later, earlier)
        YB[0, rows, 0:256] = nn(slopes.astype(BF), all_keys()).astype(BF)

    loop(2, back_query)
    dkv_copy.wait_recv()

    def back_sum(h):
        rows = pl.ds(pl.multiple_of(h * BLK, BLK), BLK)
        other = s.dkv_r[rows, :].astype(F32)
        YB[0, rows, 256:512] = ((tmp[0, rows, :] + other[:, 0:256]) * 0.0625).astype(BF)
        YB[1, rows, 0:256] = (tmp[1, rows, :] + other[:, 256:512]).astype(BF)
        YB[1, rows, 256:512] = (tmp[2, rows, :] + other[:, 512:768]).astype(BF)

    loop(ZN, back_sum)

    rs_done(1, 0, 0)
    rs_a(3, 0, (0, 1, 2), 0)
    grad_b(3, False)
    grad_sent(6)
    grad_a(2, False)
    grad_sent(5)
    grad_a(1, False)
    rs_y(3, 0, (0, 1, 2), 0, 0)
    r_pass(3, 0, 0, 0, 1)
    rs_y(3, 0, (0, 1, 2), 0, 1)
    r_pass(3, 0, 0, 1, 1)
    r_pass(2, 1, 0, 0, 2)
    rs_done(1, 0, 1)
    rs_a(3, 0, (0, 1, 2), 1)
    r_pass(2, 1, 1, 0, 2)
    grad_b(2, False)
    r_pass(2, 1, 1, 1, 2)
    rs_y(3, 0, (0, 1, 2), 1, 0)
    r_pass(3, 0, 1, 0, 1)
    grad_sent(4)
    grad_a(0, False)
    rs_y(3, 0, (0, 1, 2), 1, 1)
    rs_y(2, 1, (6,), 0, 1)
    r_pass(3, 0, 0, 0, 2)
    r_pass(3, 0, 1, 1, 1)
    r_pass(3, 0, 0, 1, 2)
    g_in = rs_c(3, 0, 0)
    n_first, rstd = normed(tok[own_rows(0), :].astype(F32))
    vec[:, 0:256] = vec[:, 0:256] + packed(jnp.sum(g_in * n_first, axis=0, keepdims=True))
    g_tok = s.ghid[0:32, :] + norm_back(n_first, rstd, g_in * gain_row(0))
    s.ostage[0, 0:32, :] = g_tok.astype(BF)
    r_pass(2, 1, 0, 1, 1)
    r_pass(3, 0, 1, 0, 2)
    r_pass(3, 0, 1, 1, 2)
    s.ostage[1, 32:64, :] = (s.hidden[32:64, :] + rs_c(2, 1, 1)).astype(BF)
    for copy in out_copies(1, 1, res_o):
        copy.start()
    grad_b(1, False)
    r_pass(2, 1, 0, 1, 2)
    g_in = rs_c(3, 0, 1)
    n_first, rstd = normed(tok[own_rows(1), :].astype(F32))
    vec[:, 0:256] = vec[:, 0:256] + packed(jnp.sum(g_in * n_first, axis=0, keepdims=True))
    g_tok = s.ghid[32:64, :] + norm_back(n_first, rstd, g_in * gain_row(0))
    s.ostage[0, 32:64, :] = g_tok.astype(BF)
    grad_b(0, False)
    for copy in out_copies(0, 0, gtok_o):
        copy.start()
    def v_copy(j, dst, dev):
        return remote(vec, dst, s.v_s.at[j], s.v_r.at[j], dev)

    v_copy(0, s.vrc, cdev).start()
    for copy in out_copies(0, 1, gtok_o):
        copy.start()
    v_copy(0, s.vrc, cdev).wait()
    vec[...] = vec[...] + s.vrc[...]
    v_copy(1, s.vrx, xdev).start()
    v_copy(1, s.vrx, xdev).wait()
    vec[...] = vec[...] + s.vrx[...]
    v_copy(2, s.vry, ydev).start()
    v_copy(2, s.vry, ydev).wait()
    vec[:, 0:512] = vec[:, 0:512] + s.vry[:, 0:512]
    vz = s.vz
    vz[z] = vec[...]
    for i in peers:
        v_copy(2 + i, vz.at[z], zdev[i]).start()
    s.ostage[1, 0:32, :] = (s.hidden[0:32, :] + rs_c(2, 1, 0)).astype(BF)
    for copy in out_copies(1, 0, res_o):
        copy.start()
    for i in peers:
        there = vz.at[zdn[i]]
        remote(there, there, s.v_s.at[2 + i], s.v_r.at[2 + i], zdev[i]).wait_recv()
    for i in peers:
        v_copy(2 + i, vz.at[z], zdev[i]).wait_send()
    vec_o[:, 0:512] = ((vz[0, :, 0:512] + vz[1, :, 0:512]) + vz[2, :, 0:512]) + vz[3, :, 0:512]
    for zz in range(ZN):
        vec_o[:, 512 + 128 * zz : 640 + 128 * zz] = vz[zz, :, 512:VW]
    for j, dst in enumerate((gtok_o, res_o)):
        for g in range(2):
            there = dst.at[pl.ds(pl.multiple_of((1 - y) * HALF + g * HR, HR), HR)]
            a, b = out_copies(j, g, dst)
            a.wait_send()
            b.wait()
            remote(there, there, s.o_s.at[j, g], s.o_r.at[j, g], ydev).wait_recv()
    for n in range(4):
        grad_sent(n)
    for n in range(NCH):
        grad_done(n)
    loop(NCH, w_done)
    kv_copy(c).wait_send()
    dkv_copy.wait_send()
    for ia, (buf, own) in enumerate(((s.first, False), (s.cot, False), (s.second, True), (s.hlow, True))):
        ag_done(buf, ia, own)
    for g in range(2):
        rs_done(2, 1, g)
        rs_done(3, 0, g)


def finish_kernel(gwa, gwf, res, gtok, vec, o_res, o_tok, o_q, o_k, o_v, o_s, o_o, o_g, o_u, o_d, o_first, o_second, o_group):
    o_res[0] = res[...].astype(F32)
    o_tok[0] = gtok[...].astype(F32)
    for n, out in enumerate((o_g, o_u, o_d)):
        out[...] = gwf[n].astype(F32)
    both = jnp.swapaxes(gwa[0].astype(F32), 0, 1)
    o_q[...] = both[:, :, 0:256]
    o_k[...] = both[:, :, 256:512]
    for n, out in enumerate((o_v, o_s, o_o)):
        out[...] = jnp.swapaxes(gwa[n + 1].astype(F32), 0, 1)
    me = lax.axis_index("fsdp") * 8 + lax.axis_index("ctx")
    quarter = lax.rem(me, 4)

    def row(r, start, stop):
        block = vec[:, start:stop]
        return jnp.sum(jnp.where(lax.broadcasted_iota(jnp.int32, block.shape, 0) == r, block, 0.0), axis=0, keepdims=True)

    for out, start in ((o_first, 0), (o_second, 256)):
        pair = row(me // 2, start, start + 256)
        out[...] = jnp.where(lax.rem(me, 2) == 0, pair[:, 0:128], pair[:, 128:256])
    for zz in range(ZN):
        line = row(me // 4, 512 + 128 * zz, 640 + 128 * zz)
        total = jnp.zeros((1, 32), F32)
        for q in range(4):
            total = total + jnp.where(quarter == q, line[:, 32 * q : 32 * q + 32], 0.0)
        o_group[zz : zz + 1, :] = total


def finish(res, gtok, gwa, gwf, vec):
    steps = 2
    rows = BLK // steps
    flat = pl.BlockSpec((rows, D), lambda i: (i, 0))
    deep = pl.BlockSpec((1, rows, D), lambda i: (0, i, 0))
    narrow = pl.BlockSpec((rows, ZN, 256), lambda i: (i, 0, 0))
    wide = pl.BlockSpec((rows, ZN, CH), lambda i: (i, 0, 0))

    def whole(*shape):
        return pl.BlockSpec(shape, lambda i: (0,) * len(shape))

    def f32(*shape):
        return jax.ShapeDtypeStruct(shape, F32)

    outs = pl.pallas_call(
        finish_kernel,
        grid=(steps,),
        in_specs=[
            pl.BlockSpec((4, ZN, rows, CH), lambda i: (0, 0, i, 0)),
            pl.BlockSpec((3, rows, D), lambda i: (0, i, 0)),
            flat,
            flat,
            whole(8, 1024),
        ],
        out_specs=[deep, deep, narrow, narrow, wide, wide, wide, flat, flat, flat, whole(1, BLK), whole(1, BLK), whole(ZN, 32)],
        out_shape=[f32(1, BLK, D)] * 2
        + [f32(BLK, ZN, 256)] * 2
        + [f32(BLK, ZN, CH)] * 3
        + [f32(BLK, D)] * 3
        + [f32(1, BLK)] * 2
        + [f32(ZN, 32)],
        compiler_params=pltpu.CompilerParams(vmem_limit_bytes=VLIM),
    )(gwa, gwf, res, gtok, vec)
    return tuple(outs[:10]) + (outs[10].reshape(BLK), outs[11].reshape(BLK), outs[12])


def start_kernel(q, k, v, sw, o, g_first, g_second, g_group, rate, pk, gp, lr):
    for ref, at in ((q, 0), (k, 256), (v, 512), (sw, 1024), (o, 1536)):
        pk[:, :, at : at + ref.shape[2]] = jnp.swapaxes(ref[...], 0, 1)
    me = lax.axis_index("fsdp") * 8 + lax.axis_index("ctx")
    quarter = lax.rem(me, 4)
    gp[...] = jnp.zeros((8, BLK), F32)
    gp[0:1, :] = g_first[...].astype(F32)
    gp[1:2, :] = g_second[...].astype(F32)
    lane = lax.broadcasted_iota(jnp.int32, (ZN, BLK), 1) // 32
    wide = jnp.concatenate([g_group[...].astype(F32)] * 4, axis=1)
    gp[2:6, :] = jnp.where(lane == quarter, wide, 0.0)
    lr[...] = jnp.log(rate[...])


def begin(w_query, w_key, w_value, w_swish, w_output, gain_first, gain_second, gain_group, decay_rate):
    steps = 2
    rows = BLK // steps
    narrow = pl.BlockSpec((rows, ZN, 256), lambda i: (i, 0, 0))
    wide = pl.BlockSpec((rows, ZN, CH), lambda i: (i, 0, 0))

    def whole(*shape):
        return pl.BlockSpec(shape, lambda i: (0,) * len(shape))

    pk, gp, lr = pl.pallas_call(
        start_kernel,
        grid=(steps,),
        in_specs=[narrow, narrow, wide, wide, wide, whole(1, BLK), whole(1, BLK), whole(ZN, 32), whole(1, ZN)],
        out_specs=[pl.BlockSpec((ZN, rows, 4 * CH), lambda i: (0, i, 0)), whole(8, BLK), whole(1, ZN)],
        out_shape=[
            jax.ShapeDtypeStruct((ZN, BLK, 4 * CH), BF),
            jax.ShapeDtypeStruct((8, BLK), F32),
            jax.ShapeDtypeStruct((1, ZN), F32),
        ],
        compiler_params=pltpu.CompilerParams(vmem_limit_bytes=VLIM),
    )(w_query, w_key, w_value, w_swish, w_output, gain_first[None], gain_second[None], gain_group, decay_rate[None])
    return pk, gp, lr[0]


def fused(
    tokens, w_query, w_key, w_value, w_swish, w_output, w_gelu, w_up, w_down, gain_first, gain_second, gain_group, decay_rate, cotangent
):
    pk, gp, lr = begin(w_query, w_key, w_value, w_swish, w_output, gain_first, gain_second, gain_group, decay_rate)
    shapes = [
        jax.ShapeDtypeStruct((BLK, D), BF),
        jax.ShapeDtypeStruct((BLK, D), BF),
        jax.ShapeDtypeStruct((4, ZN, BLK, CH), BF),
        jax.ShapeDtypeStruct((3, BLK, D), BF),
        jax.ShapeDtypeStruct((8, 1024), F32),
    ]
    hbm = pl.BlockSpec(memory_space=pl.ANY)
    vmem = pl.BlockSpec(memory_space=pltpu.VMEM)
    smem = pl.BlockSpec(memory_space=pltpu.SMEM)
    scratch = [pltpu.VMEM(*v) for v in SCRATCH.values()]
    for shape in SEMS.values():
        scratch.append(pltpu.SemaphoreType.REGULAR((3,)) if shape is None else pltpu.SemaphoreType.DMA(shape))
    result, g_tok, gwa, gwf, vec = pl.pallas_call(
        kernel,
        out_shape=shapes,
        in_specs=[vmem, vmem, smem, hbm, hbm, hbm, hbm, hbm],
        out_specs=[hbm, hbm, hbm, hbm, vmem],
        scratch_shapes=scratch,
        compiler_params=pltpu.CompilerParams(collective_id=0, has_side_effects=True, vmem_limit_bytes=VLIM),
    )(tokens[0], gp, lr, cotangent[0], pk, w_gelu, w_up, w_down)
    return finish(result, g_tok, gwa, gwf, vec)


highest_precision = lax.Precision.HIGHEST


def prefix(part, axis, combine, identity):
    place = lax.axis_index(axis)
    gathered = jax.tree.map(lambda a: lax.all_gather(a, axis), part)
    state = jax.tree.map(lambda a, e: jnp.zeros_like(a) + jnp.asarray(e, a.dtype), part, identity)

    def one(turn, state):
        return combine(
            state, jax.tree.map(lambda a: lax.dynamic_index_in_dim(a, turn, 0, False), gathered)
        )

    return lax.fori_loop(0, place, one, state)


def entering_2(value, axis, combine, identity):
    devices, mine = (lax.axis_size(axis), lax.axis_index(axis))
    everything = jax.tree.map(
        lambda part, kind: lax.all_gather(part.astype(kind), axis),
        value,
        jax.tree.map(lambda a: jnp.bfloat16 if a.dtype == jnp.float32 else a.dtype, value),
    )
    start = jax.tree.map(
        lambda part, zero: jnp.broadcast_to(jnp.asarray(zero, part.dtype), part.shape),
        value,
        identity,
    )

    def turn(k, before):
        at = devices - 1 - k
        reached = at > mine
        new = combine(
            before, jax.tree.map(lambda part, own: part[at].astype(own.dtype), everything, value)
        )
        return jax.tree.map(lambda a, b: jnp.where(reached, a, b), new, before)

    return lax.fori_loop(0, devices, turn, start)


def norm_rows(values, gain):
    center = values - jnp.mean(values, axis=-1, keepdims=True)
    spread = jnp.mean(center * center, axis=-1, keepdims=True)
    return center * lax.rsqrt(spread + 1e-05) * gain


def entry_weights(length, log_rate):
    position = jnp.arange(length).astype(jnp.float32)
    return jnp.exp((position[:, None] + 1.0) * log_rate[None, :])


def exit_weights(length, log_rate):
    position = jnp.arange(length).astype(jnp.float32)
    return jnp.exp((length - 1.0 - position)[:, None] * log_rate[None, :])


def decay_matrix(length, log_rate):
    position = jnp.arange(length).astype(jnp.float32)
    distance = position[:, None] - position[None, :]
    causal = distance >= 0.0
    return jnp.where(
        causal[None], jnp.exp(jnp.where(causal, distance, 0.0)[None] * log_rate[:, None, None]), 0.0
    )


def retain_out(query_block, key_block_rows, value_block_rows, retention_state, log_rate):
    length = query_block.shape[1]
    scores = (
        jnp.einsum("sthk,sqhk->shtq", query_block, key_block_rows, precision=highest_precision)
        * decay_matrix(length, log_rate)[None]
    )
    within = jnp.einsum("shtq,sqhv->sthv", scores, value_block_rows, precision=highest_precision)
    carried_state = jnp.einsum(
        "sthk,shkv->sthv",
        query_block * entry_weights(length, log_rate)[None, :, :, None],
        retention_state,
        precision=highest_precision,
    )
    return within + carried_state


def retain_low(query_low, key_low, query_wide, value_wide, retention_state, log_rate):
    length = query_low.shape[1]
    raw_scores = jnp.einsum(
        "sthk,sqhk->shtq", query_low, key_low, preferred_element_type=jnp.float32
    )
    scores = raw_scores * decay_matrix(length, log_rate)[None]
    within = jnp.einsum("shtq,sqhv->sthv", scores, value_wide, precision=highest_precision)
    carried_state = jnp.einsum(
        "sthk,shkv->sthv",
        query_wide * entry_weights(length, log_rate)[None, :, :, None],
        retention_state,
        precision=highest_precision,
    )
    return within + carried_state


def own_states(key_block_rows, value_block_rows, log_rate):
    length = key_block_rows.shape[1]
    return jnp.einsum(
        "sthk,sthv->shkv",
        key_block_rows * exit_weights(length, log_rate)[None, :, :, None],
        value_block_rows,
        precision=highest_precision,
    )


def combine_states(earlier, later):
    return (earlier[0] * later[0], later[0][None, :, None, None] * earlier[1] + later[1])


def gate_section(retained, swish_in, gain):
    return norm_rows(retained, gain) * jax.nn.silu(swish_in)


def mlp_section(act_gelu, act_up):
    return jax.nn.gelu(act_gelu) * act_up


def general(
    tokens,
    w_query,
    w_key,
    w_value,
    w_swish,
    w_output,
    w_gelu,
    w_up,
    w_down,
    gain_first,
    gain_second,
    gain_group,
    decay_rate,
    cotangent,
):
    f32 = jnp.float32
    bf16 = jnp.bfloat16
    gathered = (
        lax.all_gather(w_query, ("fsdp", "ctx"), axis=0, tiled=True),
        lax.all_gather(w_key, ("fsdp", "ctx"), axis=0, tiled=True),
        lax.all_gather(w_value, ("fsdp", "ctx"), axis=0, tiled=True),
        lax.all_gather(w_swish, ("fsdp", "ctx"), axis=0, tiled=True),
        lax.all_gather(w_output, ("fsdp", "ctx"), axis=0, tiled=True),
        lax.all_gather(w_gelu, ("fsdp", "ctx"), axis=0, tiled=True),
        lax.all_gather(w_up, ("fsdp", "ctx"), axis=0, tiled=True),
        lax.all_gather(w_down, ("fsdp", "ctx"), axis=0, tiled=True),
        lax.all_gather(gain_first, ("fsdp", "ctx"), axis=0, tiled=True),
        lax.all_gather(gain_second, ("fsdp", "ctx"), axis=0, tiled=True),
        lax.all_gather(gain_group, ("fsdp", "ctx"), axis=1, tiled=True),
    )
    (
        full_query,
        full_key,
        full_value,
        full_swish,
        full_output,
        full_gelu,
        full_up,
        full_down,
        full_first,
        full_second,
        full_group,
    ) = gathered
    log_rate = jnp.log(decay_rate)
    piece = tokens.shape[1]
    key_scale = full_query.shape[2] ** (-0.5)
    factor = jnp.exp(piece * log_rate)
    inputs = tokens.astype(f32)
    first_gain = full_first.astype(f32)
    second_gain = full_second.astype(f32)
    group_gain = full_group.astype(f32)
    first_low = norm_rows(inputs, first_gain).astype(bf16)
    query_block = jnp.einsum(
        "spd,dhk->sphk", first_low, full_query, preferred_element_type=f32
    ).astype(bf16)
    key_block_rows = (
        jnp.einsum("spd,dhk->sphk", first_low, full_key, preferred_element_type=f32) * key_scale
    ).astype(bf16)
    value_block_rows = jnp.einsum(
        "spd,dhv->sphv", first_low, full_value, preferred_element_type=f32
    ).astype(bf16)
    swish_in = jnp.einsum("spd,dhv->sphv", first_low, full_swish, preferred_element_type=f32)
    query_wide = query_block.astype(f32)
    key_wide = key_block_rows.astype(f32)
    value_wide = value_block_rows.astype(f32)
    local_state = own_states(key_wide, value_wide, log_rate)
    identity = (jnp.ones_like(factor), jnp.zeros_like(local_state))
    _, entering = prefix((factor, local_state), "ctx", combine_states, identity)
    retained = retain_low(query_block, key_block_rows, query_wide, value_wide, entering, log_rate)
    gated = gate_section(retained, swish_in, group_gain).astype(bf16)
    attn_terms = jnp.einsum("sphv,dhv->spd", gated, full_output, preferred_element_type=f32)
    hidden = inputs + lax.psum(attn_terms, "tp")
    second_low = norm_rows(hidden, second_gain).astype(bf16)
    act_gelu = jnp.einsum("spd,df->spf", second_low, full_gelu, preferred_element_type=f32)
    act_up = jnp.einsum("spd,df->spf", second_low, full_up, preferred_element_type=f32)
    mixed = mlp_section(act_gelu, act_up).astype(bf16)
    mlp_terms = jnp.einsum("spf,df->spd", mixed, full_down, preferred_element_type=f32)
    result = hidden + lax.psum(mlp_terms.astype(jnp.bfloat16), "tp").astype(jnp.float32)
    back_query, back_key, back_value, back_swish, back_output, back_gelu, back_up, back_down = gathered[:8]
    grad_mixed = jnp.einsum("spd,df->spf", cotangent, back_down, preferred_element_type=f32)
    grad_down = jnp.einsum("spd,spf->df", cotangent, mixed, preferred_element_type=f32).astype(bf16)
    _, pull_mlp = jax.vjp(mlp_section, act_gelu, act_up)
    grad_act_gelu, grad_act_up = pull_mlp(grad_mixed)
    gelu_low = grad_act_gelu.astype(bf16)
    up_low = grad_act_up.astype(bf16)
    grad_gelu = jnp.einsum("spd,spf->df", second_low, gelu_low, preferred_element_type=f32).astype(bf16)
    grad_up = jnp.einsum("spd,spf->df", second_low, up_low, preferred_element_type=f32).astype(bf16)
    second_terms = jnp.einsum(
        "spf,df->spd", gelu_low, back_gelu, preferred_element_type=f32
    ) + jnp.einsum("spf,df->spd", up_low, back_up, preferred_element_type=f32)
    grad_second_in = lax.psum(second_terms, "tp")
    _, pull_second = jax.vjp(norm_rows, hidden, second_gain)
    hidden_from_norm, grad_second = pull_second(grad_second_in)
    grad_hidden = cotangent.astype(f32) + hidden_from_norm
    hidden_low = grad_hidden.astype(bf16)
    grad_gated = jnp.einsum("spd,dhv->sphv", hidden_low, back_output, preferred_element_type=f32)
    grad_output = jnp.einsum("spd,sphv->dhv", hidden_low, gated, preferred_element_type=f32).astype(bf16)
    _, pull_gate = jax.vjp(gate_section, retained, swish_in, group_gain)
    grad_retained, grad_swish_in, grad_group = pull_gate(grad_gated)
    swish_low = grad_swish_in.astype(bf16)
    entry_grad = jnp.einsum(
        "sthk,sthv->shkv",
        query_wide * entry_weights(piece, log_rate)[None, :, :, None],
        grad_retained,
        precision=highest_precision,
    )
    _, later_grad = entering_2((factor, entry_grad), "ctx", combine_states, identity)
    _, pull_retain = jax.vjp(
        lambda rows_q, rows_k, rows_v: (
            retain_out(rows_q, rows_k, rows_v, entering, log_rate),
            own_states(rows_k, rows_v, log_rate),
        ),
        query_wide,
        key_wide,
        value_wide,
    )
    grad_query_act, grad_key_act, grad_value_act = pull_retain((grad_retained, later_grad))
    query_low = grad_query_act.astype(bf16)
    key_low = (grad_key_act.astype(bf16).astype(f32) * key_scale).astype(bf16)
    value_low = grad_value_act.astype(bf16)
    grad_query = jnp.einsum("spd,sphk->dhk", first_low, query_low, preferred_element_type=f32).astype(bf16)
    grad_key = jnp.einsum("spd,sphk->dhk", first_low, key_low, preferred_element_type=f32).astype(bf16)
    grad_value = jnp.einsum("spd,sphv->dhv", first_low, value_low, preferred_element_type=f32).astype(bf16)
    grad_swish = jnp.einsum("spd,sphv->dhv", first_low, swish_low, preferred_element_type=f32).astype(bf16)
    first_terms = jnp.einsum("sphk,dhk->spd", query_low, back_query, preferred_element_type=f32)
    first_terms = first_terms + jnp.einsum(
        "sphk,dhk->spd", key_low, back_key, preferred_element_type=f32
    )
    first_terms = first_terms + jnp.einsum(
        "sphv,dhv->spd", value_low, back_value, preferred_element_type=f32
    )
    first_terms = first_terms + jnp.einsum(
        "sphv,dhv->spd", swish_low, back_swish, preferred_element_type=f32
    )
    grad_first_in = lax.psum(first_terms.astype(jnp.bfloat16), "tp").astype(jnp.float32)
    _, pull_first = jax.vjp(norm_rows, inputs, first_gain)
    tokens_from_norm, grad_first = pull_first(grad_first_in)
    grad_tokens = grad_hidden + tokens_from_norm
    owned = tuple(
        lax.psum_scatter(g, ("fsdp", "ctx"), scatter_dimension=0, tiled=True).astype(f32)
        for g in (grad_query, grad_key, grad_value, grad_swish, grad_output, grad_gelu, grad_up, grad_down, grad_first, grad_second)
    ) + (lax.psum_scatter(grad_group, ("fsdp", "ctx"), scatter_dimension=1, tiled=True),)
    return (
        result,
        grad_tokens,
        owned[0],
        owned[1],
        owned[2],
        owned[3],
        owned[4],
        owned[5],
        owned[6],
        owned[7],
        owned[8],
        owned[9],
        owned[10],
    )


def solution(mesh):
    wide, flat = P(("fsdp", "ctx"), "tp", None), P(("fsdp", "ctx"), "tp")
    tok, row, group = P("fsdp", "ctx", None), P(("fsdp", "ctx")), P("tp", ("fsdp", "ctx"))
    in_specs = (tok,) + (wide,) * 5 + (flat,) * 3 + (row, row, group, P("tp"), tok)
    out_specs = (tok, tok) + (wide,) * 5 + (flat,) * 3 + (row, row, group)
    sizes = (mesh.shape["fsdp"], mesh.shape["ctx"], mesh.shape["tp"])
    local = fused if sizes == (2, 2 * ZN, 2) else general
    return jax.shard_map(local, mesh=mesh, in_specs=in_specs, out_specs=out_specs, check_vma=False)
```

```python
import types

import jax
import jax.numpy as jnp
from jax import lax
from jax.experimental import pallas as pl
from jax.experimental.pallas import tpu as pltpu
from jax.sharding import PartitionSpec as P

MESH = pl.DeviceIdType.MESH
BF = jnp.bfloat16
F32 = jnp.float32

ZN = 4
BLK = 128
ROOT = 0.7978845608028654
HR = 32
HALF = 64
TOK = ZN * BLK
D = 2048
CH = 512
NCH = 7
NC = 2
RC = D // NC
RB = 16 // NC
AC = 4
AR = HALF // AC
SETS = 4
VW = 640
VLIM = 62 * 2**20


def nt(a, b):
    return lax.dot_general(a, b, (((1,), (1,)), ((), ())), preferred_element_type=F32)


def nn(a, b):
    return lax.dot_general(a, b, (((1,), (0,)), ((), ())), preferred_element_type=F32)


def normed(v):
    center = v - jnp.mean(v, axis=-1, keepdims=True)
    rstd = lax.rsqrt(jnp.mean(center * center, axis=-1, keepdims=True) + 1e-05)
    return center * rstd, rstd


def norm_back(n, rstd, g):
    return rstd * (
        g - jnp.mean(g, axis=-1, keepdims=True) - n * jnp.mean(g * n, axis=-1, keepdims=True)
    )


def remote(src, dst, ss, rs, dev):
    return pltpu.make_async_remote_copy(src, dst, ss, rs, device_id=dev, device_id_type=MESH)


SCRATCH = dict(
    gall=((16, 8, 128), F32),
    W=((NCH, 16, BLK, CH), BF),
    first=((ZN, BLK, D), BF),
    cot=((ZN, BLK, D), BF),
    second=((ZN, BLK, D), BF),
    hlow=((ZN, BLK, D), BF),
    XT=((16, BLK, TOK), BF),
    qkv=((2, TOK, 1024), BF),
    swish=((TOK, CH), F32),
    ret=((TOK, CH), F32),
    dr=((TOK, CH), BF),
    YB=((NCH, TOK, CH), BF),
    dkv_s=((TOK, 768), BF),
    dkv_r=((TOK, 768), BF),
    tmp=((5, TOK, 256), F32),
    ysend=((2, 2, NC, ZN, HR, RC), BF),
    yrecv=((2, 2, NC, ZN, HR, RC), BF),
    zsend=((2, 2, NC, ZN, HR, RC), BF),
    zrecv=((2, 2, NC, ZN + 1, HR, RC), BF),
    hidden=((HALF, D), F32),
    ghid=((HALF, D), F32),
    rsum=((HALF, D), F32),
    ostage=((2, HALF, D), BF),
    gcs=((2, ZN, BLK, CH), BF),
    gcr=((SETS, 2, ZN, BLK, CH), BF),
    gxs=((SETS, ZN, BLK, CH), BF),
    gxr=((SETS, ZN, BLK, CH), BF),
    gzs=((SETS, ZN, BLK, CH), BF),
    vec=((8, VW), F32),
    vrc=((8, VW), F32),
    vrx=((8, VW), F32),
    vry=((8, VW), F32),
    vz=((ZN, 8, VW), F32),
)
SEMS = dict(
    g_s=(3, 8), g_r=(3, 8),
    wz_s=(NCH, 3), wz_r=(NCH, 3), wx_s=(NCH, 4), wx_r=(NCH, 4), wc_s=(NCH, 8), wc_r=(NCH, 8), wl=(NCH,),
    az_s=(4, AC, 2, ZN), az_r=(4, AC, ZN), ay_s=(4, AC, ZN), ay_r=(4, AC, ZN),
    ry_s=(4, 2, NC), ry_r=(4, 2, NC), rz_s=(4, 2, NC, ZN), rz_r=(4, 2, NC, ZN + 1),
    kv_s=(2,), kv_r=(2,),
    gc_s=(NCH, 2), gc_r=(NCH, 2), gx_s=(NCH,), gx_r=(NCH,), gz_s=(NCH, 3), gz_r=(NCH, 3), gl=(NCH,),
    v_s=(6,), v_r=(6,), o_s=(2, 2), o_r=(2, 2), ol=(1,), oo=(2, 2),
    credit=None,
)
NAMES = list(SCRATCH) + list(SEMS)


def kernel(tok, gp, lr, cot_in, pk, wg, wu, wd, res_o, gtok_o, gwa_o, gwf_o, vec_o, *scratch):
    s = types.SimpleNamespace(**dict(zip(NAMES, scratch)))
    W, YB, XT = s.W, s.YB, s.XT
    x, k, y = lax.axis_index("fsdp"), lax.axis_index("ctx"), lax.axis_index("tp")
    z, c = k // 2, k % 2
    zup = [lax.rem(z + i, ZN) for i in range(ZN)]
    zdn = [lax.rem(z + ZN - i, ZN) for i in range(ZN)]
    zdev = [(x, zup[i] * 2 + c, y) for i in range(ZN)]
    updev, dndev = zdev[1], zdev[ZN - 1]
    xdev, ydev, cdev = (1 - x, k, y), (x, k, 1 - y), (x, z * 2 + 1 - c, y)
    peers = range(1, ZN)

    def place(xx, zz, cc):
        return xx * 8 + zz * 2 + cc

    me = place(x, z, c)
    log_rate = lr[z]

    def loop(n, f):
        def step(i, carry):
            f(i)
            return carry

        lax.fori_loop(0, n, step, 0)

    barrier = pltpu.get_barrier_semaphore()
    for dev in zdev[1:] + [xdev, ydev, cdev]:
        pl.semaphore_signal(barrier, inc=1, device_id=dev, device_id_type=MESH)
    pl.semaphore_wait(barrier, 6)

    def w_src(n, zz):
        if n < 4:
            return pk.at[zz, :, pl.ds(n * CH, CH)]
        return (wg, wu, wd)[n - 4].at[:, pl.ds(pl.multiple_of(zz * CH, CH), CH)]

    def w_local(n, zz):
        return pltpu.make_async_copy(w_src(n, zz), W.at[n, me], s.wl.at[n])

    def w_piece(n, i):
        remote(w_src(n, zup[i]), W.at[n, me], s.wz_s.at[n, i - 1], s.wz_r.at[n, i - 1], zdev[i]).start()

    def w_send(n):
        for i in peers:
            w_piece(n, i)

    def w_z(n, i):
        blk = W.at[n, place(x, zdn[i], c)]
        return remote(blk, blk, s.wz_s.at[n, i - 1], s.wz_r.at[n, i - 1], zdev[i])

    def w_x(n, j, xx):
        blk = W.at[n, place(xx, zdn[j], c)]
        return remote(blk, blk, s.wx_s.at[n, j], s.wx_r.at[n, j], xdev)

    def w_c(n, j, cc):
        xx = x if j < 4 else 1 - x
        blk = W.at[n, place(xx, zdn[j % 4], cc)]
        return remote(blk, blk, s.wc_s.at[n, j], s.wc_r.at[n, j], cdev)

    def w_own(n):
        pltpu.make_async_copy(W.at[n, me], W.at[n, me], s.wl.at[n]).wait()
        w_x(n, 0, x).start()
        w_c(n, 0, c).start()

    def pump_z(n, i):
        w_z(n, i).wait_recv()
        w_x(n, i, x).start()
        w_c(n, i, c).start()

    def pump_x(n, j):
        w_x(n, j, 1 - x).wait_recv()
        w_c(n, ZN + j, c).start()

    def w_fin(n):
        for j in range(8):
            w_c(n, j, 1 - c).wait_recv()

    def w_done(n):
        for i in peers:
            w_z(n, i).wait_send()
        for j in range(ZN):
            w_x(n, j, x).wait_send()
        for j in range(8):
            w_c(n, j, c).wait_send()

    def a_rows(yy, ch):
        return pl.ds(pl.multiple_of(yy * HALF + ch * AR, AR), AR)

    def a_z(buf, ia, ch, zz, way):
        blk = buf.at[zz, a_rows(y, ch)]
        return remote(blk, blk, s.az_s.at[ia, ch, way, zz], s.az_r.at[ia, ch, zz], (updev, dndev)[way])

    def a_y(buf, ia, ch, zz, yy):
        blk = buf.at[zz, a_rows(yy, ch)]
        return remote(blk, blk, s.ay_s.at[ia, ch, zz], s.ay_r.at[ia, ch, zz], ydev)

    def ag_sends(buf, ia, ch, zz, do):
        pl.when((zz <= z) & (z < ZN - 1))(lambda: do(a_z(buf, ia, ch, zz, 0)))
        pl.when((zz >= z) & (z > 0))(lambda: do(a_z(buf, ia, ch, zz, 1)))

    def ag_send(buf, ia, own, part):
        def f(at):
            ch = at + part * (AC // 2)
            ag_sends(buf, ia, ch, z, lambda copy: copy.start())
            if own:
                a_y(buf, ia, ch, z, y).start()

        loop(AC // 2, f)

    def ag_forward(buf, ia, d, part):
        def f(at):
            ch = at + part * (AC // 2)

            def pass_on(zz):
                a_z(buf, ia, ch, zz, 0).wait_recv()
                ag_sends(buf, ia, ch, zz, lambda copy: copy.start())
                a_y(buf, ia, ch, zz, y).start()

            pl.when(z >= d)(lambda: pass_on(z - d))
            pl.when(z + d < ZN)(lambda: pass_on(z + d))

        loop(AC // 2, f)

    def ag_wait(buf, ia, own, part):
        def f(at):
            ch = at + part * (AC // 2)
            for i in range(0 if own else 1, ZN):
                a_y(buf, ia, ch, zdn[i], 1 - y).wait_recv()

        loop(AC // 2, f)

    def ag_done(buf, ia, own):
        def f(ch):
            for i in range(ZN):
                ag_sends(buf, ia, ch, zdn[i], lambda copy: copy.wait_send())
                if own or i > 0:
                    a_y(buf, ia, ch, zdn[i], y).wait_send()

        loop(AC, f)

    def group_rows(buf, g):
        return jnp.concatenate([buf[zz, yy * HALF + g * HR : yy * HALF + g * HR + HR, :] for zz in range(ZN) for yy in range(2)], axis=0)

    def product(chunks, j, yy, g):
        total = None
        for n in chunks:
            rows = []
            for zz in range(ZN):
                at = (g * ZN + zz) * HALF + yy * HR if n > 3 else zz * BLK + yy * HALF + g * HR
                rows.append(YB[n, pl.ds(pl.multiple_of(at, HR), HR), :])
            lhs = jnp.concatenate(rows, axis=0)
            rhs = W[n, pl.ds(j * RB, RB)].reshape(RC, CH)
            part = nt(lhs, rhs)
            total = part if total is None else total + part
        return total.reshape(ZN, HR, RC)

    def r_y(ir, b, g, j):
        return remote(s.ysend.at[b, g, j], s.yrecv.at[b, g, j], s.ry_s.at[ir, g, j], s.ry_r.at[ir, g, j], ydev)

    def r_z(ir, b, g, j, d, way):
        slot = d if way == 0 else jnp.where(d == z - 1, ZN, d)
        return remote(
            s.zsend.at[b, g, j, d],
            s.zrecv.at[b, g, j, slot],
            s.rz_s.at[ir, g, j, d],
            s.rz_r.at[ir, g, j, slot],
            (updev, dndev)[way],
        )

    def r_arrived(ir, b, g, j, slot):
        there = s.zrecv.at[b, g, j, slot]
        remote(there, there, s.rz_s.at[ir, g, j, 0], s.rz_r.at[ir, g, j, slot], updev).wait_recv()

    def rs_a(ir, b, chunks, g):
        def f(j):
            s.ysend[b, g, j] = product(chunks, j, 1 - y, g).astype(BF)
            r_y(ir, b, g, j).start()

        loop(NC, f)

    def r_pass(ir, b, g, j, level):
        def go(dests, way):
            for d in dests:
                if level > 0:
                    r_arrived(ir, b, g, j, d)
                    s.zsend[b, g, j, d] = (s.zsend[b, g, j, d].astype(F32) + s.zrecv[b, g, j, d].astype(F32)).astype(BF)
                r_z(ir, b, g, j, d, way).start()

        pl.when(z == level)(lambda: go(range(ZN - 1, level, -1), 0))
        pl.when(z == ZN - 1 - level)(lambda: go(range(ZN - 1 - level), 1))

    def rs_y(ir, b, chunks, g, j):
        own = product(chunks, j, y, g)
        r_y(ir, b, g, j).wait_recv()
        s.zsend[b, g, j] = (own + s.yrecv[b, g, j].astype(F32)).astype(BF)
        r_pass(ir, b, g, j, 0)

    def rs_c(ir, b, g):
        mine = pl.ds(g * HR, HR)

        def f(j):
            cols = pl.ds(pl.multiple_of(j * RC, RC), RC)
            s.rsum[mine, cols] = s.zsend[b, g, j, z].astype(F32)

            def add(slot):
                r_arrived(ir, b, g, j, slot)
                s.rsum[mine, cols] = s.rsum[mine, cols] + s.zrecv[b, g, j, slot].astype(F32)

            pl.when(z > 0)(lambda: add(z))
            pl.when(z < ZN - 1)(lambda: add(ZN))

        loop(NC, f)
        return s.rsum[mine, :]

    def rs_done(ir, b, g):
        def f(j):
            r_y(ir, b, g, j).wait_send()
            for i in peers:
                r_z(ir, b, g, j, zdn[i], 0).wait_send()

        loop(NC, f)

    def transpose(buf, grouped):
        def f(q):
            cols = pl.ds(pl.multiple_of(q * BLK, BLK), BLK)
            if grouped:
                parts = []
                for g in range(2):
                    for zz in range(ZN):
                        for yy in range(2):
                            parts.append(buf[zz, yy * HALF + g * HR : yy * HALF + g * HR + HR, cols])
                XT[q] = jnp.concatenate(parts, axis=0).T
            else:
                XT[q] = buf[:, :, cols].reshape(TOK, BLK).T

        loop(16, f)

    def grad_rows(n, xx, cc):
        lhs = jnp.concatenate([XT[place(xx, zz, cc)] for zz in range(ZN)], axis=0)
        return nn(lhs, YB[n]).reshape(ZN, BLK, CH)

    def g_c(n, xx):
        return remote(s.gcs.at[xx], s.gcr.at[n % SETS, xx], s.gc_s.at[n, xx], s.gc_r.at[n, xx], cdev)

    def g_x(n):
        return remote(s.gxs.at[n % SETS], s.gxr.at[n % SETS], s.gx_s.at[n], s.gx_r.at[n], xdev)

    def g_dst(n):
        if n < 4:
            return gwa_o.at[n, z]
        return gwf_o.at[n - 4, :, pl.ds(pl.multiple_of(z * CH, CH), CH)]

    def g_z(n, i):
        return remote(s.gzs.at[n % SETS, zup[i]], g_dst(n), s.gz_s.at[n, i - 1], s.gz_r.at[n, i - 1], zdev[i])

    def g_local(n):
        return pltpu.make_async_copy(s.gzs.at[n % SETS, z], g_dst(n), s.gl.at[n])

    def grad_a(n, first_use):
        b = n % SETS

        def f(t):
            xx = (1 - x) * (1 - t) + x * t
            s.gcs[xx] = grad_rows(n, xx, 1 - c).astype(BF)
            g_c(n, xx).start()

        loop(2, f)
        own = grad_rows(n, 1 - x, c)
        g_c(n, 1 - x).wait_recv()
        if not first_use:
            pl.semaphore_wait(s.credit.at[b], 1)
        s.gxs[b] = (own + s.gcr[b, 1 - x].astype(F32)).astype(BF)
        g_x(n).start()
        own = grad_rows(n, x, c)
        g_c(n, x).wait_recv()
        s.gzs[b] = (own + s.gcr[b, x].astype(F32)).astype(BF)
        for xx in range(2):
            g_c(n, xx).wait_send()

    def grad_b(n, more):
        b = n % SETS
        g_x(n).wait_recv()
        s.gzs[b] = (s.gzs[b].astype(F32) + s.gxr[b].astype(F32)).astype(BF)
        for i in peers:
            g_z(n, i).start()
        g_local(n).start()
        g_x(n).wait_send()
        if more:
            pl.semaphore_signal(s.credit.at[b], inc=1, device_id=xdev, device_id_type=MESH)

    def grad_sent(n):
        for i in peers:
            g_z(n, i).wait_send()
        g_local(n).wait()

    def grad_done(n):
        for i in peers:
            g_z(n, i).wait_recv()

    def gain_row(r):
        return jnp.concatenate([s.gall[q, r : r + 1, :] for q in range(16)], axis=1)

    def group_gain():
        pick = lax.broadcasted_iota(jnp.int32, (8, 128), 0) == 2 + z
        parts = []
        for r in range(4):
            total = s.gall[4 * r]
            for q in range(4 * r + 1, 4 * r + 4):
                total = total + s.gall[q]
            parts.append(jnp.sum(jnp.where(pick, total, 0.0), axis=0, keepdims=True))
        return jnp.concatenate(parts, axis=1)

    def packed(row):
        return jnp.concatenate([row[:, 256 * q : 256 * q + 256] for q in range(D // 256)], axis=0)

    def position(shape, dim, both, start):
        r = lax.broadcasted_iota(jnp.int32, shape, dim) + start
        if both:
            core, r = r // TOK, lax.rem(r, TOK)
        else:
            core = c
        return r + (r // BLK) * BLK + core * BLK

    def decay(later, earlier):
        gap = later - earlier
        keep = gap >= 0
        return jnp.where(keep, jnp.exp(jnp.where(keep, gap, 0).astype(F32) * log_rate), 0.0)

    def own_rows(g):
        return pl.ds(pl.multiple_of(y * HALF + g * HR, HR), HR)

    gall = s.gall
    gall[me] = gp[...]

    def g_gain(j, i, dev, q):
        return remote(gall.at[q], gall.at[q], s.g_s.at[j, i], s.g_r.at[j, i], dev)

    for i in peers:
        g_gain(0, i, zdev[i], me).start()
    w_send(0)
    for n in range(NCH):
        w_local(n, z).start()
    cot_local = pltpu.make_async_copy(cot_in, s.cot.at[z], s.ol.at[0])
    cot_local.start()
    s.rsum[...], _ = normed(tok[pl.ds(pl.multiple_of(y * HALF, HALF), HALF), :].astype(F32))
    s.ghid[...], _ = normed(tok[pl.ds(pl.multiple_of((1 - y) * HALF, HALF), HALF), :].astype(F32))
    for i in peers:
        g_gain(0, i, zdev[i], place(x, zdn[i], c)).wait_recv()
    for i in range(ZN):
        g_gain(1, i, xdev, place(x, zdn[i], c)).start()
    for i in range(ZN):
        g_gain(2, i, cdev, place(x, zdn[i], c)).start()
    for i in range(ZN):
        g_gain(1, i, xdev, place(1 - x, zdn[i], c)).wait_recv()
        g_gain(2, ZN + i, cdev, place(1 - x, zdn[i], c)).start()
    for i in range(8):
        xx = x if i < ZN else 1 - x
        g_gain(2, i, cdev, place(xx, zdn[i % ZN], 1 - c)).wait_recv()
    for i in peers:
        g_gain(0, i, zdev[i], me).wait_send()
    for i in range(ZN):
        g_gain(1, i, xdev, place(x, zdn[i], c)).wait_send()
    for i in range(8):
        xx = x if i < ZN else 1 - x
        g_gain(2, i, cdev, place(xx, zdn[i % ZN], c)).wait_send()
    vec = s.vec
    vec[...] = jnp.zeros((8, VW), F32)
    tmp, qkv, swish = s.tmp, s.qkv, s.swish

    def columns(n, t):
        return W[n, :, :, pl.ds(pl.multiple_of(t * 256, 256), 256)].reshape(D, 256)

    def all_keys():
        return qkv[:, :, 256:512].reshape(2 * TOK, 256)

    def all_values():
        return qkv[:, :, 512:1024].reshape(2 * TOK, CH)

    def out_copies(j, g, dst):
        here, there = s.ostage.at[j, pl.ds(g * HR, HR)], dst.at[own_rows(g)]
        return (
            remote(here, there, s.o_s.at[j, g], s.o_r.at[j, g], ydev),
            pltpu.make_async_copy(here, there, s.oo.at[j, g]),
        )

    w_own(4)
    gain_1 = gain_row(0)
    s.first[z, pl.ds(pl.multiple_of(y * HALF, HALF), HALF), :] = (s.rsum[...] * gain_1).astype(BF)
    for part in range(2):
        ag_send(s.first, 0, False, part)
    s.first[z, pl.ds(pl.multiple_of((1 - y) * HALF, HALF), HALF), :] = (s.ghid[...] * gain_1).astype(BF)
    w_own(1)
    w_own(6)
    w_own(5)
    w_own(2)
    pump_z(0, 1)
    ag_forward(s.first, 0, 1, 0)
    w_send(1)
    w_own(0)
    ag_forward(s.first, 0, 1, 1)
    ag_forward(s.first, 0, 2, 0)
    pump_z(1, 1)
    pump_z(0, 2)
    pump_x(0, 0)
    pump_x(0, 1)
    w_send(2)
    pump_z(0, 3)
    ag_forward(s.first, 0, 2, 1)
    pump_x(0, 2)
    pump_x(0, 3)
    w_own(3)
    ag_forward(s.first, 0, 3, 0)
    w_send(3)
    pump_z(2, 1)
    pump_z(2, 2)
    pump_x(1, 0)
    pump_x(1, 1)
    pump_x(2, 0)
    pump_x(2, 1)
    pump_z(1, 2)
    pump_z(1, 3)
    cot_local.wait()
    for part in range(2):
        ag_send(s.cot, 1, False, part)
    ag_forward(s.first, 0, 3, 1)
    pump_z(2, 3)
    pump_z(3, 1)
    pump_z(3, 2)
    pump_x(1, 2)
    pump_x(1, 3)
    w_send(6)
    ag_forward(s.cot, 1, 1, 0)
    for part in range(2):
        ag_wait(s.first, 0, False, part)
    pump_x(2, 2)
    pump_x(2, 3)
    w_fin(0)

    def project_qk(t):
        scale = jnp.where(t == 1, 0.0625, 1.0)
        out = nn(s.first[...].reshape(TOK, D), columns(0, t)) * scale
        qkv[c, :, pl.ds(pl.multiple_of(t * 256, 256), 256)] = out.astype(BF)

    loop(2, project_qk)
    w_fin(1)

    def project_v(t):
        out = nn(s.first[...].reshape(TOK, D), columns(1, t))
        qkv[c, :, pl.ds(pl.multiple_of(512 + t * 256, 256), 256)] = out.astype(BF)

    loop(2, project_v)

    def kv_copy(cc):
        blk = qkv.at[cc, :, pl.ds(256, 768)]
        return remote(blk, blk, s.kv_s.at[0], s.kv_r.at[0], cdev)

    kv_copy(c).start()
    w_fin(2)

    def project_s(t):
        out = nn(s.first[...].reshape(TOK, D), columns(2, t))
        swish[:, pl.ds(pl.multiple_of(t * 256, 256), 256)] = out

    loop(2, project_s)
    pump_z(3, 3)
    kv_copy(1 - c).wait_recv()

    def retain(h):
        rows = pl.ds(pl.multiple_of(h * 256, 256), 256)
        later = position((256, 2 * TOK), 0, False, h * 256)
        earlier = position((256, 2 * TOK), 1, True, 0)
        scores = nt(qkv[c, rows, 0:256], all_keys()) * decay(later, earlier)
        s.ret[rows, :] = nn(scores.astype(BF), all_values())

    loop(2, retain)
    ag_forward(s.cot, 1, 1, 1)
    w_send(4)
    pump_x(3, 0)
    pump_x(3, 1)
    pump_x(3, 2)
    pump_x(3, 3)
    w_send(5)
    gain_g = group_gain()

    def gate(h):
        rows = pl.ds(pl.multiple_of(h * BLK, BLK), BLK)
        n, _ = normed(s.ret[rows, :])
        w = swish[rows, :]
        YB[3, rows, :] = (n * gain_g * (w / (1.0 + jnp.exp(-w)))).astype(BF)

    loop(ZN, gate)
    pump_z(6, 1)
    w_fin(3)
    rs_a(0, 0, (3,), 0)
    rs_a(0, 0, (3,), 1)
    ag_forward(s.cot, 1, 2, 0)
    pump_z(6, 2)
    pump_z(6, 3)
    pump_x(6, 0)
    pump_x(6, 1)
    rs_y(0, 0, (3,), 0, 0)
    ag_forward(s.cot, 1, 2, 1)
    rs_y(0, 0, (3,), 0, 1)
    r_pass(0, 0, 0, 0, 1)
    r_pass(0, 0, 0, 1, 1)
    pump_z(4, 1)
    pump_z(4, 2)
    rs_y(0, 0, (3,), 1, 0)
    rs_y(0, 0, (3,), 1, 1)
    ag_forward(s.cot, 1, 3, 0)
    r_pass(0, 0, 1, 0, 1)
    pump_z(4, 3)
    ag_forward(s.cot, 1, 3, 1)
    r_pass(0, 0, 0, 0, 2)
    r_pass(0, 0, 0, 1, 2)
    r_pass(0, 0, 1, 1, 1)
    pump_z(5, 1)
    hidden = tok[own_rows(0), :].astype(F32) + rs_c(0, 0, 0)
    s.hidden[0:32, :] = hidden
    n_second, _ = normed(hidden)
    s.second[z, own_rows(0), :] = (n_second * gain_row(1)).astype(BF)
    ag_send(s.second, 2, True, 0)
    pump_z(5, 2)
    r_pass(0, 0, 1, 0, 2)
    pump_z(5, 3)
    r_pass(0, 0, 1, 1, 2)
    pump_x(5, 0)
    pump_x(5, 1)
    pump_x(4, 0)
    pump_x(4, 1)
    pump_x(4, 2)
    pump_x(4, 3)
    for part in range(2):
        ag_wait(s.cot, 1, False, part)
    ag_forward(s.second, 2, 1, 0)
    hidden = tok[own_rows(1), :].astype(F32) + rs_c(0, 0, 1)
    s.hidden[32:64, :] = hidden
    n_second, _ = normed(hidden)
    s.second[z, own_rows(1), :] = (n_second * gain_row(1)).astype(BF)
    ag_send(s.second, 2, True, 1)
    ag_forward(s.second, 2, 2, 0)
    ag_forward(s.second, 2, 1, 1)
    ag_forward(s.second, 2, 3, 0)
    pump_x(5, 2)
    pump_x(5, 3)
    pump_x(6, 2)
    pump_x(6, 3)
    w_fin(4)
    w_fin(5)

    def feed(g):
        rows_g = pl.ds(g * 256, 256)

        def tile(t):
            sec = group_rows(s.second, g)
            cols = pl.ds(pl.multiple_of(t * 256, 256), 256)
            tmp[2 * t, rows_g, :] = nn(sec, columns(4, t))
            tmp[2 * t + 1, rows_g, :] = nn(sec, columns(5, t))

            def act(h):
                rows = pl.ds(pl.multiple_of(g * 256 + h * HALF, HALF), HALF)
                a, u = tmp[2 * t, rows, :], tmp[2 * t + 1, rows, :]
                th = jnp.tanh(ROOT * (a + 0.044715 * (a * a * a)))
                half = 0.5 * (1.0 + th)
                gelu = a * half
                slope = half + 0.5 * a * (1.0 - th * th) * (ROOT * (1.0 + 0.134145 * (a * a)))
                YB[6, rows, cols] = (gelu * u).astype(BF)
                tmp[2 * t, rows, :] = u * slope
                tmp[2 * t + 1, rows, :] = gelu

            loop(4, act)

        loop(2, tile)

    ag_forward(s.second, 2, 2, 1)
    w_fin(6)

    def feed_back(g):
        rows_g = pl.ds(g * 256, 256)

        def tile(t):
            cols = pl.ds(pl.multiple_of(t * 256, 256), 256)
            tmp[4, rows_g, :] = nn(group_rows(s.cot, g), columns(6, t))

            def act(h):
                rows = pl.ds(pl.multiple_of(g * 256 + h * HALF, HALF), HALF)
                gm = tmp[4, rows, :]
                YB[4, rows, cols] = (gm * tmp[2 * t, rows, :]).astype(BF)
                YB[5, rows, cols] = (gm * tmp[2 * t + 1, rows, :]).astype(BF)

            loop(4, act)

        loop(2, tile)

    ag_wait(s.second, 2, True, 0)
    ag_forward(s.second, 2, 3, 1)
    feed(0)
    feed_back(0)
    rs_done(0, 0, 0)
    rs_a(1, 0, (4, 5), 0)
    ag_wait(s.second, 2, True, 1)
    feed(1)
    transpose(s.second, True)
    feed_back(1)
    grad_a(4, True)
    rs_y(1, 0, (4, 5), 0, 0)
    rs_done(0, 0, 1)
    rs_a(1, 0, (4, 5), 1)
    rs_y(1, 0, (4, 5), 0, 1)
    r_pass(1, 0, 0, 0, 1)
    rs_a(2, 1, (6,), 1)
    grad_a(5, True)
    r_pass(1, 0, 0, 0, 2)
    rs_y(1, 0, (4, 5), 1, 0)
    r_pass(1, 0, 0, 1, 1)
    r_pass(1, 0, 0, 1, 2)
    r_pass(1, 0, 1, 0, 1)
    rs_y(1, 0, (4, 5), 1, 1)
    g_in = rs_c(1, 0, 0)
    n_second, rstd = normed(s.hidden[0:32, :])
    vec[:, 256:512] = vec[:, 256:512] + packed(jnp.sum(g_in * n_second, axis=0, keepdims=True))
    ghid = s.cot[z, own_rows(0), :].astype(F32) + norm_back(n_second, rstd, g_in * gain_row(1))
    s.ghid[0:32, :] = ghid
    s.hlow[z, own_rows(0), :] = ghid.astype(BF)
    ag_send(s.hlow, 3, True, 0)
    transpose(s.cot, True)
    r_pass(1, 0, 1, 0, 2)
    r_pass(1, 0, 1, 1, 1)
    rs_y(2, 1, (6,), 1, 0)
    r_pass(1, 0, 1, 1, 2)
    ag_forward(s.hlow, 3, 1, 0)
    g_in = rs_c(1, 0, 1)
    n_second, rstd = normed(s.hidden[32:64, :])
    vec[:, 256:512] = vec[:, 256:512] + packed(jnp.sum(g_in * n_second, axis=0, keepdims=True))
    ghid = s.cot[z, own_rows(1), :].astype(F32) + norm_back(n_second, rstd, g_in * gain_row(1))
    s.ghid[32:64, :] = ghid
    s.hlow[z, own_rows(1), :] = ghid.astype(BF)
    ag_send(s.hlow, 3, True, 1)
    r_pass(2, 1, 1, 0, 1)
    rs_y(2, 1, (6,), 1, 1)
    grad_a(6, True)
    ag_forward(s.hlow, 3, 2, 0)
    ag_forward(s.hlow, 3, 1, 1)
    r_pass(2, 1, 1, 1, 1)
    ag_forward(s.hlow, 3, 2, 1)
    grad_b(5, True)
    ag_forward(s.hlow, 3, 3, 0)
    grad_b(6, True)
    ag_forward(s.hlow, 3, 3, 1)
    ag_wait(s.hlow, 3, True, 0)
    rs_a(2, 1, (6,), 0)
    def back_gated(g):
        def tile(t):
            out = nn(group_rows(s.hlow, g), columns(3, t))
            for q in range(8):
                tmp[t, q * HALF + g * HR : q * HALF + g * HR + HR, :] = out[q * HR : q * HR + HR]

        loop(2, tile)

        def back_gate(h, total):
            rows = pl.ds(pl.multiple_of(h * HALF + g * HR, HR), HR)
            n, rstd = normed(s.ret[rows, :])
            w, g_out = swish[rows, :], jnp.concatenate([tmp[0, rows, :], tmp[1, rows, :]], axis=1)
            sig = 1.0 / (1.0 + jnp.exp(-w))
            silu = w * sig
            YB[2, rows, :] = (g_out * (n * gain_g) * (sig * (1.0 + w * (1.0 - sig)))).astype(BF)
            gs = g_out * silu
            s.dr[rows, :] = norm_back(n, rstd, gs * gain_g).astype(BF)
            return total + jnp.sum(gs * n, axis=0, keepdims=True)

        group = lax.fori_loop(0, 8, back_gate, jnp.zeros((1, CH), F32))
        vec[0:4, 512:VW] = vec[0:4, 512:VW] + jnp.concatenate([group[:, 128 * q : 128 * q + 128] for q in range(4)], axis=0)

    back_gated(0)
    grad_b(4, True)
    ag_wait(s.hlow, 3, True, 1)
    transpose(s.hlow, False)
    grad_a(3, True)
    rs_y(2, 1, (6,), 0, 0)
    back_gated(1)
    transpose(s.first, False)
    def back_keys(core, h):
        rows = pl.ds(pl.multiple_of(h * 256, 256), 256)
        keys, values = qkv[core, rows, 256:512], qkv[core, rows, 512:1024]
        query = qkv[c, :, 0:256]
        r = lax.broadcasted_iota(jnp.int32, (256, TOK), 0) + h * 256
        earlier = r + (r // BLK) * BLK + core * BLK
        table = decay(position((256, TOK), 1, False, 0), earlier)
        weights = (nt(keys, query) * table).astype(BF)
        slopes = (nt(values, s.dr[...]) * table).astype(BF)
        return rows, nn(slopes, query), nn(weights, s.dr[...])

    def back_other(h):
        rows, dk, dv = back_keys(1 - c, h)
        s.dkv_s[rows, 0:256] = dk.astype(BF)
        s.dkv_s[rows, 256:768] = dv.astype(BF)

    def back_own(h):
        rows, dk, dv = back_keys(c, h)
        tmp[0, rows, :] = dk
        tmp[1, rows, :] = dv[:, 0:256]
        tmp[2, rows, :] = dv[:, 256:512]

    loop(2, back_other)
    dkv_copy = remote(s.dkv_s, s.dkv_r, s.kv_s.at[1], s.kv_r.at[1], cdev)
    dkv_copy.start()
    loop(2, back_own)

    r_pass(2, 1, 0, 0, 1)
    def back_query(h):
        rows = pl.ds(pl.multiple_of(h * 256, 256), 256)
        later = position((256, 2 * TOK), 0, False, h * 256)
        earlier = position((256, 2 * TOK), 1, True, 0)
        slopes = nt(s.dr[rows, :], all_values()) * decay(later, earlier)
        YB[0, rows, 0:256] = nn(slopes.astype(BF), all_keys()).astype(BF)

    loop(2, back_query)
    dkv_copy.wait_recv()

    def back_sum(h):
        rows = pl.ds(pl.multiple_of(h * BLK, BLK), BLK)
        other = s.dkv_r[rows, :].astype(F32)
        YB[0, rows, 256:512] = ((tmp[0, rows, :] + other[:, 0:256]) * 0.0625).astype(BF)
        YB[1, rows, 0:256] = (tmp[1, rows, :] + other[:, 256:512]).astype(BF)
        YB[1, rows, 256:512] = (tmp[2, rows, :] + other[:, 512:768]).astype(BF)

    loop(ZN, back_sum)

    rs_done(1, 0, 0)
    rs_a(3, 0, (0, 1, 2), 0)
    grad_b(3, False)
    grad_sent(6)
    grad_a(2, False)
    grad_sent(5)
    grad_a(1, False)
    rs_y(3, 0, (0, 1, 2), 0, 0)
    r_pass(3, 0, 0, 0, 1)
    rs_y(3, 0, (0, 1, 2), 0, 1)
    r_pass(3, 0, 0, 1, 1)
    r_pass(2, 1, 0, 0, 2)
    rs_done(1, 0, 1)
    rs_a(3, 0, (0, 1, 2), 1)
    r_pass(2, 1, 1, 0, 2)
    grad_b(2, False)
    r_pass(2, 1, 1, 1, 2)
    rs_y(3, 0, (0, 1, 2), 1, 0)
    r_pass(3, 0, 1, 0, 1)
    grad_sent(4)
    grad_a(0, False)
    rs_y(3, 0, (0, 1, 2), 1, 1)
    rs_y(2, 1, (6,), 0, 1)
    r_pass(3, 0, 0, 0, 2)
    r_pass(3, 0, 1, 1, 1)
    r_pass(3, 0, 0, 1, 2)
    g_in = rs_c(3, 0, 0)
    n_first, rstd = normed(tok[own_rows(0), :].astype(F32))
    vec[:, 0:256] = vec[:, 0:256] + packed(jnp.sum(g_in * n_first, axis=0, keepdims=True))
    g_tok = s.ghid[0:32, :] + norm_back(n_first, rstd, g_in * gain_row(0))
    s.ostage[0, 0:32, :] = g_tok.astype(BF)
    r_pass(2, 1, 0, 1, 1)
    r_pass(3, 0, 1, 0, 2)
    r_pass(3, 0, 1, 1, 2)
    s.ostage[1, 32:64, :] = (s.hidden[32:64, :] + rs_c(2, 1, 1)).astype(BF)
    for copy in out_copies(1, 1, res_o):
        copy.start()
    grad_b(1, False)
    r_pass(2, 1, 0, 1, 2)
    g_in = rs_c(3, 0, 1)
    n_first, rstd = normed(tok[own_rows(1), :].astype(F32))
    vec[:, 0:256] = vec[:, 0:256] + packed(jnp.sum(g_in * n_first, axis=0, keepdims=True))
    g_tok = s.ghid[32:64, :] + norm_back(n_first, rstd, g_in * gain_row(0))
    s.ostage[0, 32:64, :] = g_tok.astype(BF)
    grad_b(0, False)
    for copy in out_copies(0, 0, gtok_o):
        copy.start()
    def v_copy(j, dst, dev):
        return remote(vec, dst, s.v_s.at[j], s.v_r.at[j], dev)

    v_copy(0, s.vrc, cdev).start()
    for copy in out_copies(0, 1, gtok_o):
        copy.start()
    v_copy(0, s.vrc, cdev).wait()
    vec[...] = vec[...] + s.vrc[...]
    v_copy(1, s.vrx, xdev).start()
    v_copy(1, s.vrx, xdev).wait()
    vec[...] = vec[...] + s.vrx[...]
    v_copy(2, s.vry, ydev).start()
    v_copy(2, s.vry, ydev).wait()
    vec[:, 0:512] = vec[:, 0:512] + s.vry[:, 0:512]
    vz = s.vz
    vz[z] = vec[...]
    for i in peers:
        v_copy(2 + i, vz.at[z], zdev[i]).start()
    s.ostage[1, 0:32, :] = (s.hidden[0:32, :] + rs_c(2, 1, 0)).astype(BF)
    for copy in out_copies(1, 0, res_o):
        copy.start()
    for i in peers:
        there = vz.at[zdn[i]]
        remote(there, there, s.v_s.at[2 + i], s.v_r.at[2 + i], zdev[i]).wait_recv()
    for i in peers:
        v_copy(2 + i, vz.at[z], zdev[i]).wait_send()
    vec_o[:, 0:512] = ((vz[0, :, 0:512] + vz[1, :, 0:512]) + vz[2, :, 0:512]) + vz[3, :, 0:512]
    for zz in range(ZN):
        vec_o[:, 512 + 128 * zz : 640 + 128 * zz] = vz[zz, :, 512:VW]
    for j, dst in enumerate((gtok_o, res_o)):
        for g in range(2):
            there = dst.at[pl.ds(pl.multiple_of((1 - y) * HALF + g * HR, HR), HR)]
            a, b = out_copies(j, g, dst)
            a.wait_send()
            b.wait()
            remote(there, there, s.o_s.at[j, g], s.o_r.at[j, g], ydev).wait_recv()
    for n in range(4):
        grad_sent(n)
    for n in range(NCH):
        grad_done(n)
    loop(NCH, w_done)
    kv_copy(c).wait_send()
    dkv_copy.wait_send()
    for ia, (buf, own) in enumerate(((s.first, False), (s.cot, False), (s.second, True), (s.hlow, True))):
        ag_done(buf, ia, own)
    for g in range(2):
        rs_done(2, 1, g)
        rs_done(3, 0, g)


def finish_kernel(gwa, gwf, res, gtok, vec, o_res, o_tok, o_q, o_k, o_v, o_s, o_o, o_g, o_u, o_d, o_first, o_second, o_group):
    o_res[0] = res[...].astype(F32)
    o_tok[0] = gtok[...].astype(F32)
    for n, out in enumerate((o_g, o_u, o_d)):
        out[...] = gwf[n].astype(F32)
    both = jnp.swapaxes(gwa[0].astype(F32), 0, 1)
    o_q[...] = both[:, :, 0:256]
    o_k[...] = both[:, :, 256:512]
    for n, out in enumerate((o_v, o_s, o_o)):
        out[...] = jnp.swapaxes(gwa[n + 1].astype(F32), 0, 1)
    me = lax.axis_index("fsdp") * 8 + lax.axis_index("ctx")
    quarter = lax.rem(me, 4)

    def row(r, start, stop):
        block = vec[:, start:stop]
        return jnp.sum(jnp.where(lax.broadcasted_iota(jnp.int32, block.shape, 0) == r, block, 0.0), axis=0, keepdims=True)

    for out, start in ((o_first, 0), (o_second, 256)):
        pair = row(me // 2, start, start + 256)
        out[...] = jnp.where(lax.rem(me, 2) == 0, pair[:, 0:128], pair[:, 128:256])
    for zz in range(ZN):
        line = row(me // 4, 512 + 128 * zz, 640 + 128 * zz)
        total = jnp.zeros((1, 32), F32)
        for q in range(4):
            total = total + jnp.where(quarter == q, line[:, 32 * q : 32 * q + 32], 0.0)
        o_group[zz : zz + 1, :] = total


def finish(res, gtok, gwa, gwf, vec):
    steps = 2
    rows = BLK // steps
    flat = pl.BlockSpec((rows, D), lambda i: (i, 0))
    deep = pl.BlockSpec((1, rows, D), lambda i: (0, i, 0))
    narrow = pl.BlockSpec((rows, ZN, 256), lambda i: (i, 0, 0))
    wide = pl.BlockSpec((rows, ZN, CH), lambda i: (i, 0, 0))

    def whole(*shape):
        return pl.BlockSpec(shape, lambda i: (0,) * len(shape))

    def f32(*shape):
        return jax.ShapeDtypeStruct(shape, F32)

    outs = pl.pallas_call(
        finish_kernel,
        grid=(steps,),
        in_specs=[
            pl.BlockSpec((4, ZN, rows, CH), lambda i: (0, 0, i, 0)),
            pl.BlockSpec((3, rows, D), lambda i: (0, i, 0)),
            flat,
            flat,
            whole(8, 1024),
        ],
        out_specs=[deep, deep, narrow, narrow, wide, wide, wide, flat, flat, flat, whole(1, BLK), whole(1, BLK), whole(ZN, 32)],
        out_shape=[f32(1, BLK, D)] * 2
        + [f32(BLK, ZN, 256)] * 2
        + [f32(BLK, ZN, CH)] * 3
        + [f32(BLK, D)] * 3
        + [f32(1, BLK)] * 2
        + [f32(ZN, 32)],
        compiler_params=pltpu.CompilerParams(vmem_limit_bytes=VLIM),
    )(gwa, gwf, res, gtok, vec)
    return tuple(outs[:10]) + (outs[10].reshape(BLK), outs[11].reshape(BLK), outs[12])


def start_kernel(q, k, v, sw, o, g_first, g_second, g_group, rate, pk, gp, lr):
    for ref, at in ((q, 0), (k, 256), (v, 512), (sw, 1024), (o, 1536)):
        pk[:, :, at : at + ref.shape[2]] = jnp.swapaxes(ref[...], 0, 1)
    me = lax.axis_index("fsdp") * 8 + lax.axis_index("ctx")
    quarter = lax.rem(me, 4)
    gp[...] = jnp.zeros((8, BLK), F32)
    gp[0:1, :] = g_first[...].astype(F32)
    gp[1:2, :] = g_second[...].astype(F32)
    lane = lax.broadcasted_iota(jnp.int32, (ZN, BLK), 1) // 32
    wide = jnp.concatenate([g_group[...].astype(F32)] * 4, axis=1)
    gp[2:6, :] = jnp.where(lane == quarter, wide, 0.0)
    lr[...] = jnp.log(rate[...])


def begin(w_query, w_key, w_value, w_swish, w_output, gain_first, gain_second, gain_group, decay_rate):
    steps = 2
    rows = BLK // steps
    narrow = pl.BlockSpec((rows, ZN, 256), lambda i: (i, 0, 0))
    wide = pl.BlockSpec((rows, ZN, CH), lambda i: (i, 0, 0))

    def whole(*shape):
        return pl.BlockSpec(shape, lambda i: (0,) * len(shape))

    pk, gp, lr = pl.pallas_call(
        start_kernel,
        grid=(steps,),
        in_specs=[narrow, narrow, wide, wide, wide, whole(1, BLK), whole(1, BLK), whole(ZN, 32), whole(1, ZN)],
        out_specs=[pl.BlockSpec((ZN, rows, 4 * CH), lambda i: (0, i, 0)), whole(8, BLK), whole(1, ZN)],
        out_shape=[
            jax.ShapeDtypeStruct((ZN, BLK, 4 * CH), BF),
            jax.ShapeDtypeStruct((8, BLK), F32),
            jax.ShapeDtypeStruct((1, ZN), F32),
        ],
        compiler_params=pltpu.CompilerParams(vmem_limit_bytes=VLIM),
    )(w_query, w_key, w_value, w_swish, w_output, gain_first[None], gain_second[None], gain_group, decay_rate[None])
    return pk, gp, lr[0]


def fused(
    tokens, w_query, w_key, w_value, w_swish, w_output, w_gelu, w_up, w_down, gain_first, gain_second, gain_group, decay_rate, cotangent
):
    pk, gp, lr = begin(w_query, w_key, w_value, w_swish, w_output, gain_first, gain_second, gain_group, decay_rate)
    shapes = [
        jax.ShapeDtypeStruct((BLK, D), BF),
        jax.ShapeDtypeStruct((BLK, D), BF),
        jax.ShapeDtypeStruct((4, ZN, BLK, CH), BF),
        jax.ShapeDtypeStruct((3, BLK, D), BF),
        jax.ShapeDtypeStruct((8, 1024), F32),
    ]
    hbm = pl.BlockSpec(memory_space=pl.ANY)
    vmem = pl.BlockSpec(memory_space=pltpu.VMEM)
    smem = pl.BlockSpec(memory_space=pltpu.SMEM)
    scratch = [pltpu.VMEM(*v) for v in SCRATCH.values()]
    for shape in SEMS.values():
        scratch.append(pltpu.SemaphoreType.REGULAR((3,)) if shape is None else pltpu.SemaphoreType.DMA(shape))
    result, g_tok, gwa, gwf, vec = pl.pallas_call(
        kernel,
        out_shape=shapes,
        in_specs=[vmem, vmem, smem, hbm, hbm, hbm, hbm, hbm],
        out_specs=[hbm, hbm, hbm, hbm, vmem],
        scratch_shapes=scratch,
        compiler_params=pltpu.CompilerParams(collective_id=0, has_side_effects=True, vmem_limit_bytes=VLIM),
    )(tokens[0], gp, lr, cotangent[0], pk, w_gelu, w_up, w_down)
    return finish(result, g_tok, gwa, gwf, vec)


highest_precision = lax.Precision.HIGHEST


def prefix(part, axis, combine, identity):
    place = lax.axis_index(axis)
    gathered = jax.tree.map(lambda a: lax.all_gather(a, axis), part)
    state = jax.tree.map(lambda a, e: jnp.zeros_like(a) + jnp.asarray(e, a.dtype), part, identity)

    def one(turn, state):
        return combine(
            state, jax.tree.map(lambda a: lax.dynamic_index_in_dim(a, turn, 0, False), gathered)
        )

    return lax.fori_loop(0, place, one, state)


def entering_2(value, axis, combine, identity):
    devices, mine = (lax.axis_size(axis), lax.axis_index(axis))
    everything = jax.tree.map(
        lambda part, kind: lax.all_gather(part.astype(kind), axis),
        value,
        jax.tree.map(lambda a: jnp.bfloat16 if a.dtype == jnp.float32 else a.dtype, value),
    )
    start = jax.tree.map(
        lambda part, zero: jnp.broadcast_to(jnp.asarray(zero, part.dtype), part.shape),
        value,
        identity,
    )

    def turn(k, before):
        at = devices - 1 - k
        reached = at > mine
        new = combine(
            before, jax.tree.map(lambda part, own: part[at].astype(own.dtype), everything, value)
        )
        return jax.tree.map(lambda a, b: jnp.where(reached, a, b), new, before)

    return lax.fori_loop(0, devices, turn, start)


def norm_rows(values, gain):
    center = values - jnp.mean(values, axis=-1, keepdims=True)
    spread = jnp.mean(center * center, axis=-1, keepdims=True)
    return center * lax.rsqrt(spread + 1e-05) * gain


def entry_weights(length, log_rate):
    position = jnp.arange(length).astype(jnp.float32)
    return jnp.exp((position[:, None] + 1.0) * log_rate[None, :])


def exit_weights(length, log_rate):
    position = jnp.arange(length).astype(jnp.float32)
    return jnp.exp((length - 1.0 - position)[:, None] * log_rate[None, :])


def decay_matrix(length, log_rate):
    position = jnp.arange(length).astype(jnp.float32)
    distance = position[:, None] - position[None, :]
    causal = distance >= 0.0
    return jnp.where(
        causal[None], jnp.exp(jnp.where(causal, distance, 0.0)[None] * log_rate[:, None, None]), 0.0
    )


def retain_out(query_block, key_block_rows, value_block_rows, retention_state, log_rate):
    length = query_block.shape[1]
    scores = (
        jnp.einsum("sthk,sqhk->shtq", query_block, key_block_rows, precision=highest_precision)
        * decay_matrix(length, log_rate)[None]
    )
    within = jnp.einsum("shtq,sqhv->sthv", scores, value_block_rows, precision=highest_precision)
    carried_state = jnp.einsum(
        "sthk,shkv->sthv",
        query_block * entry_weights(length, log_rate)[None, :, :, None],
        retention_state,
        precision=highest_precision,
    )
    return within + carried_state


def retain_low(query_low, key_low, query_wide, value_wide, retention_state, log_rate):
    length = query_low.shape[1]
    raw_scores = jnp.einsum(
        "sthk,sqhk->shtq", query_low, key_low, preferred_element_type=jnp.float32
    )
    scores = raw_scores * decay_matrix(length, log_rate)[None]
    within = jnp.einsum("shtq,sqhv->sthv", scores, value_wide, precision=highest_precision)
    carried_state = jnp.einsum(
        "sthk,shkv->sthv",
        query_wide * entry_weights(length, log_rate)[None, :, :, None],
        retention_state,
        precision=highest_precision,
    )
    return within + carried_state


def own_states(key_block_rows, value_block_rows, log_rate):
    length = key_block_rows.shape[1]
    return jnp.einsum(
        "sthk,sthv->shkv",
        key_block_rows * exit_weights(length, log_rate)[None, :, :, None],
        value_block_rows,
        precision=highest_precision,
    )


def combine_states(earlier, later):
    return (earlier[0] * later[0], later[0][None, :, None, None] * earlier[1] + later[1])


def gate_section(retained, swish_in, gain):
    return norm_rows(retained, gain) * jax.nn.silu(swish_in)


def mlp_section(act_gelu, act_up):
    return jax.nn.gelu(act_gelu) * act_up


def general(
    tokens,
    w_query,
    w_key,
    w_value,
    w_swish,
    w_output,
    w_gelu,
    w_up,
    w_down,
    gain_first,
    gain_second,
    gain_group,
    decay_rate,
    cotangent,
):
    f32 = jnp.float32
    bf16 = jnp.bfloat16
    gathered = (
        lax.all_gather(w_query, ("fsdp", "ctx"), axis=0, tiled=True),
        lax.all_gather(w_key, ("fsdp", "ctx"), axis=0, tiled=True),
        lax.all_gather(w_value, ("fsdp", "ctx"), axis=0, tiled=True),
        lax.all_gather(w_swish, ("fsdp", "ctx"), axis=0, tiled=True),
        lax.all_gather(w_output, ("fsdp", "ctx"), axis=0, tiled=True),
        lax.all_gather(w_gelu, ("fsdp", "ctx"), axis=0, tiled=True),
        lax.all_gather(w_up, ("fsdp", "ctx"), axis=0, tiled=True),
        lax.all_gather(w_down, ("fsdp", "ctx"), axis=0, tiled=True),
        lax.all_gather(gain_first, ("fsdp", "ctx"), axis=0, tiled=True),
        lax.all_gather(gain_second, ("fsdp", "ctx"), axis=0, tiled=True),
        lax.all_gather(gain_group, ("fsdp", "ctx"), axis=1, tiled=True),
    )
    (
        full_query,
        full_key,
        full_value,
        full_swish,
        full_output,
        full_gelu,
        full_up,
        full_down,
        full_first,
        full_second,
        full_group,
    ) = gathered
    log_rate = jnp.log(decay_rate)
    piece = tokens.shape[1]
    key_scale = full_query.shape[2] ** (-0.5)
    factor = jnp.exp(piece * log_rate)
    inputs = tokens.astype(f32)
    first_gain = full_first.astype(f32)
    second_gain = full_second.astype(f32)
    group_gain = full_group.astype(f32)
    first_low = norm_rows(inputs, first_gain).astype(bf16)
    query_block = jnp.einsum(
        "spd,dhk->sphk", first_low, full_query, preferred_element_type=f32
    ).astype(bf16)
    key_block_rows = (
        jnp.einsum("spd,dhk->sphk", first_low, full_key, preferred_element_type=f32) * key_scale
    ).astype(bf16)
    value_block_rows = jnp.einsum(
        "spd,dhv->sphv", first_low, full_value, preferred_element_type=f32
    ).astype(bf16)
    swish_in = jnp.einsum("spd,dhv->sphv", first_low, full_swish, preferred_element_type=f32)
    query_wide = query_block.astype(f32)
    key_wide = key_block_rows.astype(f32)
    value_wide = value_block_rows.astype(f32)
    local_state = own_states(key_wide, value_wide, log_rate)
    identity = (jnp.ones_like(factor), jnp.zeros_like(local_state))
    _, entering = prefix((factor, local_state), "ctx", combine_states, identity)
    retained = retain_low(query_block, key_block_rows, query_wide, value_wide, entering, log_rate)
    gated = gate_section(retained, swish_in, group_gain).astype(bf16)
    attn_terms = jnp.einsum("sphv,dhv->spd", gated, full_output, preferred_element_type=f32)
    hidden = inputs + lax.psum(attn_terms, "tp")
    second_low = norm_rows(hidden, second_gain).astype(bf16)
    act_gelu = jnp.einsum("spd,df->spf", second_low, full_gelu, preferred_element_type=f32)
    act_up = jnp.einsum("spd,df->spf", second_low, full_up, preferred_element_type=f32)
    mixed = mlp_section(act_gelu, act_up).astype(bf16)
    mlp_terms = jnp.einsum("spf,df->spd", mixed, full_down, preferred_element_type=f32)
    result = hidden + lax.psum(mlp_terms.astype(jnp.bfloat16), "tp").astype(jnp.float32)
    back_query, back_key, back_value, back_swish, back_output, back_gelu, back_up, back_down = gathered[:8]
    grad_mixed = jnp.einsum("spd,df->spf", cotangent, back_down, preferred_element_type=f32)
    grad_down = jnp.einsum("spd,spf->df", cotangent, mixed, preferred_element_type=f32).astype(bf16)
    _, pull_mlp = jax.vjp(mlp_section, act_gelu, act_up)
    grad_act_gelu, grad_act_up = pull_mlp(grad_mixed)
    gelu_low = grad_act_gelu.astype(bf16)
    up_low = grad_act_up.astype(bf16)
    grad_gelu = jnp.einsum("spd,spf->df", second_low, gelu_low, preferred_element_type=f32).astype(bf16)
    grad_up = jnp.einsum("spd,spf->df", second_low, up_low, preferred_element_type=f32).astype(bf16)
    second_terms = jnp.einsum(
        "spf,df->spd", gelu_low, back_gelu, preferred_element_type=f32
    ) + jnp.einsum("spf,df->spd", up_low, back_up, preferred_element_type=f32)
    grad_second_in = lax.psum(second_terms, "tp")
    _, pull_second = jax.vjp(norm_rows, hidden, second_gain)
    hidden_from_norm, grad_second = pull_second(grad_second_in)
    grad_hidden = cotangent.astype(f32) + hidden_from_norm
    hidden_low = grad_hidden.astype(bf16)
    grad_gated = jnp.einsum("spd,dhv->sphv", hidden_low, back_output, preferred_element_type=f32)
    grad_output = jnp.einsum("spd,sphv->dhv", hidden_low, gated, preferred_element_type=f32).astype(bf16)
    _, pull_gate = jax.vjp(gate_section, retained, swish_in, group_gain)
    grad_retained, grad_swish_in, grad_group = pull_gate(grad_gated)
    swish_low = grad_swish_in.astype(bf16)
    entry_grad = jnp.einsum(
        "sthk,sthv->shkv",
        query_wide * entry_weights(piece, log_rate)[None, :, :, None],
        grad_retained,
        precision=highest_precision,
    )
    _, later_grad = entering_2((factor, entry_grad), "ctx", combine_states, identity)
    _, pull_retain = jax.vjp(
        lambda rows_q, rows_k, rows_v: (
            retain_out(rows_q, rows_k, rows_v, entering, log_rate),
            own_states(rows_k, rows_v, log_rate),
        ),
        query_wide,
        key_wide,
        value_wide,
    )
    grad_query_act, grad_key_act, grad_value_act = pull_retain((grad_retained, later_grad))
    query_low = grad_query_act.astype(bf16)
    key_low = (grad_key_act.astype(bf16).astype(f32) * key_scale).astype(bf16)
    value_low = grad_value_act.astype(bf16)
    grad_query = jnp.einsum("spd,sphk->dhk", first_low, query_low, preferred_element_type=f32).astype(bf16)
    grad_key = jnp.einsum("spd,sphk->dhk", first_low, key_low, preferred_element_type=f32).astype(bf16)
    grad_value = jnp.einsum("spd,sphv->dhv", first_low, value_low, preferred_element_type=f32).astype(bf16)
    grad_swish = jnp.einsum("spd,sphv->dhv", first_low, swish_low, preferred_element_type=f32).astype(bf16)
    first_terms = jnp.einsum("sphk,dhk->spd", query_low, back_query, preferred_element_type=f32)
    first_terms = first_terms + jnp.einsum(
        "sphk,dhk->spd", key_low, back_key, preferred_element_type=f32
    )
    first_terms = first_terms + jnp.einsum(
        "sphv,dhv->spd", value_low, back_value, preferred_element_type=f32
    )
    first_terms = first_terms + jnp.einsum(
        "sphv,dhv->spd", swish_low, back_swish, preferred_element_type=f32
    )
    grad_first_in = lax.psum(first_terms.astype(jnp.bfloat16), "tp").astype(jnp.float32)
    _, pull_first = jax.vjp(norm_rows, inputs, first_gain)
    tokens_from_norm, grad_first = pull_first(grad_first_in)
    grad_tokens = grad_hidden + tokens_from_norm
    owned = tuple(
        lax.psum_scatter(g, ("fsdp", "ctx"), scatter_dimension=0, tiled=True).astype(f32)
        for g in (grad_query, grad_key, grad_value, grad_swish, grad_output, grad_gelu, grad_up, grad_down, grad_first, grad_second)
    ) + (lax.psum_scatter(grad_group, ("fsdp", "ctx"), scatter_dimension=1, tiled=True),)
    return (
        result,
        grad_tokens,
        owned[0],
        owned[1],
        owned[2],
        owned[3],
        owned[4],
        owned[5],
        owned[6],
        owned[7],
        owned[8],
        owned[9],
        owned[10],
    )


def solution(mesh):
    wide, flat = P(("fsdp", "ctx"), "tp", None), P(("fsdp", "ctx"), "tp")
    tok, row, group = P("fsdp", "ctx", None), P(("fsdp", "ctx")), P("tp", ("fsdp", "ctx"))
    in_specs = (tok,) + (wide,) * 5 + (flat,) * 3 + (row, row, group, P("tp"), tok)
    out_specs = (tok, tok) + (wide,) * 5 + (flat,) * 3 + (row, row, group)
    sizes = (mesh.shape["fsdp"], mesh.shape["ctx"], mesh.shape["tp"])
    local = fused if sizes == (2, 2 * ZN, 2) else general
    return jax.shard_map(local, mesh=mesh, in_specs=in_specs, out_specs=out_specs, check_vma=False)
```
